128 devices in a mesh: gx: 8 (over z_hi, x), gy: 16 (over z_lo, y, core).
Axes of the slice: x: 4, y: 4, z: 4 (z_hi: 2, z_lo: 2; z = z_hi * 2 + z_lo), core: 2. Of those that a mesh axis runs over, the one named last changes fastest.
Arguments:
- tracers: float32 [2, 8, 1024, 2048], P(None, None, 'gy', 'gx'), may hold values from -6 to 6
- east_speed: float32 [8, 1024, 2048], P(None, 'gy', 'gx'), may hold values from -0.2 to 0.2
- north_speed: float32 [8, 1024, 2048], P(None, 'gy', 'gx'), may hold values from -0.2 to 0.2
- vertical_mix: float32 [7, 1024, 2048], P(None, 'gy', 'gx'), may hold values from 0.05 to 5
- level_count: int32 [1024, 2048], P('gy', 'gx'), may hold values from 0 to 8, as said below
- atmosphere_flux: float32 [8, 256, 1024], P(None, 'gy', 'gx'), may hold values from -6 to 6
- intersection_source: int32 [8192, 1024], P('gy', 'gx'), may hold values from 0 to 2047, as said below
- intersection_target: int32 [8192, 1024], P('gy', 'gx'), may hold values from 0 to 16383, as said below
- intersection_weight: float32 [8192, 1024], P('gy', 'gx'), may hold values from 0 to 1, as said below
Outputs:
- tracers_out: float32 [2, 8, 1024, 2048], P(None, None, 'gy', 'gx')
- surface_flux: float32 [8, 1024, 2048], P(None, 'gy', 'gx')
The draws below stay inside these ranges and needn't reach their ends.
Inputs may be any that keep to these rules, and one draw needn't show every extreme that they name: `intersection_source`: the slot from one atmosphere tile to one ocean tile of the same longitude tile has 4096 entries, live entries first. A slot from latitude tile s to latitude tile d holds live entries only where |d - s| <= 1, or where d >= 14 and s >= 7; every such slot has at least one; other slots are all padding. Padded entries have source cell 0, target cell 0 and weight 0. `intersection_target`: padded entries name cell 0. `intersection_weight`: zero on padded entries, positive on live ones. `level_count`: 0 marks land.
All inputs are finite; a program needn't handle non-finite values.
Results may differ from the reference program's by a relative error of at most 0.0003.
Values sent between devices are 32-bit elements; how exact they have to be, the bound alone decides.
No kernel may reach another device: no remote copies, remote signals or barrier semaphores. Data moves between devices by JAX's collectives and lax.ppermute only.
A program may use at most 64 MiB of HBM per device.

```python
import math
import jax
import jax.numpy as jnp
from jax import lax

FIELDS = 8
TRACERS = 2
BLOCK = 128
NZ = 8
CJ = 64
CI = 256
AJ = 16
AI = 128
CAP = 32
NJ = 1024
NI = 2048
AJG = 256
AIG = 1024
N_GX = 8
N_GY = 16


def slot_layout(key):
    slot_size = CAP * BLOCK
    tile_shape = (N_GY, N_GY, N_GX)
    source_grid = lax.broadcasted_iota(jnp.int32, tile_shape, 0)
    target_grid = lax.broadcasted_iota(jnp.int32, tile_shape, 1)
    nearby = jnp.abs(target_grid - source_grid) <= 1
    arctic = (target_grid >= N_GY - 2) & (source_grid >= N_GY // 2 - 1)
    linked = nearby | arctic
    hot_target = jax.random.randint(jax.random.fold_in(key, 101), (N_GX,), 0, N_GY)
    counts = jax.random.randint(jax.random.fold_in(key, 102), tile_shape, slot_size // 3, slot_size * 3 // 4 + 1)
    counts = jnp.where(target_grid == hot_target[None, None, :], slot_size, counts)
    counts = jnp.where(linked, jnp.maximum(counts, 1), 0)
    list_shape = (N_GY * N_GY * CAP, N_GX * BLOCK)
    row_ids = lax.broadcasted_iota(jnp.int32, list_shape, 0)
    column_ids = lax.broadcasted_iota(jnp.int32, list_shape, 1)
    source_tile = row_ids // (N_GY * CAP)
    target_tile = row_ids // CAP % N_GY
    block_index = row_ids % CAP
    longitude_tile = column_ids // BLOCK
    position = block_index * BLOCK + column_ids % BLOCK
    limit = counts[source_tile, target_tile, longitude_tile]
    return (position < limit, source_tile, target_tile)


def draw_intersection_source(key, part):
    live, source_tile, target_tile = slot_layout(key)
    key = jax.random.fold_in(key, 3)
    raw_rows = jax.random.randint(jax.random.fold_in(key, 1), live.shape, 0, AJ)
    raw_columns = jax.random.randint(jax.random.fold_in(key, 2), live.shape, 0, AI)
    rows_used = jnp.where(target_tile > source_tile, (raw_rows + AJ) // 2, jnp.where(target_tile < source_tile, raw_rows // 2, raw_rows))
    cells = rows_used * AI + raw_columns
    return jnp.where(live, cells, 0).astype(jnp.int32)


def draw_intersection_target(key, part):
    live, source_tile, target_tile = slot_layout(key)
    key = jax.random.fold_in(key, 5)
    raw_rows = jax.random.randint(jax.random.fold_in(key, 1), live.shape, 0, CJ)
    raw_columns = jax.random.randint(jax.random.fold_in(key, 2), live.shape, 0, CI)
    rows_used = jnp.where(target_tile > source_tile, raw_rows // 2, jnp.where(target_tile < source_tile, (raw_rows + CJ) // 2, raw_rows))
    cells = rows_used * CI + raw_columns
    return jnp.where(live, cells, 0).astype(jnp.int32)


def draw_intersection_weight(key, part):
    live, source_tile, target_tile = slot_layout(key)
    key = jax.random.fold_in(key, 7)
    uniform_part = jax.random.uniform(key, live.shape, jnp.float32, 0.0, 1.0)
    weights = 0.2 + 0.8 * uniform_part
    return jnp.where(live, weights, 0.0).astype(jnp.float32)


def draw_level_count(key, part):
    key = jax.random.fold_in(key, 9)
    shape_here = (CJ * N_GY, CI * N_GX)
    landed = jax.random.randint(jax.random.fold_in(key, 1), shape_here, 0, 10) < 3
    levels = jax.random.randint(jax.random.fold_in(key, 2), shape_here, 1, NZ + 1)
    return jnp.where(landed, 0, levels).astype(jnp.int32)


def block_levels(own_key, shape, shards, smallest, top_value):
    loudness, own = 1.0, jax.random.fold_in(own_key, 6)
    for axis_at, parts in shards:
        steps = jnp.exp(jax.random.uniform(jax.random.fold_in(own, axis_at), (parts,), jnp.float32, smallest / len(shards), top_value / len(shards)))
        loudness = loudness * jnp.repeat(steps, shape[axis_at] // parts).reshape([-1 if axis == axis_at else 1 for axis in range(len(shape))])
    return loudness


def scatter_about(rng, shape, scale, reach, split=(), kind=jnp.bfloat16):
    gain = block_levels(rng, shape, split, -0.22, 0.18) if split else 1.0
    array = jax.random.normal(rng, shape, jnp.float32) * scale * gain
    return jnp.minimum(jnp.maximum(array, -reach), reach).astype(kind)


def setup_inputs(seed: int = 0) -> dict:
    splits = jax.random.split(jax.random.key(seed), 10)
    return {
        "tracers": scatter_about(splits[0], (TRACERS, NZ, NJ, NI), 1.0, 6.0, ((2, 16), (3, 8)), jnp.float32),
        "east_speed": jnp.clip(jax.random.uniform(splits[1], (NZ, NJ, NI), jnp.float32, -0.2, 0.2) * block_levels(splits[1], (NZ, NJ, NI), ((1, 16), (2, 8)), -0.4, 0.0), -0.2, 0.2),
        "north_speed": jnp.clip(jax.random.uniform(splits[2], (NZ, NJ, NI), jnp.float32, -0.2, 0.2) * block_levels(splits[2], (NZ, NJ, NI), ((1, 16), (2, 8)), -0.4, 0.0), -0.2, 0.2),
        "vertical_mix": jnp.clip(jnp.exp(math.log(5.0) - 4.6051702 * jax.random.uniform(splits[3], (NZ - 1, NJ, NI), jnp.float32) ** block_levels(splits[3], (NZ - 1, NJ, NI), ((1, 16), (2, 8)), -0.2, 0.2)), 0.05, 5.0),
        "level_count": draw_level_count(jax.random.fold_in(splits[9], 71), 0),
        "atmosphere_flux": scatter_about(splits[5], (FIELDS, AJG, AIG), 1.0, 6.0, ((1, 16), (2, 8)), jnp.float32),
        "intersection_source": draw_intersection_source(jax.random.fold_in(splits[9], 71), 0),
        "intersection_target": draw_intersection_target(jax.random.fold_in(splits[9], 71), 0),
        "intersection_weight": draw_intersection_weight(jax.random.fold_in(splits[9], 71), 0),
    }


DIFFUSE = 0.05


def combine(centre, east_side, west_side, north_side, south_side, mask_here, mask_east, mask_west, mask_north, mask_south, speed_east, speed_west, speed_north, speed_south):
    carry_east = speed_east * jnp.where(speed_east > 0, centre, east_side) * mask_here * mask_east
    carry_west = speed_west * jnp.where(speed_west > 0, west_side, centre) * mask_west * mask_here
    carry_north = speed_north * jnp.where(speed_north > 0, centre, north_side) * mask_here * mask_north
    carry_south = speed_south * jnp.where(speed_south > 0, south_side, centre) * mask_south * mask_here
    spread_east = DIFFUSE * (east_side - centre) * mask_here * mask_east
    spread_west = DIFFUSE * (centre - west_side) * mask_west * mask_here
    spread_north = DIFFUSE * (north_side - centre) * mask_here * mask_north
    spread_south = DIFFUSE * (centre - south_side) * mask_south * mask_here
    updated = centre + (carry_west - carry_east + carry_south - carry_north + spread_east - spread_west + spread_north - spread_south)
    return jnp.where(mask_here > 0, updated, centre)


def vertical(advected, ocean_mask, vertical_mix, forcing):
    level_total = advected.shape[1]
    ratio_prev = jnp.zeros_like(advected[:, 0])
    partial_prev = jnp.zeros_like(advected[:, 0])
    ratios = []
    partials = []
    for level_index in range(level_total):
        thickness = 1.0 + level_index / level_total
        if level_index >= 1:
            upper_coef = jnp.where(ocean_mask[level_index] > 0, vertical_mix[level_index - 1] / thickness, 0.0)
        else:
            upper_coef = jnp.zeros_like(ocean_mask[0])
        if level_index <= level_total - 2:
            lower_coef = jnp.where(ocean_mask[level_index + 1] > 0, vertical_mix[level_index] / thickness, 0.0)
        else:
            lower_coef = jnp.zeros_like(ocean_mask[0])
        right_side = advected[:, level_index]
        if level_index == 0:
            right_side = right_side + forcing * ocean_mask[0] / thickness
        pivot_value = 1.0 + upper_coef + lower_coef - upper_coef * ratio_prev
        ratio_prev = lower_coef / pivot_value
        partial_prev = (right_side + upper_coef * partial_prev) / pivot_value
        ratios.append(ratio_prev)
        partials.append(partial_prev)
    solved = [partials[-1]]
    for level_index in range(level_total - 2, -1, -1):
        solved.append(partials[level_index] + ratios[level_index] * solved[-1])
    return jnp.stack(solved[::-1], axis=1)


def horizontal_level(inputs):
    values, mask_level, east_level, north_level = inputs
    zero_values = jnp.zeros_like(values[:, :1, :])
    zero_row = jnp.zeros_like(mask_level[:1, :])
    east_side = jnp.roll(values, -1, axis=2)
    west_side = jnp.roll(values, 1, axis=2)
    north_side = jnp.concatenate([values[:, 1:, :], values[:, -1:, ::-1]], axis=1)
    south_side = jnp.concatenate([zero_values, values[:, :-1, :]], axis=1)
    mask_east = jnp.roll(mask_level, -1, axis=1)
    mask_west = jnp.roll(mask_level, 1, axis=1)
    mask_north = jnp.concatenate([mask_level[1:, :], mask_level[-1:, ::-1]], axis=0)
    mask_south = jnp.concatenate([zero_row, mask_level[:-1, :]], axis=0)
    speed_west = jnp.roll(east_level, 1, axis=1)
    speed_south = jnp.concatenate([zero_row, north_level[:-1, :]], axis=0)
    return combine(values, east_side, west_side, north_side, south_side, mask_level, mask_east, mask_west, mask_north, mask_south, east_level, speed_west, north_level, speed_south)


def reference(tracers, east_speed, north_speed, vertical_mix, level_count, atmosphere_flux, intersection_source, intersection_target, intersection_weight):
    ocean_mask = (lax.broadcasted_iota(jnp.int32, east_speed.shape, 0) < level_count[None]).astype(jnp.float32)
    atmos_tiles = atmosphere_flux.reshape(FIELDS, N_GY, AJ, N_GX, AI).transpose(0, 1, 3, 2, 4).reshape(FIELDS, N_GY * N_GX * AJ * AI)
    list_shape = (N_GY, N_GY, CAP, N_GX, BLOCK)
    source_row = lax.broadcasted_iota(jnp.int32, list_shape, 0)
    target_row = lax.broadcasted_iota(jnp.int32, list_shape, 1)
    tile_column = lax.broadcasted_iota(jnp.int32, list_shape, 3)
    flat_source = ((source_row * N_GX + tile_column) * (AJ * AI) + intersection_source.reshape(list_shape)).reshape(-1)
    flat_target = ((target_row * N_GX + tile_column) * (CJ * CI) + intersection_target.reshape(list_shape)).reshape(-1)
    contributed = jnp.take(atmos_tiles, flat_source, axis=1) * intersection_weight.reshape(-1)[None]
    summed = jnp.zeros((FIELDS, N_GY * N_GX * CJ * CI), jnp.float32).at[:, flat_target].add(contributed)
    surface_flux = summed.reshape(FIELDS, N_GY, N_GX, CJ, CI).transpose(0, 1, 3, 2, 4).reshape(FIELDS, NJ, NI)
    heat_total = surface_flux[0] + surface_flux[1] + surface_flux[2] + surface_flux[3] + surface_flux[4]
    salt_total = surface_flux[7] - surface_flux[5] - surface_flux[6]
    forcing = jnp.stack([heat_total, salt_total])
    open_north = north_speed.at[:, -1, :].set(0.0)
    result = tracers
    for section_index in range(2):
        advected = lax.map(horizontal_level, (jnp.moveaxis(result, 1, 0), ocean_mask, east_speed, open_north))
        result = vertical(jnp.moveaxis(advected, 0, 1), ocean_mask, vertical_mix, forcing)
    return result, surface_flux
```

```python
import functools

import jax
import jax.numpy as jnp
from jax import lax
from jax.experimental import pallas as pl
from jax.experimental.pallas import tpu as pltpu
from jax.sharding import PartitionSpec as P

DIFFUSE = 0.05
FIELDS = 8
TRACERS = 2
NZ = 8
ROWS = 64
COLUMNS = 256
LANES = 128
GX = 8
GY = 16
SLOT_ROWS = 32
ATMOS_ROWS = 16
ARCTIC = 7
FIRST_ARCTIC = 7
CHANNELS = TRACERS * NZ
COUNT_AT = 24
RIM = 32
PAYLOAD = 3 * SLOT_ROWS + FIELDS * ATMOS_ROWS
SLOTS = 3 + ARCTIC
CHUNK_ROWS = 8
CHUNK = CHUNK_ROWS * LANES
CHUNKS = SLOT_ROWS // CHUNK_ROWS
VMEM_LIMIT = 48 * 1024 * 1024
F32 = jnp.float32
BF16 = jnp.bfloat16


def vmem_specs(count):
    return [pl.BlockSpec(memory_space=pltpu.VMEM) for _ in range(count)]


def call(kernel, out_shapes, operands, scratch=(), flops=0, moved=4_000_000):
    return pl.pallas_call(
        kernel,
        out_shape=[jax.ShapeDtypeStruct(shape, F32) for shape in out_shapes],
        in_specs=vmem_specs(len(operands)),
        out_specs=vmem_specs(len(out_shapes)),
        scratch_shapes=list(scratch),
        compiler_params=pltpu.CompilerParams(vmem_limit_bytes=VMEM_LIMIT),
        cost_estimate=pl.CostEstimate(flops=flops, bytes_accessed=moved, transcendentals=0),
    )(*operands)


def pack_columns(pick, channels, out_ref):
    lane = lax.broadcasted_iota(jnp.int32, (8, LANES), 1)
    for block in range(ROWS // 8):
        tile = jnp.zeros((8, LANES), F32)
        for channel in channels:
            value, at = pick(channel, block * 8)
            shift = (channel - at) % LANES
            moved = pltpu.roll(value, shift, axis=1) if shift else value
            tile = jnp.where(lane == channel, moved, tile)
        out_ref[pl.ds(block * 8, 8), :] = tile


def pack_row(value, channel, out_ref):
    out_ref[pl.ds(channel, 1), :] = value[:, :LANES]
    out_ref[pl.ds(RIM + channel, 1), :] = value[:, LANES:]


def pack_kernel(
    tracers_ref,
    east_ref,
    north_ref,
    count_ref,
    atmos_ref,
    source_ref,
    target_ref,
    weight_ref,
    to_east_ref,
    to_west_ref,
    to_north_ref,
    to_south_ref,
    own_ref,
    *arctic_refs,
):
    here = lax.axis_index("gy")

    def slot_into(out_ref, at, tile):
        rows = pl.ds(pl.multiple_of(tile * SLOT_ROWS, SLOT_ROWS), SLOT_ROWS)
        out_ref[at : at + SLOT_ROWS, :] = source_ref[rows, :].astype(F32)
        out_ref[at + SLOT_ROWS : at + 2 * SLOT_ROWS, :] = target_ref[rows, :].astype(F32)
        out_ref[at + 2 * SLOT_ROWS : at + 3 * SLOT_ROWS, :] = weight_ref[rows, :]
        for field in range(FIELDS):
            first = at + 3 * SLOT_ROWS + field * ATMOS_ROWS
            out_ref[first : first + ATMOS_ROWS, :] = atmos_ref[field]

    def east_column(channel, row):
        rows = pl.ds(row, 8)
        if channel < CHANNELS:
            return tracers_ref[channel, rows, LANES:], LANES - 1
        if channel < COUNT_AT:
            return east_ref[channel - CHANNELS, rows, LANES:], LANES - 1
        return count_ref[rows, LANES:].astype(F32), LANES - 1

    def west_column(channel, row):
        rows = pl.ds(row, 8)
        if channel < CHANNELS:
            return tracers_ref[channel, rows, :LANES], 0
        return count_ref[rows, :LANES].astype(F32), 0

    pack_columns(east_column, [*range(CHANNELS + NZ), COUNT_AT], to_east_ref)
    pack_columns(west_column, [*range(CHANNELS), COUNT_AT], to_west_ref)
    to_north_ref[0 : 2 * RIM, :] = jnp.zeros((2 * RIM, LANES), F32)
    to_south_ref[0 : 2 * RIM, :] = jnp.zeros((2 * RIM, LANES), F32)
    for channel in range(CHANNELS):
        pack_row(tracers_ref[channel, ROWS - 1 : ROWS, :], channel, to_north_ref)
        pack_row(tracers_ref[channel, 0:1, :], channel, to_south_ref)
    for level in range(NZ):
        pack_row(north_ref[level, ROWS - 1 : ROWS, :], CHANNELS + level, to_north_ref)
    pack_row(count_ref[ROWS - 1 : ROWS, :].astype(F32), COUNT_AT, to_north_ref)
    pack_row(count_ref[0:1, :].astype(F32), COUNT_AT, to_south_ref)
    slot_into(to_north_ref, 2 * RIM, jnp.minimum(here + 1, GY - 1))
    slot_into(to_south_ref, 2 * RIM, jnp.maximum(here - 1, 0))
    slot_into(own_ref, 0, here)
    for step, out_ref in enumerate(arctic_refs):
        slot_into(out_ref, 0, jnp.where(here == FIRST_ARCTIC + step, GY - 2, GY - 1))


def step_kernel(
    forced,
    q_ref,
    from_west_ref,
    from_east_ref,
    from_south_ref,
    from_north_ref,
    from_fold_ref,
    static_west_ref,
    static_east_ref,
    static_south_ref,
    static_north_ref,
    static_fold_ref,
    east_ref,
    north_ref,
    count_ref,
    mix_ref,
    *more_refs,
):
    if forced:
        out_ref, gain_ref, top_ref, static_top_ref = more_refs
    else:
        forcing_ref, out_ref, top_ref, static_top_ref = more_refs
    on_top = lax.axis_index("gy") == GY - 1
    lane = lax.broadcasted_iota(jnp.int32, (8, LANES), 1)
    row = lax.broadcasted_iota(jnp.int32, (8, LANES), 0)
    first_lane, last_lane = lane == 0, lane == LANES - 1
    first_row, last_row = row == 0, row == 7

    def set_top(north_rim, fold_rim, into):
        @pl.when(jnp.logical_not(on_top))
        def _():
            into[...] = north_rim[0 : 2 * RIM, :]

        @pl.when(on_top)
        def _():
            flipped = LANES - 1 - lane
            for half in range(2):
                for block in range(RIM // 8):
                    rows = fold_rim[pl.ds((1 - half) * RIM + block * 8, 8), :]
                    into[pl.ds(half * RIM + block * 8, 8), :] = jnp.take_along_axis(
                        rows, flipped, axis=1, mode="promise_in_bounds"
                    )

    set_top(from_north_ref, from_fold_ref, top_ref)
    set_top(static_north_ref, static_fold_ref, static_top_ref)

    def block_step(block, carry):
        at = pl.multiple_of(block * 8, 8)
        below = pl.multiple_of(jnp.maximum(block - 1, 0) * 8, 8)
        above = pl.multiple_of(jnp.minimum(block + 1, ROWS // 8 - 1) * 8, 8)
        is_first, is_last = block == 0, block == ROWS // 8 - 1
        rows = pl.ds(at, 8)

        def halves(load):
            return [load(rows, slice(0, LANES)), load(rows, slice(LANES, 2 * LANES))]

        def to_west_of(parts, rim):
            low = jnp.where(last_lane, rim, parts[0])
            high = jnp.where(last_lane, parts[0], parts[1])
            return [pltpu.roll(low, 1, axis=1), pltpu.roll(high, 1, axis=1)]

        def to_east_of(parts, rim):
            low = jnp.where(first_lane, parts[1], parts[0])
            high = jnp.where(first_lane, rim, parts[1])
            return [
                pltpu.roll(low, LANES - 1, axis=1),
                pltpu.roll(high, LANES - 1, axis=1),
            ]

        def to_south_of(load, parts, rim_ref, channel):
            found = []
            for half in range(2):
                lanes = slice(half * LANES, (half + 1) * LANES)
                rim = jnp.broadcast_to(
                    rim_ref[half * RIM + channel : half * RIM + channel + 1, :], (8, LANES)
                )
                near = jnp.where(is_first, rim, load(pl.ds(below, 8), lanes))
                found.append(pltpu.roll(jnp.where(last_row, near, parts[half]), 1, axis=0))
            return found

        def to_north_of(load, parts, rim_ref, channel):
            found = []
            for half in range(2):
                lanes = slice(half * LANES, (half + 1) * LANES)
                rim = jnp.broadcast_to(
                    rim_ref[half * RIM + channel : half * RIM + channel + 1, :], (8, LANES)
                )
                near = jnp.where(is_last, rim, load(pl.ds(above, 8), lanes))
                found.append(pltpu.roll(jnp.where(first_row, near, parts[half]), 7, axis=0))
            return found

        def west_rim(ref, channel):
            return pltpu.roll(ref[rows, :], (LANES - 1 - channel) % LANES, axis=1)

        def east_rim(ref, channel):
            shift = (LANES - channel) % LANES
            return pltpu.roll(ref[rows, :], shift, axis=1) if shift else ref[rows, :]

        def load_count(where, lanes):
            return count_ref[where, lanes].astype(F32)

        count = halves(load_count)
        sides = [
            to_east_of(count, east_rim(static_east_ref, COUNT_AT)),
            to_west_of(count, west_rim(static_west_ref, COUNT_AT)),
            to_north_of(load_count, count, static_top_ref, COUNT_AT),
            to_south_of(load_count, count, static_south_ref, COUNT_AT),
        ]
        shared = [[jnp.minimum(count[half], side[half]) for half in range(2)] for side in sides]
        closed = jnp.logical_and(jnp.logical_and(on_top, is_last), last_row)

        values = [[[None, None] for _ in range(NZ)] for _ in range(TRACERS)]
        for level in range(NZ):
            east = halves(lambda where, lanes: east_ref[level, where, lanes])
            west = to_west_of(east, west_rim(static_west_ref, CHANNELS + level))

            def load_north(where, lanes):
                return north_ref[level, where, lanes]

            north = halves(load_north)
            south = to_south_of(load_north, north, static_south_ref, CHANNELS + level)
            coefs = []
            for half in range(2):
                limit = float(level)
                up = jnp.where(closed, 0.0, north[half])
                open_e, open_w, open_n, open_s = [side[half] > limit for side in shared]

                def into(opened, speed):
                    return jnp.where(opened, DIFFUSE - jnp.minimum(speed, 0.0), 0.0)

                def away(opened, speed):
                    return jnp.where(opened, DIFFUSE + jnp.maximum(speed, 0.0), 0.0)

                from_e, lost_e = into(open_e, east[half]), away(open_e, east[half])
                from_w, lost_w = away(open_w, west[half]), into(open_w, west[half])
                from_n, lost_n = into(open_n, up), away(open_n, up)
                from_s, lost_s = away(open_s, south[half]), into(open_s, south[half])
                kept = 1.0 - ((lost_e + lost_w) + (lost_n + lost_s))
                coefs.append((kept, from_e, from_w, from_n, from_s))
            for tracer in range(TRACERS):
                channel = tracer * NZ + level

                def load_q(where, lanes):
                    return q_ref[channel, where, lanes]

                q = halves(load_q)
                q_e = to_east_of(q, east_rim(from_east_ref, channel))
                q_w = to_west_of(q, west_rim(from_west_ref, channel))
                q_n = to_north_of(load_q, q, top_ref, channel)
                q_s = to_south_of(load_q, q, from_south_ref, channel)
                for half in range(2):
                    kept, from_e, from_w, from_n, from_s = coefs[half]
                    values[tracer][level][half] = (
                        kept * q[half]
                        + (from_e * q_e[half] + from_w * q_w[half])
                        + (from_n * q_n[half] + from_s * q_s[half])
                    )
        for half in range(2):
            lanes = slice(half * LANES, (half + 1) * LANES)
            sides_here = [[values[t][k][half] for k in range(NZ)] for t in range(TRACERS)]
            surface = count[half] > 0.0
            if forced:
                sides_here.append([jnp.where(surface, 1.0, 0.0)] + [None] * (NZ - 1))
            else:
                for tracer in range(TRACERS):
                    forcing = jnp.where(surface, forcing_ref[tracer, rows, lanes], 0.0)
                    sides_here[tracer][0] = sides_here[tracer][0] + forcing
            ratios = []
            partials = [[] for _ in sides_here]
            for level in range(NZ):
                thickness = 1.0 + level / NZ
                upper = lower = None
                if level >= 1:
                    mix = mix_ref[level - 1, rows, lanes]
                    upper = jnp.where(count[half] > float(level), mix * (1.0 / thickness), 0.0)
                if level <= NZ - 2:
                    mix = mix_ref[level, rows, lanes]
                    lower = jnp.where(
                        count[half] > float(level + 1), mix * (1.0 / thickness), 0.0
                    )
                if upper is None:
                    pivot = 1.0 + lower
                elif lower is None:
                    pivot = 1.0 + upper - upper * ratios[-1]
                else:
                    pivot = 1.0 + upper + lower - upper * ratios[-1]
                inverse = 1.0 / pivot
                if lower is not None:
                    ratios.append(lower * inverse)
                for side, partial in zip(sides_here, partials, strict=True):
                    right = side[level]
                    if level >= 1:
                        carried = upper * partial[-1]
                        right = carried if right is None else right + carried
                    partial.append(right * inverse)
            for index, partial in enumerate(partials):
                solved = partial[-1]
                for level in range(NZ - 1, -1, -1):
                    if level < NZ - 1:
                        solved = partial[level] + ratios[level] * solved
                    if index < TRACERS:
                        out_ref[index * NZ + level, rows, lanes] = solved
                    else:
                        gain_ref[level, rows, lanes] = solved
        return carry

    lax.fori_loop(0, ROWS // 8, block_step, 0)


def land_kernel(
    own_ref,
    from_south_ref,
    from_north_ref,
    *refs,
):
    arctic_refs = refs[:ARCTIC]
    solved_ref, gain_ref = refs[ARCTIC : ARCTIC + 2]
    result_ref, flux_ref, forcing_ref = refs[ARCTIC + 2 : ARCTIC + 5]
    to_east_ref, to_west_ref, to_north_ref, to_south_ref = refs[ARCTIC + 5 : ARCTIC + 9]
    lists_ref, cells_ref, spread_ref, column_ref, total_ref, live_ref = refs[ARCTIC + 9 :]

    for slot in range(SLOTS):
        if slot == 0:
            ref, at = own_ref, 0
        elif slot == 1:
            ref, at = from_south_ref, 2 * RIM
        elif slot == 2:
            ref, at = from_north_ref, 2 * RIM
        else:
            ref, at = arctic_refs[slot - 3], 0
        for kind in range(3):
            rows = pl.ds(at + kind * SLOT_ROWS, SLOT_ROWS)
            lists_ref[kind, pl.ds(slot * SLOT_ROWS, SLOT_ROWS), :] = ref[rows, :]
        base = at + 3 * SLOT_ROWS
        for group in range(8):
            both = jnp.concatenate(
                [
                    ref[pl.ds(base + 2 * group, 8, stride=ATMOS_ROWS), :],
                    ref[pl.ds(base + 2 * group + 1, 8, stride=ATMOS_ROWS), :],
                ],
                axis=1,
            )
            spread_ref[group * 8 : group * 8 + 8, :] = both
        whole = spread_ref[...]
        high = whole.astype(BF16)
        low = (whole - high.astype(F32)).astype(BF16)
        cells_ref[slot, 0:64, :] = high
        cells_ref[slot, 64:128, :] = low

    found = jnp.int32(0)
    for index in range(SLOTS * CHUNKS):
        weights = lists_ref[2, pl.ds(index * CHUNK_ROWS, CHUNK_ROWS), :]
        live_ref[found] = index
        found = found + (jnp.max(weights) > 0.0).astype(jnp.int32)

    total_ref[...] = jnp.zeros_like(total_ref)
    ones, zeros = jnp.ones((), BF16), jnp.zeros((), BF16)
    iota_256 = lax.broadcasted_iota(jnp.int32, (256, LANES), 0).astype(F32).astype(BF16)
    iota_64 = lax.broadcasted_iota(jnp.int32, (ROWS, LANES), 0).astype(F32).astype(BF16)

    def chunk_step(at, carry):
        index = live_ref[at]
        slot = lax.div(index, CHUNKS)
        first = pl.multiple_of(index * CHUNK_ROWS, CHUNK_ROWS)
        rows = pl.ds(first, CHUNK_ROWS)
        source = lists_ref[0, rows, :]
        target = lists_ref[1, rows, :]
        weight = lists_ref[2, rows, :]
        source_group = jnp.floor(source * (1.0 / 256.0))
        source_cell = source - source_group * 256.0
        target_row = jnp.floor(target * (1.0 / COLUMNS))
        target_column = target - target_row * COLUMNS

        def hot(values, entry, iota):
            line = jnp.broadcast_to(values[entry : entry + 1, :].astype(BF16), iota.shape)
            return jnp.where(line == iota, ones, zeros)

        cell_hot = jnp.concatenate([hot(source_cell, e, iota_256) for e in range(CHUNK_ROWS)], axis=1)
        spread = jnp.dot(cells_ref[slot], cell_hot, preferred_element_type=F32)
        spread = spread[:64] + spread[64:]
        weighted = []
        for entry in range(CHUNK_ROWS):
            lanes = slice(entry * LANES, (entry + 1) * LANES)
            group_here = jnp.broadcast_to(source_group[entry : entry + 1, :], (8, LANES))
            picked = jnp.zeros((8, LANES), F32)
            for group in range(8):
                picked = jnp.where(
                    group_here == float(group), spread[group * 8 : group * 8 + 8, lanes], picked
                )
            weighted.append(picked * weight[entry : entry + 1, :])
        for entry in range(CHUNK_ROWS):
            row_hot = hot(target_row, entry, iota_64)
            high = weighted[entry].astype(BF16)
            low = (weighted[entry] - high.astype(F32)).astype(BF16)
            for part, values in enumerate((high, low)):
                lanes = slice(part * CHUNK + entry * LANES, part * CHUNK + (entry + 1) * LANES)
                for field in range(FIELDS):
                    line = jnp.broadcast_to(values[field : field + 1, :], (ROWS, LANES))
                    column_ref[field * ROWS : (field + 1) * ROWS, lanes] = line * row_hot
        column_hot = jnp.concatenate(
            [hot(target_column, e, iota_256) for e in range(CHUNK_ROWS)], axis=1
        )
        total_ref[...] += lax.dot_general(
            column_ref[...],
            jnp.concatenate([column_hot, column_hot], axis=1),
            (((1,), (1,)), ((), ())),
            preferred_element_type=F32,
        )
        return carry

    lax.fori_loop(0, found, chunk_step, 0)

    def finish(block, carry):
        rows = pl.ds(pl.multiple_of(block * 8, 8), 8)
        flux = []
        for field in range(FIELDS):
            value = total_ref[pl.ds(pl.multiple_of(field * ROWS + block * 8, 8), 8), :]
            flux_ref[field, rows, :] = value
            flux.append(value)
        heat = flux[0] + flux[1] + flux[2] + flux[3] + flux[4]
        salt = flux[7] - flux[5] - flux[6]
        forcing_ref[0, rows, :] = heat
        forcing_ref[1, rows, :] = salt
        for level in range(NZ):
            gain = gain_ref[level, rows, :]
            for tracer, forcing in enumerate((heat, salt)):
                channel = tracer * NZ + level
                result_ref[channel, rows, :] = solved_ref[channel, rows, :] + forcing * gain
        return carry

    lax.fori_loop(0, ROWS // 8, finish, 0)
    pack_columns(
        lambda channel, row: (result_ref[channel, pl.ds(row, 8), LANES:], LANES - 1),
        range(CHANNELS),
        to_east_ref,
    )
    pack_columns(
        lambda channel, row: (result_ref[channel, pl.ds(row, 8), :LANES], 0),
        range(CHANNELS),
        to_west_ref,
    )
    to_north_ref[...] = jnp.zeros((2 * RIM, LANES), F32)
    to_south_ref[...] = jnp.zeros((2 * RIM, LANES), F32)
    for channel in range(CHANNELS):
        pack_row(result_ref[channel, ROWS - 1 : ROWS, :], channel, to_north_ref)
        pack_row(result_ref[channel, 0:1, :], channel, to_south_ref)


EASTWARD = [(i, (i + 1) % GX) for i in range(GX)]
WESTWARD = [((i + 1) % GX, i) for i in range(GX)]
NORTHWARD = [(i, i + 1) for i in range(GY - 1)]
SOUTHWARD = [(i + 1, i) for i in range(GY - 1)]
FOLD = [(x * GY + GY - 1, (GX - 1 - x) * GY + GY - 1) for x in range(GX)]


def arctic_pairs(step):
    pairs = [(FIRST_ARCTIC + (step + 1) % ARCTIC, GY - 1)]
    if step < ARCTIC - 1:
        pairs.append((FIRST_ARCTIC + step, GY - 2))
    return pairs


def exchange(to_east, to_west, to_north, to_south, fold):
    return (
        lax.ppermute(to_east, "gx", EASTWARD),
        lax.ppermute(to_west, "gx", WESTWARD),
        lax.ppermute(to_north, "gy", NORTHWARD),
        lax.ppermute(to_south, "gy", SOUTHWARD),
        lax.ppermute(fold, ("gx", "gy"), FOLD),
    )


def local(
    tracers,
    east_speed,
    north_speed,
    vertical_mix,
    level_count,
    atmosphere_flux,
    intersection_source,
    intersection_target,
    intersection_weight,
):
    q = tracers.reshape(CHANNELS, ROWS, COLUMNS)
    column_rim, row_rim = (ROWS, LANES), (2 * RIM, LANES)
    near = (2 * RIM + PAYLOAD, LANES)
    packed = call(
        pack_kernel,
        [column_rim, column_rim, near, near] + [(PAYLOAD, LANES)] * (1 + ARCTIC),
        [
            q,
            east_speed,
            north_speed,
            level_count,
            atmosphere_flux,
            intersection_source,
            intersection_target,
            intersection_weight,
        ],
    )
    to_east, to_west, to_north, to_south, own = packed[:5]
    rims = exchange(to_east, to_west, to_north, to_south, to_north[: 2 * RIM])
    arctic = [
        lax.ppermute(slot, "gy", arctic_pairs(step)) for step, slot in enumerate(packed[5:])
    ]
    statics = [east_speed, north_speed, level_count, vertical_mix]
    rim_scratch = [pltpu.VMEM(row_rim, F32), pltpu.VMEM(row_rim, F32)]
    solved, gain = call(
        functools.partial(step_kernel, True),
        [q.shape, east_speed.shape],
        [q, *rims, *rims, *statics],
        rim_scratch,
        moved=10_000_000,
    )
    result, flux, forcing, *out_rims = call(
        land_kernel,
        [q.shape, (FIELDS, ROWS, COLUMNS), (TRACERS, ROWS, COLUMNS), column_rim, column_rim, row_rim, row_rim],
        [own, rims[2], rims[3], *arctic, solved, gain],
        [
            pltpu.VMEM((3, SLOTS * SLOT_ROWS, LANES), F32),
            pltpu.VMEM((SLOTS, 128, 256), BF16),
            pltpu.VMEM((64, 256), F32),
            pltpu.VMEM((FIELDS * ROWS, 2 * CHUNK), BF16),
            pltpu.VMEM((FIELDS * ROWS, COLUMNS), F32),
            pltpu.SMEM((SLOTS * CHUNKS + 1,), jnp.int32),
        ],
        moved=60_000_000,
    )
    second = exchange(*out_rims, out_rims[2])
    (result,) = call(
        functools.partial(step_kernel, False),
        [q.shape],
        [result, *second, *rims, *statics, forcing],
        rim_scratch,
        moved=10_000_000,
    )
    return result.reshape(tracers.shape), flux


def solution(mesh):
    in_specs = (
        P(None, None, "gy", "gx"),
        P(None, "gy", "gx"),
        P(None, "gy", "gx"),
        P(None, "gy", "gx"),
        P("gy", "gx"),
        P(None, "gy", "gx"),
        P("gy", "gx"),
        P("gy", "gx"),
        P("gy", "gx"),
    )
    out_specs = (P(None, None, "gy", "gx"), P(None, "gy", "gx"))
    return jax.shard_map(local, mesh=mesh, in_specs=in_specs, out_specs=out_specs, check_vma=False)
```

```python
import functools

import jax
import jax.numpy as jnp
from jax import lax
from jax.experimental import pallas as pl
from jax.experimental.pallas import tpu as pltpu
from jax.sharding import PartitionSpec as P

DIFFUSE = 0.05
FIELDS = 8
TRACERS = 2
NZ = 8
ROWS = 64
COLUMNS = 256
LANES = 128
GX = 8
GY = 16
SLOT_ROWS = 32
ATMOS_ROWS = 16
HELPERS = ((8, GY - 2), (13, GY - 1))
ENTRY_STEPS = (
    ((9, 8), (10, 13), (7, 14), (8, 15)),
    ((10, 8), (11, 13), (12, 14), (7, 15)),
    ((11, 8), (12, 13), (9, 15)),
)
HELPED_BY = {helper: target for helper, target in HELPERS}
CHANNELS = TRACERS * NZ
COUNT_AT = 24
RIM = 32
PAYLOAD = 3 * SLOT_ROWS + FIELDS * ATMOS_ROWS
CHUNK_ROWS = 16
CHUNK = CHUNK_ROWS * LANES
CHUNKS = SLOT_ROWS // CHUNK_ROWS
VMEM_LIMIT = 48 * 1024 * 1024
F32 = jnp.float32
BF16 = jnp.bfloat16
F8 = jnp.float8_e4m3fn
LOW_TOP = 65536.0


def call(kernel, out_shapes, operands, scratch=(), flops=0, moved=4_000_000, in_hbm=False):
    place = pl.ANY if in_hbm else pltpu.VMEM
    return pl.pallas_call(
        kernel,
        out_shape=[jax.ShapeDtypeStruct(shape, F32) for shape in out_shapes],
        in_specs=[pl.BlockSpec(memory_space=place) for _ in operands],
        out_specs=[pl.BlockSpec(memory_space=pltpu.VMEM) for _ in out_shapes],
        scratch_shapes=list(scratch),
        compiler_params=pltpu.CompilerParams(vmem_limit_bytes=VMEM_LIMIT),
        cost_estimate=pl.CostEstimate(flops=flops, bytes_accessed=moved, transcendentals=0),
    )(*operands)


def pack_columns(pick, channels, out_ref):
    lane = lax.broadcasted_iota(jnp.int32, (8, LANES), 1)
    for block in range(ROWS // 8):
        tile = jnp.zeros((8, LANES), F32)
        for channel in channels:
            value, at = pick(channel, block * 8)
            shift = (channel - at) % LANES
            moved = pltpu.roll(value, shift, axis=1) if shift else value
            tile = jnp.where(lane == channel, moved, tile)
        out_ref[pl.ds(block * 8, 8), :] = tile


def pack_row(value, channel, out_ref):
    out_ref[pl.ds(channel, 1), :] = value[:, :LANES]
    out_ref[pl.ds(RIM + channel, 1), :] = value[:, LANES:]


def is_even():
    return lax.rem(lax.axis_index("gy"), 2) == 0


def pack_rows(top_of, bottom_of, channels, sibling_ref, other_ref):
    even = is_even()
    zeros = jnp.zeros((2 * RIM, LANES), F32)
    sibling_ref[0 : 2 * RIM, :] = zeros
    other_ref[0 : 2 * RIM, :] = zeros
    for channel in channels:
        top, bottom = top_of(channel), bottom_of(channel)
        pack_row(jnp.where(even, top, bottom), channel, sibling_ref)
        pack_row(jnp.where(even, bottom, top), channel, other_ref)


def chosen(here, table, default):
    for key, value in table.items():
        default = jnp.where(here == key, value, default)
    return default


def pack_kernel(
    tracers_hbm,
    east_hbm,
    north_hbm,
    count_hbm,
    atmos_hbm,
    source_hbm,
    target_hbm,
    weight_hbm,
    to_east_ref,
    to_west_ref,
    sibling_ref,
    other_ref,
    first_ref,
    second_ref,
    *refs,
):
    entry_refs, scratch = refs[: len(ENTRY_STEPS)], refs[len(ENTRY_STEPS) :]
    tracers_ref, east_ref, north_ref, count_ref, atmos_ref, source_ref, target_ref, weight_ref = scratch[:8]
    sems = scratch[8]
    here = lax.axis_index("gy")
    even = is_even()
    lists = ((source_hbm, source_ref), (target_hbm, target_ref), (weight_hbm, weight_ref))
    copies = [
        *lists,
        (atmos_hbm, atmos_ref),
        (tracers_hbm, tracers_ref),
        (east_hbm.at[:, :, pl.ds(LANES, LANES)], east_ref),
        (north_hbm.at[:, pl.ds(ROWS - 8, 8), :], north_ref),
        (count_hbm, count_ref),
    ]
    copies = [
        pltpu.make_async_copy(source, into, sems.at[n]) for n, (source, into) in enumerate(copies)
    ]
    for copy in copies:
        copy.start()
    for copy in copies[:4]:
        copy.wait()

    def slot_into(out_ref, at, tile, valid=None):
        rows = pl.ds(pl.multiple_of(tile * SLOT_ROWS, SLOT_ROWS), SLOT_ROWS)
        out_ref[at : at + SLOT_ROWS, :] = source_ref[rows, :].astype(F32)
        out_ref[at + SLOT_ROWS : at + 2 * SLOT_ROWS, :] = target_ref[rows, :].astype(F32)
        weight = weight_ref[rows, :]
        if valid is not None:
            weight = jnp.where(valid, weight, 0.0)
        out_ref[at + 2 * SLOT_ROWS : at + 3 * SLOT_ROWS, :] = weight
        for field in range(FIELDS):
            for row in range(ATMOS_ROWS):
                to = at + 3 * SLOT_ROWS + row * FIELDS + field
                out_ref[to : to + 1, :] = atmos_ref[field, row : row + 1, :]

    for pairs, out_ref in zip(ENTRY_STEPS, entry_refs, strict=True):
        table = {source: HELPED_BY.get(target, target) for source, target in pairs}
        slot_into(out_ref, 0, chosen(here, table, here))
    slot_into(first_ref, 0, chosen(here, HELPED_BY, here))
    helps = functools.reduce(jnp.logical_or, [here == helper for helper in HELPED_BY])
    slot_into(second_ref, 0, here, helps)
    slot_into(sibling_ref, 2 * RIM, jnp.where(even, here + 1, here - 1))
    away = jnp.clip(jnp.where(even, here - 1, here + 1), 0, GY - 1)
    slot_into(other_ref, 2 * RIM, away, here != GY - 1)

    for copy in copies[4:]:
        copy.wait()

    def east_column(channel, row):
        rows = pl.ds(row, 8)
        if channel < CHANNELS:
            return tracers_ref[channel, rows, LANES:], LANES - 1
        if channel < COUNT_AT:
            return east_ref[channel - CHANNELS, rows, :], LANES - 1
        return count_ref[rows, LANES:].astype(F32), LANES - 1

    def west_column(channel, row):
        rows = pl.ds(row, 8)
        if channel < CHANNELS:
            return tracers_ref[channel, rows, :LANES], 0
        return count_ref[rows, :LANES].astype(F32), 0

    pack_columns(east_column, [*range(CHANNELS + NZ), COUNT_AT], to_east_ref)
    pack_columns(west_column, [*range(CHANNELS), COUNT_AT], to_west_ref)

    def top_of(channel):
        if channel < CHANNELS:
            return tracers_ref[channel, ROWS - 1 : ROWS, :]
        if channel < COUNT_AT:
            return north_ref[channel - CHANNELS, 7:8, :]
        return count_ref[ROWS - 1 : ROWS, :].astype(F32)

    def bottom_of(channel):
        if channel < CHANNELS:
            return tracers_ref[channel, 0:1, :]
        if channel < COUNT_AT:
            return jnp.zeros((1, COLUMNS), F32)
        return count_ref[0:1, :].astype(F32)

    pack_rows(top_of, bottom_of, range(COUNT_AT + 1), sibling_ref, other_ref)


def step_kernel(
    forced,
    q_ref,
    from_west_ref,
    from_east_ref,
    from_sibling_ref,
    from_other_ref,
    static_west_ref,
    static_east_ref,
    static_sibling_ref,
    static_other_ref,
    east_ref,
    north_ref,
    count_ref,
    mix_ref,
    *more_refs,
):
    if forced:
        out_ref, gain_ref = more_refs[:2]
    else:
        forcing_ref, out_ref = more_refs[:2]
    from_south_ref, top_ref, static_south_ref, static_top_ref = more_refs[2:]
    even = is_even()
    on_top = lax.axis_index("gy") == GY - 1
    lane = lax.broadcasted_iota(jnp.int32, (8, LANES), 1)
    row = lax.broadcasted_iota(jnp.int32, (8, LANES), 0)
    first_lane, last_lane = lane == 0, lane == LANES - 1
    first_row, last_row = row == 0, row == 7

    def set_rims(sibling_rim, other_rim, south, north):
        @pl.when(even)
        def _():
            south[...] = other_rim[0 : 2 * RIM, :]
            north[...] = sibling_rim[0 : 2 * RIM, :]

        @pl.when(jnp.logical_not(even))
        def _():
            south[...] = sibling_rim[0 : 2 * RIM, :]
            north[...] = other_rim[0 : 2 * RIM, :]

        @pl.when(on_top)
        def _():
            flipped = LANES - 1 - lane
            for half in range(2):
                for block in range(RIM // 8):
                    rows = other_rim[pl.ds((1 - half) * RIM + block * 8, 8), :]
                    north[pl.ds(half * RIM + block * 8, 8), :] = jnp.take_along_axis(
                        rows, flipped, axis=1, mode="promise_in_bounds"
                    )

    set_rims(from_sibling_ref, from_other_ref, from_south_ref, top_ref)
    set_rims(static_sibling_ref, static_other_ref, static_south_ref, static_top_ref)

    def block_step(block, carry):
        at = pl.multiple_of(block * 8, 8)
        below = pl.multiple_of(jnp.maximum(block - 1, 0) * 8, 8)
        above = pl.multiple_of(jnp.minimum(block + 1, ROWS // 8 - 1) * 8, 8)
        is_first, is_last = block == 0, block == ROWS // 8 - 1
        rows = pl.ds(at, 8)

        def halves(load):
            return [load(rows, slice(0, LANES)), load(rows, slice(LANES, 2 * LANES))]

        def to_west_of(parts, rim):
            low = jnp.where(last_lane, rim, parts[0])
            high = jnp.where(last_lane, parts[0], parts[1])
            return [pltpu.roll(low, 1, axis=1), pltpu.roll(high, 1, axis=1)]

        def to_east_of(parts, rim):
            low = jnp.where(first_lane, parts[1], parts[0])
            high = jnp.where(first_lane, rim, parts[1])
            return [
                pltpu.roll(low, LANES - 1, axis=1),
                pltpu.roll(high, LANES - 1, axis=1),
            ]

        def to_south_of(load, parts, rim_ref, channel):
            found = []
            for half in range(2):
                lanes = slice(half * LANES, (half + 1) * LANES)
                rim = jnp.broadcast_to(
                    rim_ref[half * RIM + channel : half * RIM + channel + 1, :], (8, LANES)
                )
                near = jnp.where(is_first, rim, load(pl.ds(below, 8), lanes))
                found.append(pltpu.roll(jnp.where(last_row, near, parts[half]), 1, axis=0))
            return found

        def to_north_of(load, parts, rim_ref, channel):
            found = []
            for half in range(2):
                lanes = slice(half * LANES, (half + 1) * LANES)
                rim = jnp.broadcast_to(
                    rim_ref[half * RIM + channel : half * RIM + channel + 1, :], (8, LANES)
                )
                near = jnp.where(is_last, rim, load(pl.ds(above, 8), lanes))
                found.append(pltpu.roll(jnp.where(first_row, near, parts[half]), 7, axis=0))
            return found

        def west_rim(ref, channel):
            return pltpu.roll(ref[rows, :], (LANES - 1 - channel) % LANES, axis=1)

        def east_rim(ref, channel):
            shift = (LANES - channel) % LANES
            return pltpu.roll(ref[rows, :], shift, axis=1) if shift else ref[rows, :]

        def load_count(where, lanes):
            return count_ref[where, lanes].astype(F32)

        count = halves(load_count)
        sides = [
            to_east_of(count, east_rim(static_east_ref, COUNT_AT)),
            to_west_of(count, west_rim(static_west_ref, COUNT_AT)),
            to_north_of(load_count, count, static_top_ref, COUNT_AT),
            to_south_of(load_count, count, static_south_ref, COUNT_AT),
        ]
        shared = [[jnp.minimum(count[half], side[half]) for half in range(2)] for side in sides]
        closed = jnp.logical_and(jnp.logical_and(on_top, is_last), last_row)

        values = [[[None, None] for _ in range(NZ)] for _ in range(TRACERS)]
        for level in range(NZ):
            east = halves(lambda where, lanes: east_ref[level, where, lanes])
            west = to_west_of(east, west_rim(static_west_ref, CHANNELS + level))

            def load_north(where, lanes):
                return north_ref[level, where, lanes]

            north = halves(load_north)
            south = to_south_of(load_north, north, static_south_ref, CHANNELS + level)
            coefs = []
            for half in range(2):
                limit = float(level)
                up = jnp.where(closed, 0.0, north[half])
                open_e, open_w, open_n, open_s = [side[half] > limit for side in shared]

                def into(opened, speed):
                    return jnp.where(opened, DIFFUSE - jnp.minimum(speed, 0.0), 0.0)

                def away(opened, speed):
                    return jnp.where(opened, DIFFUSE + jnp.maximum(speed, 0.0), 0.0)

                from_e, lost_e = into(open_e, east[half]), away(open_e, east[half])
                from_w, lost_w = away(open_w, west[half]), into(open_w, west[half])
                from_n, lost_n = into(open_n, up), away(open_n, up)
                from_s, lost_s = away(open_s, south[half]), into(open_s, south[half])
                kept = 1.0 - ((lost_e + lost_w) + (lost_n + lost_s))
                coefs.append((kept, from_e, from_w, from_n, from_s))
            for tracer in range(TRACERS):
                channel = tracer * NZ + level

                def load_q(where, lanes):
                    return q_ref[channel, where, lanes]

                q = halves(load_q)
                q_e = to_east_of(q, east_rim(from_east_ref, channel))
                q_w = to_west_of(q, west_rim(from_west_ref, channel))
                q_n = to_north_of(load_q, q, top_ref, channel)
                q_s = to_south_of(load_q, q, from_south_ref, channel)
                for half in range(2):
                    kept, from_e, from_w, from_n, from_s = coefs[half]
                    values[tracer][level][half] = (
                        kept * q[half]
                        + (from_e * q_e[half] + from_w * q_w[half])
                        + (from_n * q_n[half] + from_s * q_s[half])
                    )
        for half in range(2):
            lanes = slice(half * LANES, (half + 1) * LANES)
            sides_here = [[values[t][k][half] for k in range(NZ)] for t in range(TRACERS)]
            surface = count[half] > 0.0
            if forced:
                sides_here.append([jnp.where(surface, 1.0, 0.0)] + [None] * (NZ - 1))
            else:
                for tracer in range(TRACERS):
                    forcing = jnp.where(surface, forcing_ref[tracer, rows, lanes], 0.0)
                    sides_here[tracer][0] = sides_here[tracer][0] + forcing
            ratios = []
            partials = [[] for _ in sides_here]
            for level in range(NZ):
                thickness = 1.0 + level / NZ
                upper = lower = None
                if level >= 1:
                    mix = mix_ref[level - 1, rows, lanes]
                    upper = jnp.where(count[half] > float(level), mix * (1.0 / thickness), 0.0)
                if level <= NZ - 2:
                    mix = mix_ref[level, rows, lanes]
                    lower = jnp.where(
                        count[half] > float(level + 1), mix * (1.0 / thickness), 0.0
                    )
                if upper is None:
                    pivot = 1.0 + lower
                elif lower is None:
                    pivot = 1.0 + upper - upper * ratios[-1]
                else:
                    pivot = 1.0 + upper + lower - upper * ratios[-1]
                inverse = 1.0 / pivot
                if lower is not None:
                    ratios.append(lower * inverse)
                for side, partial in zip(sides_here, partials, strict=True):
                    right = side[level]
                    if level >= 1:
                        carried = upper * partial[-1]
                        right = carried if right is None else right + carried
                    partial.append(right * inverse)
            for index, partial in enumerate(partials):
                solved = partial[-1]
                for level in range(NZ - 1, -1, -1):
                    if level < NZ - 1:
                        solved = partial[level] + ratios[level] * solved
                    if index < TRACERS:
                        out_ref[index * NZ + level, rows, lanes] = solved
                    else:
                        gain_ref[level, rows, lanes] = solved
        return carry

    lax.fori_loop(0, ROWS // 8, block_step, 0)


def land_kernel(offsets, continued, *refs):
    slot_refs, refs = refs[: len(offsets)], refs[len(offsets) :]
    if continued:
        start_ref, refs = refs[0], refs[1:]
    total_ref, lists_ref, cells_ref, high_ref, low_ref, high_hot_ref, low_hot_ref, live_ref = refs
    largest = jnp.zeros((8, LANES), F32)
    for slot, (ref, at) in enumerate(zip(slot_refs, offsets, strict=True)):
        for kind in range(3):
            rows = pl.ds(at + kind * SLOT_ROWS, SLOT_ROWS)
            lists_ref[kind, pl.ds(slot * SLOT_ROWS, SLOT_ROWS), :] = ref[rows, :]
        for row in range(ATMOS_ROWS):
            cells = ref[pl.ds(at + 3 * SLOT_ROWS + row * FIELDS, FIELDS), :]
            cells_ref[slot, row] = cells
            largest = jnp.maximum(largest, jnp.abs(cells))
    scale = LOW_TOP / jnp.maximum(jnp.max(largest), 1e-30)
    unscale = 1.0 / scale

    found = jnp.int32(0)
    for index in range(len(offsets) * CHUNKS):
        weights = lists_ref[2, pl.ds(index * CHUNK_ROWS, CHUNK_ROWS), :]
        live_ref[found] = index
        found = found + (jnp.max(weights) > 0.0).astype(jnp.int32)

    if continued:
        helps = functools.reduce(
            jnp.logical_or, [lax.axis_index("gy") == helper for helper in HELPED_BY]
        )

        @pl.when(helps)
        def _():
            total_ref[...] = jnp.zeros_like(total_ref)

        @pl.when(jnp.logical_not(helps))
        def _():
            total_ref[...] = start_ref[...]
    else:
        total_ref[...] = jnp.zeros_like(total_ref)
    ones, zeros = jnp.ones((), BF16), jnp.zeros((), BF16)
    iota = lax.broadcasted_iota(jnp.int32, (COLUMNS, LANES), 0).astype(F32).astype(BF16)

    def hot(values, entry, count):
        line = jnp.broadcast_to(values[entry : entry + 1, :], (16, LANES)).astype(BF16)
        return [jnp.where(line == iota[at : at + 16], ones, zeros) for at in range(0, count, 16)]

    def chunk_step(at, carry):
        index = live_ref[at]
        slot = lax.div(index, CHUNKS)
        rows = pl.ds(pl.multiple_of(index * CHUNK_ROWS, CHUNK_ROWS), CHUNK_ROWS)
        source, target, weight = lists_ref[0, rows, :], lists_ref[1, rows, :], lists_ref[2, rows, :]
        source_row = jnp.floor(source * (1.0 / LANES))
        source_column = (source - source_row * LANES).astype(jnp.int32)
        target_row = jnp.floor(target * (1.0 / COLUMNS))
        target_column = target - target_row * COLUMNS
        for entry in range(CHUNK_ROWS):
            lanes = slice(entry * LANES, (entry + 1) * LANES)
            row_here = jnp.broadcast_to(source_row[entry : entry + 1, :], (FIELDS, LANES))
            column_here = jnp.broadcast_to(source_column[entry : entry + 1, :], (FIELDS, LANES))
            picked = jnp.zeros((FIELDS, LANES), F32)
            for row in range(ATMOS_ROWS):
                found_here = jnp.take_along_axis(
                    cells_ref[slot, row], column_here, axis=1, mode="promise_in_bounds"
                )
                picked = jnp.where(row_here == float(row), found_here, picked)
            weighted = picked * weight[entry : entry + 1, :]
            high = weighted.astype(BF16).astype(F32)
            low = (weighted - high) * scale
            row_hot = hot(target_row, entry, ROWS)
            for field in range(FIELDS):
                first = field * ROWS
                line = jnp.broadcast_to(high[field : field + 1, :], (16, LANES)).astype(BF16)
                for part in range(4):
                    high_ref[first + part * 16 : first + part * 16 + 16, lanes] = line * row_hot[part]
                line = jnp.broadcast_to(low[field : field + 1, :], (16, LANES)).astype(BF16)
                for part in range(2):
                    both = [line * row_hot[2 * part], line * row_hot[2 * part + 1]]
                    low_ref[first + part * 32 : first + part * 32 + 32, lanes] = jnp.concatenate(
                        both, axis=0
                    ).astype(F8)
            column_hot = hot(target_column, entry, COLUMNS)
            for part in range(COLUMNS // 16):
                high_hot_ref[part * 16 : part * 16 + 16, lanes] = column_hot[part]
            for part in range(COLUMNS // 32):
                low_hot_ref[part * 32 : part * 32 + 32, lanes] = jnp.concatenate(
                    column_hot[2 * part : 2 * part + 2], axis=0
                ).astype(F8)
        over_entries = (((1,), (1,)), ((), ()))
        total_ref[...] += lax.dot_general(
            high_ref[...], high_hot_ref[...], over_entries, preferred_element_type=F32
        ) + unscale * lax.dot_general(
            low_ref[...], low_hot_ref[...], over_entries, preferred_element_type=F32
        )
        return carry

    lax.fori_loop(0, found, chunk_step, 0)


def finish_kernel(
    total_ref,
    helped_ref,
    solved_ref,
    gain_ref,
    result_ref,
    flux_ref,
    forcing_ref,
    to_east_ref,
    to_west_ref,
    sibling_ref,
    other_ref,
):
    def block_step(block, carry):
        rows = pl.ds(pl.multiple_of(block * 8, 8), 8)
        flux = []
        for field in range(FIELDS):
            from_rows = pl.ds(pl.multiple_of(field * ROWS + block * 8, 8), 8)
            value = total_ref[from_rows, :] + helped_ref[from_rows, :]
            flux_ref[field, rows, :] = value
            flux.append(value)
        heat = flux[0] + flux[1] + flux[2] + flux[3] + flux[4]
        salt = flux[7] - flux[5] - flux[6]
        forcing_ref[0, rows, :] = heat
        forcing_ref[1, rows, :] = salt
        for level in range(NZ):
            gain = gain_ref[level, rows, :]
            for tracer, forcing in enumerate((heat, salt)):
                channel = tracer * NZ + level
                result_ref[channel, rows, :] = solved_ref[channel, rows, :] + forcing * gain
        return carry

    lax.fori_loop(0, ROWS // 8, block_step, 0)
    pack_columns(
        lambda channel, row: (result_ref[channel, pl.ds(row, 8), LANES:], LANES - 1),
        range(CHANNELS),
        to_east_ref,
    )
    pack_columns(
        lambda channel, row: (result_ref[channel, pl.ds(row, 8), :LANES], 0),
        range(CHANNELS),
        to_west_ref,
    )
    pack_rows(
        lambda channel: result_ref[channel, ROWS - 1 : ROWS, :],
        lambda channel: result_ref[channel, 0:1, :],
        range(CHANNELS),
        sibling_ref,
        other_ref,
    )


EASTWARD = [(i, (i + 1) % GX) for i in range(GX)]
WESTWARD = [((i + 1) % GX, i) for i in range(GX)]
SIBLINGS = [(y, y ^ 1) for y in range(GY)]
OTHERS = [
    (x * GY + y, x * GY + (y + 1 if y % 2 else y - 1)) for x in range(GX) for y in range(1, GY - 1)
] + [(x * GY + GY - 1, (GX - 1 - x) * GY + GY - 1) for x in range(GX)]


def exchange(to_east, to_west, sibling, other):
    return (
        lax.ppermute(to_east, "gx", EASTWARD),
        lax.ppermute(to_west, "gx", WESTWARD),
        lax.ppermute(sibling, "gy", SIBLINGS),
        lax.ppermute(other, ("gx", "gy"), OTHERS),
    )


def land(slots, offsets, start=()):
    count = len(slots)
    (total,) = call(
        functools.partial(land_kernel, offsets, bool(start)),
        [(FIELDS * ROWS, COLUMNS)],
        [*slots, *start],
        [
            pltpu.VMEM((3, count * SLOT_ROWS, LANES), F32),
            pltpu.VMEM((count, ATMOS_ROWS, FIELDS, LANES), F32),
            pltpu.VMEM((FIELDS * ROWS, CHUNK), BF16),
            pltpu.VMEM((FIELDS * ROWS, CHUNK), F8),
            pltpu.VMEM((COLUMNS, CHUNK), BF16),
            pltpu.VMEM((COLUMNS, CHUNK), F8),
            pltpu.SMEM((count * CHUNKS + 1,), jnp.int32),
        ],
        flops=4_000_000_000,
        moved=20_000_000,
    )
    return total


def local(
    tracers,
    east_speed,
    north_speed,
    vertical_mix,
    level_count,
    atmosphere_flux,
    intersection_source,
    intersection_target,
    intersection_weight,
):
    q = tracers.reshape(CHANNELS, ROWS, COLUMNS)
    lists = [intersection_source, intersection_target, intersection_weight]
    column_rim, row_rim = (ROWS, LANES), (2 * RIM, LANES)
    near, slot = (2 * RIM + PAYLOAD, LANES), (PAYLOAD, LANES)
    steps = len(ENTRY_STEPS)
    to_east, to_west, sibling, other, first, second, *entries = call(
        pack_kernel,
        [column_rim, column_rim, near, near] + [slot] * (2 + steps),
        [q, east_speed, north_speed, level_count, atmosphere_flux, *lists],
        [
            pltpu.VMEM(q.shape, F32),
            pltpu.VMEM((NZ, ROWS, LANES), F32),
            pltpu.VMEM((NZ, 8, COLUMNS), F32),
            pltpu.VMEM(level_count.shape, jnp.int32),
            pltpu.VMEM(atmosphere_flux.shape, F32),
            *[pltpu.VMEM(part.shape, part.dtype) for part in lists],
            pltpu.SemaphoreType.DMA((8,)),
        ],
        in_hbm=True,
    )
    entries = [
        lax.ppermute(part, "gy", list(pairs))
        for part, pairs in zip(entries, ENTRY_STEPS, strict=True)
    ]
    rims = exchange(to_east, to_west, sibling, other)
    partial = land([first, *entries], (0,) * (1 + steps))
    helped = lax.ppermute(partial, "gy", list(HELPERS))
    total = land([second, rims[2], rims[3]], (0, 2 * RIM, 2 * RIM), (partial,))
    statics = [east_speed, north_speed, level_count, vertical_mix]
    rim_scratch = [pltpu.VMEM(row_rim, F32)] * 4
    solved, gain = call(
        functools.partial(step_kernel, True),
        [q.shape, east_speed.shape],
        [q, *rims, *rims, *statics],
        rim_scratch,
        moved=8_000_000,
    )
    result, flux, forcing, *out_rims = call(
        finish_kernel,
        [q.shape, (FIELDS, ROWS, COLUMNS), (TRACERS, ROWS, COLUMNS)]
        + [column_rim, column_rim, row_rim, row_rim],
        [total, helped, solved, gain],
    )
    second_rims = exchange(*out_rims)
    (result,) = call(
        functools.partial(step_kernel, False),
        [q.shape],
        [result, *second_rims, *rims, *statics, forcing],
        rim_scratch,
        moved=8_000_000,
    )
    return result.reshape(tracers.shape), flux


def solution(mesh):
    in_specs = (
        P(None, None, "gy", "gx"),
        P(None, "gy", "gx"),
        P(None, "gy", "gx"),
        P(None, "gy", "gx"),
        P("gy", "gx"),
        P(None, "gy", "gx"),
        P("gy", "gx"),
        P("gy", "gx"),
        P("gy", "gx"),
    )
    out_specs = (P(None, None, "gy", "gx"), P(None, "gy", "gx"))
    return jax.shard_map(local, mesh=mesh, in_specs=in_specs, out_specs=out_specs, check_vma=False)
```

```python
import functools

import jax
import jax.numpy as jnp
from jax import lax
from jax.experimental import pallas as pl
from jax.experimental.pallas import tpu as pltpu
from jax.sharding import PartitionSpec as P

DIFFUSE = 0.05
FIELDS = 8
TRACERS = 2
NZ = 8
ROWS = 64
COLUMNS = 256
LANES = 128
GX = 8
GY = 16
SLOT_ROWS = 32
ATMOS_ROWS = 16
HELPED_BY = {8: GY - 2, 12: GY - 1}
DENSE = ((8, GY - 2), (12, GY - 1))
ENTRY_STEPS = (
    ((10, GY - 2), (7, GY - 1)),
    ((11, GY - 2), (8, GY - 1)),
    ((12, GY - 2), (9, GY - 1)),
    ((10, GY - 1),),
)
CHANNELS = TRACERS * NZ
COUNT_AT = 24
RIM = 32
LIST = 3 * SLOT_ROWS
ATMOS = FIELDS * ATMOS_ROWS
PAYLOAD = LIST + ATMOS
CHUNK_ROWS = 16
CHUNK = CHUNK_ROWS * LANES
CHUNKS = SLOT_ROWS // CHUNK_ROWS
VMEM_LIMIT = 48 * 1024 * 1024
PACK_LIMIT = 63 * 1024 * 1024
F32 = jnp.float32
BF16 = jnp.bfloat16
F8 = jnp.float8_e4m3fn
LOW_TOP = 65536.0


def call(kernel, out_shapes, operands, scratch=(), flops=0, moved=4_000_000, in_hbm=False):
    place = pltpu.HBM if in_hbm else pltpu.VMEM
    return pl.pallas_call(
        kernel,
        out_shape=[jax.ShapeDtypeStruct(shape, F32) for shape in out_shapes],
        in_specs=[pl.BlockSpec(memory_space=place) for _ in operands],
        out_specs=[pl.BlockSpec(memory_space=pltpu.VMEM) for _ in out_shapes],
        scratch_shapes=list(scratch),
        compiler_params=pltpu.CompilerParams(vmem_limit_bytes=PACK_LIMIT if in_hbm else VMEM_LIMIT),
        cost_estimate=pl.CostEstimate(flops=flops, bytes_accessed=moved, transcendentals=0),
    )(*operands)


def pack_columns(pick, channels, out_ref):
    lane = lax.broadcasted_iota(jnp.int32, (8, LANES), 1)
    for block in range(ROWS // 8):
        tile = jnp.zeros((8, LANES), F32)
        for channel in channels:
            value, at = pick(channel, block * 8)
            shift = (channel - at) % LANES
            moved = pltpu.roll(value, shift, axis=1) if shift else value
            tile = jnp.where(lane == channel, moved, tile)
        out_ref[pl.ds(block * 8, 8), :] = tile


def pack_row(value, channel, out_ref):
    out_ref[pl.ds(channel, 1), :] = value[:, :LANES]
    out_ref[pl.ds(RIM + channel, 1), :] = value[:, LANES:]


def is_even():
    return lax.rem(lax.axis_index("gy"), 2) == 0


def pack_rows(top_of, bottom_of, channels, sibling_ref, other_ref):
    even = is_even()
    zeros = jnp.zeros((2 * RIM, LANES), F32)
    sibling_ref[0 : 2 * RIM, :] = zeros
    other_ref[0 : 2 * RIM, :] = zeros
    for channel in channels:
        top, bottom = top_of(channel), bottom_of(channel)
        pack_row(jnp.where(even, top, bottom), channel, sibling_ref)
        pack_row(jnp.where(even, bottom, top), channel, other_ref)


def chosen(here, table, default):
    for key, value in table.items():
        default = jnp.where(here == key, value, default)
    return default


def among(here, table):
    return functools.reduce(jnp.logical_or, [here == key for key in table])


def list_into(lists, out_ref, at, tile, valid=None):
    rows = pl.ds(pl.multiple_of(tile * SLOT_ROWS, SLOT_ROWS), SLOT_ROWS)
    for kind, ref in enumerate(lists):
        part = ref[rows, :].astype(F32)
        if kind == 2 and valid is not None:
            part = jnp.where(valid, part, 0.0)
        out_ref[at + kind * SLOT_ROWS : at + (kind + 1) * SLOT_ROWS, :] = part


def pack_kernel(*refs):
    steps = len(ENTRY_STEPS)
    froms, refs = refs[:8], refs[8:]
    (to_east_ref, to_west_ref, sibling_ref, other_ref), refs = refs[:4], refs[4:]
    entry_refs, intos, (cells_ref, sems) = refs[:steps], refs[steps:-2], refs[-2:]
    tracers_ref, east_ref, north_ref, count_ref, source_ref, target_ref, weight_ref, atmos_ref = intos
    copies = [
        pltpu.make_async_copy(array, into, sems.at[n])
        for n, (array, into) in enumerate(zip(froms, intos, strict=True))
    ]
    for copy in copies:
        copy.start()
    for copy in copies:
        copy.wait()
    here = lax.axis_index("gy")
    even = is_even()
    lists = (source_ref, target_ref, weight_ref)
    for field in range(FIELDS):
        for row in range(ATMOS_ROWS):
            to = row * FIELDS + field
            cells_ref[to : to + 1, :] = atmos_ref[field, row : row + 1, :]
    cells = cells_ref[...]
    for pairs, out_ref in zip(ENTRY_STEPS, entry_refs, strict=True):
        list_into(lists, out_ref, 0, chosen(here, dict(pairs), here))
        out_ref[LIST:PAYLOAD, :] = cells
    partner = here ^ 1
    list_into(lists, sibling_ref, 2 * RIM, chosen(partner, HELPED_BY, partner))
    list_into(lists, sibling_ref, 2 * RIM + LIST, partner, among(partner, HELPED_BY))
    sibling_ref[2 * RIM + 2 * LIST :, :] = cells
    away = jnp.clip(jnp.where(even, here - 1, here + 1), 0, GY - 1)
    below_top = here != GY - 1
    helped = jnp.logical_and(below_top, among(away, HELPED_BY))
    list_into(lists, other_ref, 2 * RIM, chosen(away, HELPED_BY, away), helped)
    list_into(lists, other_ref, 2 * RIM + LIST, away, below_top)
    other_ref[2 * RIM + 2 * LIST :, :] = cells

    def east_column(channel, row):
        rows = pl.ds(row, 8)
        if channel < CHANNELS:
            return tracers_ref[channel, rows, LANES:], LANES - 1
        if channel < COUNT_AT:
            return east_ref[channel - CHANNELS, rows, LANES:], LANES - 1
        return count_ref[rows, LANES:].astype(F32), LANES - 1

    def west_column(channel, row):
        rows = pl.ds(row, 8)
        if channel < CHANNELS:
            return tracers_ref[channel, rows, :LANES], 0
        return count_ref[rows, :LANES].astype(F32), 0

    pack_columns(east_column, [*range(CHANNELS + NZ), COUNT_AT], to_east_ref)
    pack_columns(west_column, [*range(CHANNELS), COUNT_AT], to_west_ref)

    def top_of(channel):
        if channel < CHANNELS:
            return tracers_ref[channel, ROWS - 1 : ROWS, :]
        if channel < COUNT_AT:
            return north_ref[channel - CHANNELS, ROWS - 1 : ROWS, :]
        return count_ref[ROWS - 1 : ROWS, :].astype(F32)

    def bottom_of(channel):
        if channel < CHANNELS:
            return tracers_ref[channel, 0:1, :]
        if channel < COUNT_AT:
            return jnp.zeros((1, COLUMNS), F32)
        return count_ref[0:1, :].astype(F32)

    pack_rows(top_of, bottom_of, range(COUNT_AT + 1), sibling_ref, other_ref)


def step_kernel(
    forced,
    q_ref,
    from_west_ref,
    from_east_ref,
    from_sibling_ref,
    from_other_ref,
    static_west_ref,
    static_east_ref,
    static_sibling_ref,
    static_other_ref,
    east_ref,
    north_ref,
    count_ref,
    mix_ref,
    *more_refs,
):
    if forced:
        out_ref, gain_ref = more_refs[-6:-4]
    else:
        forcing_ref, out_ref = more_refs[:2]
    from_south_ref, top_ref, static_south_ref, static_top_ref = more_refs[-4:]
    even = is_even()
    on_top = lax.axis_index("gy") == GY - 1
    lane = lax.broadcasted_iota(jnp.int32, (8, LANES), 1)
    row = lax.broadcasted_iota(jnp.int32, (8, LANES), 0)
    first_lane, last_lane = lane == 0, lane == LANES - 1
    first_row, last_row = row == 0, row == 7

    def set_rims(sibling_rim, other_rim, south, north):
        @pl.when(even)
        def _():
            south[...] = other_rim[0 : 2 * RIM, :]
            north[...] = sibling_rim[0 : 2 * RIM, :]

        @pl.when(jnp.logical_not(even))
        def _():
            south[...] = sibling_rim[0 : 2 * RIM, :]
            north[...] = other_rim[0 : 2 * RIM, :]

        @pl.when(on_top)
        def _():
            flipped = LANES - 1 - lane
            for half in range(2):
                for block in range(RIM // 8):
                    rows = other_rim[pl.ds((1 - half) * RIM + block * 8, 8), :]
                    north[pl.ds(half * RIM + block * 8, 8), :] = jnp.take_along_axis(
                        rows, flipped, axis=1, mode="promise_in_bounds"
                    )

    set_rims(from_sibling_ref, from_other_ref, from_south_ref, top_ref)
    set_rims(static_sibling_ref, static_other_ref, static_south_ref, static_top_ref)

    def block_step(block, carry):
        at = pl.multiple_of(block * 8, 8)
        below = pl.multiple_of(jnp.maximum(block - 1, 0) * 8, 8)
        above = pl.multiple_of(jnp.minimum(block + 1, ROWS // 8 - 1) * 8, 8)
        is_first, is_last = block == 0, block == ROWS // 8 - 1
        rows = pl.ds(at, 8)

        def halves(load):
            return [load(rows, slice(0, LANES)), load(rows, slice(LANES, 2 * LANES))]

        def to_west_of(parts, rim):
            low = jnp.where(last_lane, rim, parts[0])
            high = jnp.where(last_lane, parts[0], parts[1])
            return [pltpu.roll(low, 1, axis=1), pltpu.roll(high, 1, axis=1)]

        def to_east_of(parts, rim):
            low = jnp.where(first_lane, parts[1], parts[0])
            high = jnp.where(first_lane, rim, parts[1])
            return [
                pltpu.roll(low, LANES - 1, axis=1),
                pltpu.roll(high, LANES - 1, axis=1),
            ]

        def to_south_of(load, parts, rim_ref, channel):
            found = []
            for half in range(2):
                lanes = slice(half * LANES, (half + 1) * LANES)
                rim = jnp.broadcast_to(
                    rim_ref[half * RIM + channel : half * RIM + channel + 1, :], (8, LANES)
                )
                near = jnp.where(is_first, rim, load(pl.ds(below, 8), lanes))
                found.append(pltpu.roll(jnp.where(last_row, near, parts[half]), 1, axis=0))
            return found

        def to_north_of(load, parts, rim_ref, channel):
            found = []
            for half in range(2):
                lanes = slice(half * LANES, (half + 1) * LANES)
                rim = jnp.broadcast_to(
                    rim_ref[half * RIM + channel : half * RIM + channel + 1, :], (8, LANES)
                )
                near = jnp.where(is_last, rim, load(pl.ds(above, 8), lanes))
                found.append(pltpu.roll(jnp.where(first_row, near, parts[half]), 7, axis=0))
            return found

        def west_rim(ref, channel):
            return pltpu.roll(ref[rows, :], (LANES - 1 - channel) % LANES, axis=1)

        def east_rim(ref, channel):
            shift = (LANES - channel) % LANES
            return pltpu.roll(ref[rows, :], shift, axis=1) if shift else ref[rows, :]

        def load_count(where, lanes):
            return count_ref[where, lanes].astype(F32)

        count = halves(load_count)
        sides = [
            to_east_of(count, east_rim(static_east_ref, COUNT_AT)),
            to_west_of(count, west_rim(static_west_ref, COUNT_AT)),
            to_north_of(load_count, count, static_top_ref, COUNT_AT),
            to_south_of(load_count, count, static_south_ref, COUNT_AT),
        ]
        shared = [[jnp.minimum(count[half], side[half]) for half in range(2)] for side in sides]
        closed = jnp.logical_and(jnp.logical_and(on_top, is_last), last_row)

        values = [[[None, None] for _ in range(NZ)] for _ in range(TRACERS)]
        for level in range(NZ):
            east = halves(lambda where, lanes: east_ref[level, where, lanes])
            west = to_west_of(east, west_rim(static_west_ref, CHANNELS + level))

            def load_north(where, lanes):
                return north_ref[level, where, lanes]

            north = halves(load_north)
            south = to_south_of(load_north, north, static_south_ref, CHANNELS + level)
            coefs = []
            for half in range(2):
                limit = float(level)
                up = jnp.where(closed, 0.0, north[half])
                open_e, open_w, open_n, open_s = [side[half] > limit for side in shared]

                def into(opened, speed):
                    return jnp.where(opened, DIFFUSE - jnp.minimum(speed, 0.0), 0.0)

                def away(opened, speed):
                    return jnp.where(opened, DIFFUSE + jnp.maximum(speed, 0.0), 0.0)

                from_e, lost_e = into(open_e, east[half]), away(open_e, east[half])
                from_w, lost_w = away(open_w, west[half]), into(open_w, west[half])
                from_n, lost_n = into(open_n, up), away(open_n, up)
                from_s, lost_s = away(open_s, south[half]), into(open_s, south[half])
                kept = 1.0 - ((lost_e + lost_w) + (lost_n + lost_s))
                coefs.append((kept, from_e, from_w, from_n, from_s))
            for tracer in range(TRACERS):
                channel = tracer * NZ + level

                def load_q(where, lanes):
                    return q_ref[channel, where, lanes]

                q = halves(load_q)
                q_e = to_east_of(q, east_rim(from_east_ref, channel))
                q_w = to_west_of(q, west_rim(from_west_ref, channel))
                q_n = to_north_of(load_q, q, top_ref, channel)
                q_s = to_south_of(load_q, q, from_south_ref, channel)
                for half in range(2):
                    kept, from_e, from_w, from_n, from_s = coefs[half]
                    values[tracer][level][half] = (
                        kept * q[half]
                        + (from_e * q_e[half] + from_w * q_w[half])
                        + (from_n * q_n[half] + from_s * q_s[half])
                    )
        for half in range(2):
            lanes = slice(half * LANES, (half + 1) * LANES)
            sides_here = [[values[t][k][half] for k in range(NZ)] for t in range(TRACERS)]
            surface = count[half] > 0.0
            if forced:
                sides_here.append([jnp.where(surface, 1.0, 0.0)] + [None] * (NZ - 1))
            else:
                for tracer in range(TRACERS):
                    forcing = jnp.where(surface, forcing_ref[tracer, rows, lanes], 0.0)
                    sides_here[tracer][0] = sides_here[tracer][0] + forcing
            ratios = []
            partials = [[] for _ in sides_here]
            for level in range(NZ):
                thickness = 1.0 + level / NZ
                upper = lower = None
                if level >= 1:
                    mix = mix_ref[level - 1, rows, lanes]
                    upper = jnp.where(count[half] > float(level), mix * (1.0 / thickness), 0.0)
                if level <= NZ - 2:
                    mix = mix_ref[level, rows, lanes]
                    lower = jnp.where(
                        count[half] > float(level + 1), mix * (1.0 / thickness), 0.0
                    )
                if upper is None:
                    pivot = 1.0 + lower
                elif lower is None:
                    pivot = 1.0 + upper - upper * ratios[-1]
                else:
                    pivot = 1.0 + upper + lower - upper * ratios[-1]
                inverse = 1.0 / pivot
                if lower is not None:
                    ratios.append(lower * inverse)
                for side, partial in zip(sides_here, partials, strict=True):
                    right = side[level]
                    if level >= 1:
                        carried = upper * partial[-1]
                        right = carried if right is None else right + carried
                    partial.append(right * inverse)
            for index, partial in enumerate(partials):
                solved = partial[-1]
                for level in range(NZ - 1, -1, -1):
                    if level < NZ - 1:
                        solved = partial[level] + ratios[level] * solved
                    if index < TRACERS:
                        out_ref[index * NZ + level, rows, lanes] = solved
                    else:
                        gain_ref[level, rows, lanes] = solved
        return carry

    lax.fori_loop(0, ROWS // 8, block_step, 0)


def land_kernel(slots, own_slot, reset, *refs):
    operand_refs, refs = refs[:-8], refs[-8:]
    if own_slot:
        own, operand_refs = operand_refs[:4], operand_refs[4:]
    here = lax.axis_index("gy")
    helps = among(here, HELPED_BY)
    if reset is not None:
        start_ref = operand_refs[-1]
    total_ref, lists_ref, cells_ref, high_ref, low_ref, high_hot_ref, low_hot_ref, live_ref = refs
    largest = jnp.zeros((8, LANES), F32)
    if own_slot:
        tile = here if reset else chosen(here, HELPED_BY, here)
        rows = pl.ds(pl.multiple_of(tile * SLOT_ROWS, SLOT_ROWS), SLOT_ROWS)
        for kind in range(3):
            part = own[kind][rows, :].astype(F32)
            if kind == 2 and reset:
                part = jnp.where(helps, part, 0.0)
            lists_ref[kind, 0:SLOT_ROWS, :] = part
        for field in range(FIELDS):
            largest = jnp.maximum(largest, jnp.abs(own[3][field, 0:8, :]))
            largest = jnp.maximum(largest, jnp.abs(own[3][field, 8:16, :]))
            for row in range(ATMOS_ROWS):
                cells_ref[0, row, field : field + 1, :] = own[3][field, row : row + 1, :]
    count = own_slot + len(slots)
    for slot, (operand, list_at, cells_at) in enumerate(slots, own_slot):
        ref = operand_refs[operand]
        for kind in range(3):
            rows = pl.ds(list_at + kind * SLOT_ROWS, SLOT_ROWS)
            lists_ref[kind, pl.ds(slot * SLOT_ROWS, SLOT_ROWS), :] = ref[rows, :]
        for row in range(ATMOS_ROWS):
            cells = ref[pl.ds(cells_at + row * FIELDS, FIELDS), :]
            cells_ref[slot, row] = cells
            largest = jnp.maximum(largest, jnp.abs(cells))
    scale = LOW_TOP / jnp.maximum(jnp.max(largest), 1e-30)
    unscale = 1.0 / scale

    found = jnp.int32(0)
    for index in range(count * CHUNKS):
        weights = lists_ref[2, pl.ds(index * CHUNK_ROWS, CHUNK_ROWS), :]
        live_ref[found] = index
        found = found + (jnp.max(weights) > 0.0).astype(jnp.int32)

    if reset is None:
        total_ref[...] = jnp.zeros_like(total_ref)
    elif reset:

        @pl.when(helps)
        def _():
            total_ref[...] = jnp.zeros_like(total_ref)

        @pl.when(jnp.logical_not(helps))
        def _():
            total_ref[...] = start_ref[...]
    else:
        total_ref[...] = start_ref[...]
    ones, zeros = jnp.ones((), BF16), jnp.zeros((), BF16)
    iota = lax.broadcasted_iota(jnp.int32, (COLUMNS, LANES), 0).astype(F32).astype(BF16)

    def hot(values, entry, height):
        line = jnp.broadcast_to(values[entry : entry + 1, :], (16, LANES)).astype(BF16)
        return [jnp.where(line == iota[at : at + 16], ones, zeros) for at in range(0, height, 16)]

    def chunk_step(at, carry):
        index = live_ref[at]
        slot = lax.div(index, CHUNKS)
        rows = pl.ds(pl.multiple_of(index * CHUNK_ROWS, CHUNK_ROWS), CHUNK_ROWS)
        source, target, weight = lists_ref[0, rows, :], lists_ref[1, rows, :], lists_ref[2, rows, :]
        source_row = jnp.floor(source * (1.0 / LANES))
        source_column = (source - source_row * LANES).astype(jnp.int32)
        target_row = jnp.floor(target * (1.0 / COLUMNS))
        target_column = target - target_row * COLUMNS
        for entry in range(CHUNK_ROWS):
            lanes = slice(entry * LANES, (entry + 1) * LANES)
            row_here = jnp.broadcast_to(source_row[entry : entry + 1, :], (FIELDS, LANES))
            column_here = jnp.broadcast_to(source_column[entry : entry + 1, :], (FIELDS, LANES))
            picked = jnp.zeros((FIELDS, LANES), F32)
            for row in range(ATMOS_ROWS):
                found_here = jnp.take_along_axis(
                    cells_ref[slot, row], column_here, axis=1, mode="promise_in_bounds"
                )
                picked = jnp.where(row_here == float(row), found_here, picked)
            weighted = picked * weight[entry : entry + 1, :]
            high = weighted.astype(BF16).astype(F32)
            low = (weighted - high) * scale
            row_hot = hot(target_row, entry, ROWS)
            for field in range(FIELDS):
                first = field * ROWS
                line = jnp.broadcast_to(high[field : field + 1, :], (16, LANES)).astype(BF16)
                for part in range(4):
                    high_ref[first + part * 16 : first + part * 16 + 16, lanes] = line * row_hot[part]
                line = jnp.broadcast_to(low[field : field + 1, :], (16, LANES)).astype(BF16)
                for part in range(2):
                    both = [line * row_hot[2 * part], line * row_hot[2 * part + 1]]
                    low_ref[first + part * 32 : first + part * 32 + 32, lanes] = jnp.concatenate(
                        both, axis=0
                    ).astype(F8)
            column_hot = hot(target_column, entry, COLUMNS)
            for part in range(COLUMNS // 16):
                high_hot_ref[part * 16 : part * 16 + 16, lanes] = column_hot[part]
            for part in range(COLUMNS // 32):
                low_hot_ref[part * 32 : part * 32 + 32, lanes] = jnp.concatenate(
                    column_hot[2 * part : 2 * part + 2], axis=0
                ).astype(F8)
        over_entries = (((1,), (1,)), ((), ()))
        total_ref[...] += lax.dot_general(
            high_ref[...], high_hot_ref[...], over_entries, preferred_element_type=F32
        ) + unscale * lax.dot_general(
            low_ref[...], low_hot_ref[...], over_entries, preferred_element_type=F32
        )
        return carry

    lax.fori_loop(0, found, chunk_step, 0)


def finish_kernel(
    total_ref,
    helped_ref,
    solved_ref,
    gain_ref,
    result_ref,
    flux_ref,
    forcing_ref,
    to_east_ref,
    to_west_ref,
    sibling_ref,
    other_ref,
):
    def block_step(block, carry):
        rows = pl.ds(pl.multiple_of(block * 8, 8), 8)
        flux = []
        for field in range(FIELDS):
            from_rows = pl.ds(pl.multiple_of(field * ROWS + block * 8, 8), 8)
            value = total_ref[from_rows, :] + helped_ref[from_rows, :]
            flux_ref[field, rows, :] = value
            flux.append(value)
        heat = flux[0] + flux[1] + flux[2] + flux[3] + flux[4]
        salt = flux[7] - flux[5] - flux[6]
        forcing_ref[0, rows, :] = heat
        forcing_ref[1, rows, :] = salt
        for level in range(NZ):
            gain = gain_ref[level, rows, :]
            for tracer, forcing in enumerate((heat, salt)):
                channel = tracer * NZ + level
                result_ref[channel, rows, :] = solved_ref[channel, rows, :] + forcing * gain
        return carry

    lax.fori_loop(0, ROWS // 8, block_step, 0)
    pack_columns(
        lambda channel, row: (result_ref[channel, pl.ds(row, 8), LANES:], LANES - 1),
        range(CHANNELS),
        to_east_ref,
    )
    pack_columns(
        lambda channel, row: (result_ref[channel, pl.ds(row, 8), :LANES], 0),
        range(CHANNELS),
        to_west_ref,
    )
    pack_rows(
        lambda channel: result_ref[channel, ROWS - 1 : ROWS, :],
        lambda channel: result_ref[channel, 0:1, :],
        range(CHANNELS),
        sibling_ref,
        other_ref,
    )


EASTWARD = [(i, (i + 1) % GX) for i in range(GX)]
WESTWARD = [((i + 1) % GX, i) for i in range(GX)]
SIBLINGS = [(y, y ^ 1) for y in range(GY)]
OTHERS = [
    (x * GY + y, x * GY + (y + 1 if y % 2 else y - 1)) for x in range(GX) for y in range(1, GY - 1)
] + [(x * GY + GY - 1, (GX - 1 - x) * GY + GY - 1) for x in range(GX)]


def exchange(to_east, to_west, sibling, other):
    return (
        lax.ppermute(to_east, "gx", EASTWARD),
        lax.ppermute(to_west, "gx", WESTWARD),
        lax.ppermute(sibling, "gy", SIBLINGS),
        lax.ppermute(other, ("gx", "gy"), OTHERS),
    )


def land(operands, slots, own_slot, reset):
    count = own_slot + len(slots)
    (total,) = call(
        functools.partial(land_kernel, slots, own_slot, reset),
        [(FIELDS * ROWS, COLUMNS)],
        operands,
        [
            pltpu.VMEM((3, count * SLOT_ROWS, LANES), F32),
            pltpu.VMEM((count, ATMOS_ROWS, FIELDS, LANES), F32),
            pltpu.VMEM((FIELDS * ROWS, CHUNK), BF16),
            pltpu.VMEM((FIELDS * ROWS, CHUNK), F8),
            pltpu.VMEM((COLUMNS, CHUNK), BF16),
            pltpu.VMEM((COLUMNS, CHUNK), F8),
            pltpu.SMEM((count * CHUNKS + 1,), jnp.int32),
        ],
        moved=100_000,
    )
    return total


def local(
    tracers,
    east_speed,
    north_speed,
    vertical_mix,
    level_count,
    atmosphere_flux,
    intersection_source,
    intersection_target,
    intersection_weight,
):
    q = tracers.reshape(CHANNELS, ROWS, COLUMNS)
    statics = [east_speed, north_speed, level_count, vertical_mix]
    lists = [intersection_source, intersection_target, intersection_weight, atmosphere_flux]
    column_rim, row_rim = (ROWS, LANES), (2 * RIM, LANES)
    both = (2 * RIM + LIST + PAYLOAD, LANES)
    steps = len(ENTRY_STEPS)
    packed = call(
        pack_kernel,
        [column_rim, column_rim, both, both] + [(PAYLOAD, LANES)] * steps,
        [q, *statics[:3], *lists],
        [
            *[pltpu.VMEM(part.shape, part.dtype) for part in (q, *statics[:3], *lists)],
            pltpu.VMEM((ATMOS, LANES), F32),
            pltpu.SemaphoreType.DMA((8,)),
        ],
        in_hbm=True,
    )
    entries = [
        lax.ppermute(part, "gy", list(pairs))
        for part, pairs in zip(packed[4:], ENTRY_STEPS, strict=True)
    ]
    own = land(lists, (), 1, None)
    rims = exchange(*packed[:4])
    first, second, cells = 2 * RIM, 2 * RIM + LIST, 2 * RIM + 2 * LIST
    most = land([rims[2], own], ((0, first, cells),), 0, False)
    partial = land([rims[3], *entries, most], ((0, first, cells),), 0, False)
    helped = lax.ppermute(partial, "gy", list(DENSE))
    total = land(
        [*lists, rims[2], rims[3], *entries, partial],
        ((0, second, cells), (1, second, cells))
        + tuple((2 + step, 0, LIST) for step in range(steps)),
        1,
        True,
    )
    rim_scratch = [pltpu.VMEM(row_rim, F32)] * 4
    solved, gain = call(
        functools.partial(step_kernel, True),
        [q.shape, east_speed.shape],
        [q, *rims, *rims, *statics, partial],
        rim_scratch,
        moved=8_000_000,
    )
    result, flux, forcing, *out_rims = call(
        finish_kernel,
        [q.shape, (FIELDS, ROWS, COLUMNS), (TRACERS, ROWS, COLUMNS)]
        + [column_rim, column_rim, row_rim, row_rim],
        [total, helped, solved, gain],
    )
    second_rims = exchange(*out_rims)
    (result,) = call(
        functools.partial(step_kernel, False),
        [q.shape],
        [result, *second_rims, *rims, *statics, forcing],
        rim_scratch,
        moved=8_000_000,
    )
    return result.reshape(tracers.shape), flux


def solution(mesh):
    in_specs = (
        P(None, None, "gy", "gx"),
        P(None, "gy", "gx"),
        P(None, "gy", "gx"),
        P(None, "gy", "gx"),
        P("gy", "gx"),
        P(None, "gy", "gx"),
        P("gy", "gx"),
        P("gy", "gx"),
        P("gy", "gx"),
    )
    out_specs = (P(None, None, "gy", "gx"), P(None, "gy", "gx"))
    return jax.shard_map(local, mesh=mesh, in_specs=in_specs, out_specs=out_specs, check_vma=False)
```

```python
import functools

import jax
import jax.numpy as jnp
from jax import lax
from jax.experimental import pallas as pl
from jax.experimental.pallas import tpu as pltpu
from jax.sharding import PartitionSpec as P

DIFFUSE = 0.05
FIELDS = 8
TRACERS = 2
NZ = 8
ROWS = 64
COLUMNS = 256
LANES = 128
GX = 8
GY = 16
SLOT_ROWS = 32
ATMOS_ROWS = 16
HELPED_BY = {12: GY - 2, 11: GY - 1}
DENSE = ((12, GY - 2), (11, GY - 1))
SENT_AWAY = 13
ENTRY_STEPS = (
    ((7, GY - 2), (8, GY - 1), (10, 12), (9, 11)),
    ((8, GY - 2), (7, GY - 1)),
    ((9, GY - 2), (13, GY - 1)),
)
CHANNELS = TRACERS * NZ
COUNT_AT = 24
RIM = 32
LIST = 3 * SLOT_ROWS
ATMOS = FIELDS * ATMOS_ROWS
PAYLOAD = LIST + ATMOS
CHUNK_ROWS = 16
CHUNK = CHUNK_ROWS * LANES
CHUNKS = SLOT_ROWS // CHUNK_ROWS
VMEM_LIMIT = 48 * 1024 * 1024
PACK_LIMIT = 63 * 1024 * 1024
F32 = jnp.float32
BF16 = jnp.bfloat16
F8 = jnp.float8_e4m3fn
LOW_TOP = 65536.0


def call(
    kernel, out_shapes, operands, scratch=(), flops=0, moved=4_000_000, in_hbm=False, out_hbm=False
):
    place = pltpu.HBM if in_hbm else pltpu.VMEM
    out_place = pl.ANY if out_hbm else pltpu.VMEM
    return pl.pallas_call(
        kernel,
        out_shape=[jax.ShapeDtypeStruct(shape, F32) for shape in out_shapes],
        in_specs=[pl.BlockSpec(memory_space=place) for _ in operands],
        out_specs=[pl.BlockSpec(memory_space=out_place) for _ in out_shapes],
        scratch_shapes=list(scratch),
        compiler_params=pltpu.CompilerParams(vmem_limit_bytes=PACK_LIMIT if in_hbm else VMEM_LIMIT),
        cost_estimate=pl.CostEstimate(flops=flops, bytes_accessed=moved, transcendentals=0),
    )(*operands)


def pack_columns(pick, channels, out_ref):
    lane = lax.broadcasted_iota(jnp.int32, (8, LANES), 1)
    for block in range(ROWS // 8):
        tile = jnp.zeros((8, LANES), F32)
        for channel in channels:
            value, at = pick(channel, block * 8)
            shift = (channel - at) % LANES
            moved = pltpu.roll(value, shift, axis=1) if shift else value
            tile = jnp.where(lane == channel, moved, tile)
        out_ref[pl.ds(block * 8, 8), :] = tile


def pack_row(value, channel, out_ref):
    out_ref[pl.ds(channel, 1), :] = value[:, :LANES]
    out_ref[pl.ds(RIM + channel, 1), :] = value[:, LANES:]


def is_even():
    return lax.rem(lax.axis_index("gy"), 2) == 0


def pack_rows(top_of, bottom_of, channels, sibling_ref, other_ref):
    even = is_even()
    zeros = jnp.zeros((2 * RIM, LANES), F32)
    sibling_ref[0 : 2 * RIM, :] = zeros
    other_ref[0 : 2 * RIM, :] = zeros
    for channel in channels:
        top, bottom = top_of(channel), bottom_of(channel)
        pack_row(jnp.where(even, top, bottom), channel, sibling_ref)
        pack_row(jnp.where(even, bottom, top), channel, other_ref)


def chosen(here, table, default):
    for key, value in table.items():
        default = jnp.where(here == key, value, default)
    return default


def among(here, table):
    return functools.reduce(jnp.logical_or, [here == key for key in table])


def list_into(lists, out_ref, at, tile, valid=None):
    rows = pl.ds(pl.multiple_of(tile * SLOT_ROWS, SLOT_ROWS), SLOT_ROWS)
    for kind, ref in enumerate(lists):
        part = ref[rows, :].astype(F32)
        if kind == 2 and valid is not None:
            part = jnp.where(valid, part, 0.0)
        out_ref[at + kind * SLOT_ROWS : at + (kind + 1) * SLOT_ROWS, :] = part


def pack_kernel(*refs):
    steps = len(ENTRY_STEPS)
    froms, refs = refs[:8], refs[8:]
    (to_east_ref, to_west_ref, sibling_ref, other_ref), refs = refs[:4], refs[4:]
    entry_refs, intos, (cells_ref, sems) = refs[:steps], refs[steps:-2], refs[-2:]
    tracers_ref, east_ref, north_ref, count_ref, source_ref, target_ref, weight_ref, atmos_ref = intos
    copies = [
        pltpu.make_async_copy(array, into, sems.at[n])
        for n, (array, into) in enumerate(zip(froms, intos, strict=True))
    ]
    for copy in copies:
        copy.start()
    for copy in copies[4:]:
        copy.wait()
    here = lax.axis_index("gy")
    even = is_even()
    lists = (source_ref, target_ref, weight_ref)
    for field in range(FIELDS):
        for row in range(ATMOS_ROWS):
            to = row * FIELDS + field
            cells_ref[to : to + 1, :] = atmos_ref[field, row : row + 1, :]
    cells = cells_ref[...]
    for pairs, out_ref in zip(ENTRY_STEPS, entry_refs, strict=True):
        wanted = {source: HELPED_BY.get(to, to) for source, to in pairs}
        list_into(lists, out_ref, 0, chosen(here, wanted, here))
        out_ref[LIST:PAYLOAD, :] = cells
    partner = here ^ 1
    list_into(lists, sibling_ref, 2 * RIM, chosen(partner, HELPED_BY, partner))
    list_into(lists, sibling_ref, 2 * RIM + LIST, partner, among(partner, HELPED_BY))
    sibling_ref[2 * RIM + 2 * LIST :, :] = cells
    away = jnp.clip(jnp.where(even, here - 1, here + 1), 0, GY - 1)
    below_top = here != GY - 1
    helped = jnp.logical_and(below_top, among(away, HELPED_BY))
    list_into(lists, other_ref, 2 * RIM, chosen(away, HELPED_BY, away), helped)
    direct = jnp.logical_and(below_top, here != SENT_AWAY)
    list_into(lists, other_ref, 2 * RIM + LIST, away, direct)
    other_ref[2 * RIM + 2 * LIST :, :] = cells

    for copy in copies[:4]:
        copy.wait()

    def east_column(channel, row):
        rows = pl.ds(row, 8)
        if channel < CHANNELS:
            return tracers_ref[channel, rows, LANES:], LANES - 1
        if channel < COUNT_AT:
            return east_ref[channel - CHANNELS, rows, LANES:], LANES - 1
        return count_ref[rows, LANES:].astype(F32), LANES - 1

    def west_column(channel, row):
        rows = pl.ds(row, 8)
        if channel < CHANNELS:
            return tracers_ref[channel, rows, :LANES], 0
        return count_ref[rows, :LANES].astype(F32), 0

    pack_columns(east_column, [*range(CHANNELS + NZ), COUNT_AT], to_east_ref)
    pack_columns(west_column, [*range(CHANNELS), COUNT_AT], to_west_ref)

    def top_of(channel):
        if channel < CHANNELS:
            return tracers_ref[channel, ROWS - 1 : ROWS, :]
        if channel < COUNT_AT:
            return north_ref[channel - CHANNELS, ROWS - 1 : ROWS, :]
        return count_ref[ROWS - 1 : ROWS, :].astype(F32)

    def bottom_of(channel):
        if channel < CHANNELS:
            return tracers_ref[channel, 0:1, :]
        if channel < COUNT_AT:
            return jnp.zeros((1, COLUMNS), F32)
        return count_ref[0:1, :].astype(F32)

    pack_rows(top_of, bottom_of, range(COUNT_AT + 1), sibling_ref, other_ref)


def step_kernel(
    forced,
    q_ref,
    from_west_ref,
    from_east_ref,
    from_sibling_ref,
    from_other_ref,
    static_west_ref,
    static_east_ref,
    static_sibling_ref,
    static_other_ref,
    east_ref,
    north_ref,
    count_ref,
    mix_ref,
    *more_refs,
):
    if forced:
        out_ref, gain_ref = more_refs[-6:-4]
    else:
        forcing_ref, out_hbm, out_ref, sems = more_refs[:4]
    from_south_ref, top_ref, static_south_ref, static_top_ref = more_refs[-4:]
    even = is_even()
    on_top = lax.axis_index("gy") == GY - 1
    lane = lax.broadcasted_iota(jnp.int32, (8, LANES), 1)
    row = lax.broadcasted_iota(jnp.int32, (8, LANES), 0)
    first_lane, last_lane = lane == 0, lane == LANES - 1
    first_row, last_row = row == 0, row == 7

    def set_rims(sibling_rim, other_rim, south, north):
        @pl.when(even)
        def _():
            south[...] = other_rim[0 : 2 * RIM, :]
            north[...] = sibling_rim[0 : 2 * RIM, :]

        @pl.when(jnp.logical_not(even))
        def _():
            south[...] = sibling_rim[0 : 2 * RIM, :]
            north[...] = other_rim[0 : 2 * RIM, :]

        @pl.when(on_top)
        def _():
            flipped = LANES - 1 - lane
            for half in range(2):
                for block in range(RIM // 8):
                    rows = other_rim[pl.ds((1 - half) * RIM + block * 8, 8), :]
                    north[pl.ds(half * RIM + block * 8, 8), :] = jnp.take_along_axis(
                        rows, flipped, axis=1, mode="promise_in_bounds"
                    )

    set_rims(from_sibling_ref, from_other_ref, from_south_ref, top_ref)
    set_rims(static_sibling_ref, static_other_ref, static_south_ref, static_top_ref)

    def block_step(block, carry):
        at = pl.multiple_of(block * 8, 8)
        below = pl.multiple_of(jnp.maximum(block - 1, 0) * 8, 8)
        above = pl.multiple_of(jnp.minimum(block + 1, ROWS // 8 - 1) * 8, 8)
        is_first, is_last = block == 0, block == ROWS // 8 - 1
        rows = pl.ds(at, 8)

        def halves(load):
            return [load(rows, slice(0, LANES)), load(rows, slice(LANES, 2 * LANES))]

        def to_west_of(parts, rim):
            low = jnp.where(last_lane, rim, parts[0])
            high = jnp.where(last_lane, parts[0], parts[1])
            return [pltpu.roll(low, 1, axis=1), pltpu.roll(high, 1, axis=1)]

        def to_east_of(parts, rim):
            low = jnp.where(first_lane, parts[1], parts[0])
            high = jnp.where(first_lane, rim, parts[1])
            return [
                pltpu.roll(low, LANES - 1, axis=1),
                pltpu.roll(high, LANES - 1, axis=1),
            ]

        def to_south_of(load, parts, rim_ref, channel):
            found = []
            for half in range(2):
                lanes = slice(half * LANES, (half + 1) * LANES)
                rim = jnp.broadcast_to(
                    rim_ref[half * RIM + channel : half * RIM + channel + 1, :], (8, LANES)
                )
                near = jnp.where(is_first, rim, load(pl.ds(below, 8), lanes))
                found.append(pltpu.roll(jnp.where(last_row, near, parts[half]), 1, axis=0))
            return found

        def to_north_of(load, parts, rim_ref, channel):
            found = []
            for half in range(2):
                lanes = slice(half * LANES, (half + 1) * LANES)
                rim = jnp.broadcast_to(
                    rim_ref[half * RIM + channel : half * RIM + channel + 1, :], (8, LANES)
                )
                near = jnp.where(is_last, rim, load(pl.ds(above, 8), lanes))
                found.append(pltpu.roll(jnp.where(first_row, near, parts[half]), 7, axis=0))
            return found

        def west_rim(ref, channel):
            return pltpu.roll(ref[rows, :], (LANES - 1 - channel) % LANES, axis=1)

        def east_rim(ref, channel):
            shift = (LANES - channel) % LANES
            return pltpu.roll(ref[rows, :], shift, axis=1) if shift else ref[rows, :]

        def load_count(where, lanes):
            return count_ref[where, lanes].astype(F32)

        count = halves(load_count)
        sides = [
            to_east_of(count, east_rim(static_east_ref, COUNT_AT)),
            to_west_of(count, west_rim(static_west_ref, COUNT_AT)),
            to_north_of(load_count, count, static_top_ref, COUNT_AT),
            to_south_of(load_count, count, static_south_ref, COUNT_AT),
        ]
        shared = [[jnp.minimum(count[half], side[half]) for half in range(2)] for side in sides]
        closed = jnp.logical_and(jnp.logical_and(on_top, is_last), last_row)

        values = [[[None, None] for _ in range(NZ)] for _ in range(TRACERS)]
        for level in range(NZ):
            east = halves(lambda where, lanes: east_ref[level, where, lanes])
            west = to_west_of(east, west_rim(static_west_ref, CHANNELS + level))

            def load_north(where, lanes):
                return north_ref[level, where, lanes]

            north = halves(load_north)
            south = to_south_of(load_north, north, static_south_ref, CHANNELS + level)
            coefs = []
            for half in range(2):
                limit = float(level)
                up = jnp.where(closed, 0.0, north[half])
                open_e, open_w, open_n, open_s = [side[half] > limit for side in shared]

                def into(opened, speed):
                    return jnp.where(opened, DIFFUSE - jnp.minimum(speed, 0.0), 0.0)

                def away(opened, speed):
                    return jnp.where(opened, DIFFUSE + jnp.maximum(speed, 0.0), 0.0)

                from_e, lost_e = into(open_e, east[half]), away(open_e, east[half])
                from_w, lost_w = away(open_w, west[half]), into(open_w, west[half])
                from_n, lost_n = into(open_n, up), away(open_n, up)
                from_s, lost_s = away(open_s, south[half]), into(open_s, south[half])
                kept = 1.0 - ((lost_e + lost_w) + (lost_n + lost_s))
                coefs.append((kept, from_e, from_w, from_n, from_s))
            for tracer in range(TRACERS):
                channel = tracer * NZ + level

                def load_q(where, lanes):
                    return q_ref[channel, where, lanes]

                q = halves(load_q)
                q_e = to_east_of(q, east_rim(from_east_ref, channel))
                q_w = to_west_of(q, west_rim(from_west_ref, channel))
                q_n = to_north_of(load_q, q, top_ref, channel)
                q_s = to_south_of(load_q, q, from_south_ref, channel)
                for half in range(2):
                    kept, from_e, from_w, from_n, from_s = coefs[half]
                    values[tracer][level][half] = (
                        kept * q[half]
                        + (from_e * q_e[half] + from_w * q_w[half])
                        + (from_n * q_n[half] + from_s * q_s[half])
                    )
        for half in range(2):
            lanes = slice(half * LANES, (half + 1) * LANES)
            sides_here = [[values[t][k][half] for k in range(NZ)] for t in range(TRACERS)]
            surface = count[half] > 0.0
            if forced:
                sides_here.append([jnp.where(surface, 1.0, 0.0)] + [None] * (NZ - 1))
            else:
                for tracer in range(TRACERS):
                    forcing = jnp.where(surface, forcing_ref[tracer, rows, lanes], 0.0)
                    sides_here[tracer][0] = sides_here[tracer][0] + forcing
            ratios = []
            partials = [[] for _ in sides_here]
            for level in range(NZ):
                thickness = 1.0 + level / NZ
                upper = lower = None
                if level >= 1:
                    mix = mix_ref[level - 1, rows, lanes]
                    upper = jnp.where(count[half] > float(level), mix * (1.0 / thickness), 0.0)
                if level <= NZ - 2:
                    mix = mix_ref[level, rows, lanes]
                    lower = jnp.where(
                        count[half] > float(level + 1), mix * (1.0 / thickness), 0.0
                    )
                if upper is None:
                    pivot = 1.0 + lower
                elif lower is None:
                    pivot = 1.0 + upper - upper * ratios[-1]
                else:
                    pivot = 1.0 + upper + lower - upper * ratios[-1]
                inverse = 1.0 / pivot
                if lower is not None:
                    ratios.append(lower * inverse)
                for side, partial in zip(sides_here, partials, strict=True):
                    right = side[level]
                    if level >= 1:
                        carried = upper * partial[-1]
                        right = carried if right is None else right + carried
                    partial.append(right * inverse)
            for index, partial in enumerate(partials):
                solved = partial[-1]
                for level in range(NZ - 1, -1, -1):
                    if level < NZ - 1:
                        solved = partial[level] + ratios[level] * solved
                    if index < TRACERS:
                        out_ref[index * NZ + level, rows, lanes] = solved
                    else:
                        gain_ref[level, rows, lanes] = solved
        if not forced:
            block_copy(block).start()
        return carry

    def block_copy(block):
        rows = pl.ds(pl.multiple_of(block * 8, 8), 8)
        return pltpu.make_async_copy(out_ref.at[:, rows, :], out_hbm.at[:, rows, :], sems.at[block])

    lax.fori_loop(0, ROWS // 8, block_step, 0)
    if not forced:
        for block in range(ROWS // 8):
            block_copy(block).wait()


def land_kernel(slots, own_slot, reset, *refs):
    operand_refs, refs = refs[:-8], refs[-8:]
    if own_slot:
        own, operand_refs = operand_refs[:4], operand_refs[4:]
    here = lax.axis_index("gy")
    helps = among(here, HELPED_BY)
    if reset is not None:
        start_ref = operand_refs[-1]
    total_ref, lists_ref, cells_ref, high_ref, low_ref, high_hot_ref, low_hot_ref, live_ref = refs
    largest = jnp.zeros((8, LANES), F32)
    if own_slot:
        tile = here if reset else chosen(here, HELPED_BY, here)
        rows = pl.ds(pl.multiple_of(tile * SLOT_ROWS, SLOT_ROWS), SLOT_ROWS)
        for kind in range(3):
            part = own[kind][rows, :].astype(F32)
            if kind == 2 and reset:
                part = jnp.where(helps, part, 0.0)
            lists_ref[kind, 0:SLOT_ROWS, :] = part
        for field in range(FIELDS):
            largest = jnp.maximum(largest, jnp.abs(own[3][field, 0:8, :]))
            largest = jnp.maximum(largest, jnp.abs(own[3][field, 8:16, :]))
            for row in range(ATMOS_ROWS):
                cells_ref[0, row, field : field + 1, :] = own[3][field, row : row + 1, :]
    count = own_slot + len(slots)
    for slot, (operand, list_at, cells_at, only) in enumerate(slots, own_slot):
        ref = operand_refs[operand]
        for kind in range(3):
            rows = pl.ds(list_at + kind * SLOT_ROWS, SLOT_ROWS)
            part = ref[rows, :]
            if kind == 2 and only is not None:
                part = jnp.where(helps == only, part, 0.0)
            lists_ref[kind, pl.ds(slot * SLOT_ROWS, SLOT_ROWS), :] = part
        for row in range(ATMOS_ROWS):
            cells = ref[pl.ds(cells_at + row * FIELDS, FIELDS), :]
            cells_ref[slot, row] = cells
            largest = jnp.maximum(largest, jnp.abs(cells))
    scale = LOW_TOP / jnp.maximum(jnp.max(largest), 1e-30)
    unscale = 1.0 / scale

    found = jnp.int32(0)
    for index in range(count * CHUNKS):
        weights = lists_ref[2, pl.ds(index * CHUNK_ROWS, CHUNK_ROWS), :]
        live_ref[found] = index
        found = found + (jnp.max(weights) > 0.0).astype(jnp.int32)

    if reset is None:
        total_ref[...] = jnp.zeros_like(total_ref)
    elif reset:

        @pl.when(helps)
        def _():
            total_ref[...] = jnp.zeros_like(total_ref)

        @pl.when(jnp.logical_not(helps))
        def _():
            total_ref[...] = start_ref[...]
    else:
        total_ref[...] = start_ref[...]
    ones, zeros = jnp.ones((), BF16), jnp.zeros((), BF16)
    iota = lax.broadcasted_iota(jnp.int32, (COLUMNS, LANES), 0).astype(F32).astype(BF16)

    def hot(values, entry, height):
        line = jnp.broadcast_to(values[entry : entry + 1, :], (16, LANES)).astype(BF16)
        return [jnp.where(line == iota[at : at + 16], ones, zeros) for at in range(0, height, 16)]

    def chunk_step(at, carry):
        index = live_ref[at]
        slot = lax.div(index, CHUNKS)
        rows = pl.ds(pl.multiple_of(index * CHUNK_ROWS, CHUNK_ROWS), CHUNK_ROWS)
        source, target, weight = lists_ref[0, rows, :], lists_ref[1, rows, :], lists_ref[2, rows, :]
        source_row = jnp.floor(source * (1.0 / LANES))
        source_column = (source - source_row * LANES).astype(jnp.int32)
        target_row = jnp.floor(target * (1.0 / COLUMNS))
        target_column = target - target_row * COLUMNS
        for entry in range(CHUNK_ROWS):
            lanes = slice(entry * LANES, (entry + 1) * LANES)
            row_here = jnp.broadcast_to(source_row[entry : entry + 1, :], (FIELDS, LANES))
            column_here = jnp.broadcast_to(source_column[entry : entry + 1, :], (FIELDS, LANES))
            picked = jnp.zeros((FIELDS, LANES), F32)
            for row in range(ATMOS_ROWS):
                found_here = jnp.take_along_axis(
                    cells_ref[slot, row], column_here, axis=1, mode="promise_in_bounds"
                )
                picked = jnp.where(row_here == float(row), found_here, picked)
            weighted = picked * weight[entry : entry + 1, :]
            high = weighted.astype(BF16).astype(F32)
            low = (weighted - high) * scale
            row_hot = hot(target_row, entry, ROWS)
            for field in range(FIELDS):
                first = field * ROWS
                line = jnp.broadcast_to(high[field : field + 1, :], (16, LANES)).astype(BF16)
                for part in range(4):
                    high_ref[first + part * 16 : first + part * 16 + 16, lanes] = line * row_hot[part]
                line = jnp.broadcast_to(low[field : field + 1, :], (16, LANES)).astype(BF16)
                for part in range(2):
                    both = [line * row_hot[2 * part], line * row_hot[2 * part + 1]]
                    low_ref[first + part * 32 : first + part * 32 + 32, lanes] = jnp.concatenate(
                        both, axis=0
                    ).astype(F8)
            column_hot = hot(target_column, entry, COLUMNS)
            for part in range(COLUMNS // 16):
                high_hot_ref[part * 16 : part * 16 + 16, lanes] = column_hot[part]
            for part in range(COLUMNS // 32):
                low_hot_ref[part * 32 : part * 32 + 32, lanes] = jnp.concatenate(
                    column_hot[2 * part : 2 * part + 2], axis=0
                ).astype(F8)
        over_entries = (((1,), (1,)), ((), ()))
        total_ref[...] += lax.dot_general(
            high_ref[...], high_hot_ref[...], over_entries, preferred_element_type=F32
        ) + unscale * lax.dot_general(
            low_ref[...], low_hot_ref[...], over_entries, preferred_element_type=F32
        )
        return carry

    lax.fori_loop(0, found, chunk_step, 0)


def finish_kernel(
    total_ref,
    helped_ref,
    solved_ref,
    gain_ref,
    result_ref,
    flux_ref,
    forcing_ref,
    to_east_ref,
    to_west_ref,
    sibling_ref,
    other_ref,
):
    def block_step(block, carry):
        rows = pl.ds(pl.multiple_of(block * 8, 8), 8)
        flux = []
        for field in range(FIELDS):
            from_rows = pl.ds(pl.multiple_of(field * ROWS + block * 8, 8), 8)
            value = total_ref[from_rows, :] + helped_ref[from_rows, :]
            flux_ref[field, rows, :] = value
            flux.append(value)
        heat = flux[0] + flux[1] + flux[2] + flux[3] + flux[4]
        salt = flux[7] - flux[5] - flux[6]
        forcing_ref[0, rows, :] = heat
        forcing_ref[1, rows, :] = salt
        for level in range(NZ):
            gain = gain_ref[level, rows, :]
            for tracer, forcing in enumerate((heat, salt)):
                channel = tracer * NZ + level
                result_ref[channel, rows, :] = solved_ref[channel, rows, :] + forcing * gain
        return carry

    lax.fori_loop(0, ROWS // 8, block_step, 0)
    pack_columns(
        lambda channel, row: (result_ref[channel, pl.ds(row, 8), LANES:], LANES - 1),
        range(CHANNELS),
        to_east_ref,
    )
    pack_columns(
        lambda channel, row: (result_ref[channel, pl.ds(row, 8), :LANES], 0),
        range(CHANNELS),
        to_west_ref,
    )
    pack_rows(
        lambda channel: result_ref[channel, ROWS - 1 : ROWS, :],
        lambda channel: result_ref[channel, 0:1, :],
        range(CHANNELS),
        sibling_ref,
        other_ref,
    )


EASTWARD = [(i, (i + 1) % GX) for i in range(GX)]
WESTWARD = [((i + 1) % GX, i) for i in range(GX)]
SIBLINGS = [(y, y ^ 1) for y in range(GY)]
OTHERS = [
    (x * GY + y, x * GY + (y + 1 if y % 2 else y - 1)) for x in range(GX) for y in range(1, GY - 1)
] + [(x * GY + GY - 1, (GX - 1 - x) * GY + GY - 1) for x in range(GX)]


def exchange(to_east, to_west, sibling, other):
    return (
        lax.ppermute(to_east, "gx", EASTWARD),
        lax.ppermute(to_west, "gx", WESTWARD),
        lax.ppermute(sibling, "gy", SIBLINGS),
        lax.ppermute(other, ("gx", "gy"), OTHERS),
    )


def land(operands, slots, own_slot, reset):
    count = own_slot + len(slots)
    (total,) = call(
        functools.partial(land_kernel, slots, own_slot, reset),
        [(FIELDS * ROWS, COLUMNS)],
        operands,
        [
            pltpu.VMEM((3, count * SLOT_ROWS, LANES), F32),
            pltpu.VMEM((count, ATMOS_ROWS, FIELDS, LANES), F32),
            pltpu.VMEM((FIELDS * ROWS, CHUNK), BF16),
            pltpu.VMEM((FIELDS * ROWS, CHUNK), F8),
            pltpu.VMEM((COLUMNS, CHUNK), BF16),
            pltpu.VMEM((COLUMNS, CHUNK), F8),
            pltpu.SMEM((count * CHUNKS + 1,), jnp.int32),
        ],
        moved=100_000,
    )
    return total


def local(
    tracers,
    east_speed,
    north_speed,
    vertical_mix,
    level_count,
    atmosphere_flux,
    intersection_source,
    intersection_target,
    intersection_weight,
):
    q = tracers.reshape(CHANNELS, ROWS, COLUMNS)
    statics = [east_speed, north_speed, level_count, vertical_mix]
    lists = [intersection_source, intersection_target, intersection_weight, atmosphere_flux]
    column_rim, row_rim = (ROWS, LANES), (2 * RIM, LANES)
    both = (2 * RIM + LIST + PAYLOAD, LANES)
    steps = len(ENTRY_STEPS)
    packed = call(
        pack_kernel,
        [column_rim, column_rim, both, both] + [(PAYLOAD, LANES)] * steps,
        [q, *statics[:3], *lists],
        [
            *[pltpu.VMEM(part.shape, part.dtype) for part in (q, *statics[:3], *lists)],
            pltpu.VMEM((ATMOS, LANES), F32),
            pltpu.SemaphoreType.DMA((8,)),
        ],
        in_hbm=True,
    )
    entries = [
        lax.ppermute(part, "gy", list(pairs))
        for part, pairs in zip(packed[4:], ENTRY_STEPS, strict=True)
    ]
    own = land(lists, (), 1, None)
    rims = exchange(*packed[:4])
    first, second, cells = 2 * RIM, 2 * RIM + LIST, 2 * RIM + 2 * LIST
    most = land([rims[2], own], ((0, first, cells, None),), 0, False)
    partial = land(
        [rims[3], *entries, most], ((0, first, cells, None), (1, 0, LIST, True)), 0, False
    )
    helped = lax.ppermute(partial, "gy", list(DENSE))
    total = land(
        [*lists, rims[2], rims[3], *entries, partial],
        ((0, second, cells, None), (1, second, cells, None), (2, 0, LIST, False))
        + tuple((2 + step, 0, LIST, None) for step in range(1, steps)),
        1,
        True,
    )
    rim_scratch = [pltpu.VMEM(row_rim, F32)] * 4
    solved, gain = call(
        functools.partial(step_kernel, True),
        [q.shape, east_speed.shape],
        [q, *rims, *rims, *statics, partial],
        rim_scratch,
        moved=8_000_000,
    )
    result, flux, forcing, *out_rims = call(
        finish_kernel,
        [q.shape, (FIELDS, ROWS, COLUMNS), (TRACERS, ROWS, COLUMNS)]
        + [column_rim, column_rim, row_rim, row_rim],
        [total, helped, solved, gain],
    )
    second_rims = exchange(*out_rims)
    (result,) = call(
        functools.partial(step_kernel, False),
        [q.shape],
        [result, *second_rims, *rims, *statics, forcing],
        [pltpu.VMEM(q.shape, F32), pltpu.SemaphoreType.DMA((ROWS // 8,)), *rim_scratch],
        moved=8_000_000,
        out_hbm=True,
    )
    return result.reshape(tracers.shape), flux


def solution(mesh):
    in_specs = (
        P(None, None, "gy", "gx"),
        P(None, "gy", "gx"),
        P(None, "gy", "gx"),
        P(None, "gy", "gx"),
        P("gy", "gx"),
        P(None, "gy", "gx"),
        P("gy", "gx"),
        P("gy", "gx"),
        P("gy", "gx"),
    )
    out_specs = (P(None, None, "gy", "gx"), P(None, "gy", "gx"))
    return jax.shard_map(local, mesh=mesh, in_specs=in_specs, out_specs=out_specs, check_vma=False)
```

```python
import functools

import jax
import jax.numpy as jnp
from jax import lax
from jax.experimental import pallas as pl
from jax.experimental.pallas import tpu as pltpu
from jax.sharding import PartitionSpec as P

DIFFUSE = 0.05
FIELDS = 8
TRACERS = 2
NZ = 8
ROWS = 64
COLUMNS = 256
LANES = 128
GX = 8
GY = 16
SLOT_ROWS = 32
ATMOS_ROWS = 16
HELPED_BY = {12: GY - 2, 11: GY - 1}
DENSE = ((12, GY - 2), (11, GY - 1))
SENT_AWAY = 13
ENTRY_STEPS = (
    ((7, GY - 2), (8, GY - 1), (10, 12), (9, 11)),
    ((8, GY - 2), (7, GY - 1)),
    ((9, GY - 2), (13, GY - 1)),
)
CHANNELS = TRACERS * NZ
COUNT_AT = 24
RIM = 32
LIST = 3 * SLOT_ROWS
ATMOS = FIELDS * ATMOS_ROWS
PAYLOAD = LIST + ATMOS
CHUNK_ROWS = 16
CHUNK = CHUNK_ROWS * LANES
VMEM_LIMIT = 48 * 1024 * 1024
PACK_LIMIT = 63 * 1024 * 1024
F32 = jnp.float32
BF16 = jnp.bfloat16
F8 = jnp.float8_e4m3fn
LOW_TOP = 65536.0


def call(
    kernel, out_shapes, operands, scratch=(), flops=0, moved=4_000_000, in_hbm=False, out_hbm=False
):
    place = pltpu.HBM if in_hbm else pltpu.VMEM
    out_place = pl.ANY if out_hbm else pltpu.VMEM
    return pl.pallas_call(
        kernel,
        out_shape=[jax.ShapeDtypeStruct(shape, F32) for shape in out_shapes],
        in_specs=[pl.BlockSpec(memory_space=place) for _ in operands],
        out_specs=[pl.BlockSpec(memory_space=out_place) for _ in out_shapes],
        scratch_shapes=list(scratch),
        compiler_params=pltpu.CompilerParams(vmem_limit_bytes=PACK_LIMIT if in_hbm else VMEM_LIMIT),
        cost_estimate=pl.CostEstimate(flops=flops, bytes_accessed=moved, transcendentals=0),
    )(*operands)


def pack_columns(pick, channels, out_ref):
    lane = lax.broadcasted_iota(jnp.int32, (8, LANES), 1)
    for block in range(ROWS // 8):
        tile = jnp.zeros((8, LANES), F32)
        for channel in channels:
            value, at = pick(channel, block * 8)
            shift = (channel - at) % LANES
            moved = pltpu.roll(value, shift, axis=1) if shift else value
            tile = jnp.where(lane == channel, moved, tile)
        out_ref[pl.ds(block * 8, 8), :] = tile


def pack_row(value, channel, out_ref):
    out_ref[pl.ds(channel, 1), :] = value[:, :LANES]
    out_ref[pl.ds(RIM + channel, 1), :] = value[:, LANES:]


def is_even():
    return lax.rem(lax.axis_index("gy"), 2) == 0


def pack_rows(top_of, bottom_of, channels, sibling_ref, other_ref):
    even = is_even()
    zeros = jnp.zeros((2 * RIM, LANES), F32)
    sibling_ref[0 : 2 * RIM, :] = zeros
    other_ref[0 : 2 * RIM, :] = zeros
    for channel in channels:
        top, bottom = top_of(channel), bottom_of(channel)
        pack_row(jnp.where(even, top, bottom), channel, sibling_ref)
        pack_row(jnp.where(even, bottom, top), channel, other_ref)


def chosen(here, table, default):
    for key, value in table.items():
        default = jnp.where(here == key, value, default)
    return default


def among(here, table):
    return functools.reduce(jnp.logical_or, [here == key for key in table])


def list_into(lists, out_ref, at, tile, valid=None):
    rows = pl.ds(pl.multiple_of(tile * SLOT_ROWS, SLOT_ROWS), SLOT_ROWS)
    for kind, ref in enumerate(lists):
        part = ref[rows, :].astype(F32)
        if kind == 2 and valid is not None:
            part = jnp.where(valid, part, 0.0)
        out_ref[at + kind * SLOT_ROWS : at + (kind + 1) * SLOT_ROWS, :] = part


def pack_kernel(*refs):
    steps = len(ENTRY_STEPS)
    froms, refs = refs[:8], refs[8:]
    (to_east_ref, to_west_ref, sibling_ref, other_ref), refs = refs[:4], refs[4:]
    entry_refs, intos, (cells_ref, sems) = refs[:steps], refs[steps:-2], refs[-2:]
    tracers_ref, east_ref, north_ref, count_ref, source_ref, target_ref, weight_ref, atmos_ref = intos
    copies = [
        pltpu.make_async_copy(array, into, sems.at[n])
        for n, (array, into) in enumerate(zip(froms, intos, strict=True))
    ]
    for copy in copies:
        copy.start()
    for copy in copies[4:]:
        copy.wait()
    here = lax.axis_index("gy")
    even = is_even()
    lists = (source_ref, target_ref, weight_ref)
    for field in range(FIELDS):
        for row in range(ATMOS_ROWS):
            to = row * FIELDS + field
            cells_ref[to : to + 1, :] = atmos_ref[field, row : row + 1, :]
    cells = cells_ref[...]
    for pairs, out_ref in zip(ENTRY_STEPS, entry_refs, strict=True):
        wanted = {source: HELPED_BY.get(to, to) for source, to in pairs}
        list_into(lists, out_ref, 0, chosen(here, wanted, here))
        out_ref[LIST:PAYLOAD, :] = cells
    partner = here ^ 1
    list_into(lists, sibling_ref, 2 * RIM, chosen(partner, HELPED_BY, partner))
    list_into(lists, sibling_ref, 2 * RIM + LIST, partner, among(partner, HELPED_BY))
    sibling_ref[2 * RIM + 2 * LIST :, :] = cells
    away = jnp.clip(jnp.where(even, here - 1, here + 1), 0, GY - 1)
    below_top = here != GY - 1
    helped = jnp.logical_and(below_top, among(away, HELPED_BY))
    list_into(lists, other_ref, 2 * RIM, chosen(away, HELPED_BY, away), helped)
    direct = jnp.logical_and(below_top, here != SENT_AWAY)
    list_into(lists, other_ref, 2 * RIM + LIST, away, direct)
    other_ref[2 * RIM + 2 * LIST :, :] = cells

    for copy in copies[:4]:
        copy.wait()

    def east_column(channel, row):
        rows = pl.ds(row, 8)
        if channel < CHANNELS:
            return tracers_ref[channel, rows, LANES:], LANES - 1
        if channel < COUNT_AT:
            return east_ref[channel - CHANNELS, rows, LANES:], LANES - 1
        return count_ref[rows, LANES:].astype(F32), LANES - 1

    def west_column(channel, row):
        rows = pl.ds(row, 8)
        if channel < CHANNELS:
            return tracers_ref[channel, rows, :LANES], 0
        return count_ref[rows, :LANES].astype(F32), 0

    pack_columns(east_column, [*range(CHANNELS + NZ), COUNT_AT], to_east_ref)
    pack_columns(west_column, [*range(CHANNELS), COUNT_AT], to_west_ref)

    def top_of(channel):
        if channel < CHANNELS:
            return tracers_ref[channel, ROWS - 1 : ROWS, :]
        if channel < COUNT_AT:
            return north_ref[channel - CHANNELS, ROWS - 1 : ROWS, :]
        return count_ref[ROWS - 1 : ROWS, :].astype(F32)

    def bottom_of(channel):
        if channel < CHANNELS:
            return tracers_ref[channel, 0:1, :]
        if channel < COUNT_AT:
            return jnp.zeros((1, COLUMNS), F32)
        return count_ref[0:1, :].astype(F32)

    pack_rows(top_of, bottom_of, range(COUNT_AT + 1), sibling_ref, other_ref)


def step_kernel(
    forced,
    q_ref,
    from_west_ref,
    from_east_ref,
    from_sibling_ref,
    from_other_ref,
    static_west_ref,
    static_east_ref,
    static_sibling_ref,
    static_other_ref,
    east_ref,
    north_ref,
    count_ref,
    mix_ref,
    *more_refs,
):
    if forced:
        out_ref, gain_ref = more_refs[-6:-4]
    else:
        forcing_ref, out_hbm, out_ref, sems = more_refs[:4]
    from_south_ref, top_ref, static_south_ref, static_top_ref = more_refs[-4:]
    even = is_even()
    on_top = lax.axis_index("gy") == GY - 1
    lane = lax.broadcasted_iota(jnp.int32, (8, LANES), 1)
    row = lax.broadcasted_iota(jnp.int32, (8, LANES), 0)
    first_lane, last_lane = lane == 0, lane == LANES - 1
    first_row, last_row = row == 0, row == 7

    def set_rims(sibling_rim, other_rim, south, north):
        @pl.when(even)
        def _():
            south[...] = other_rim[0 : 2 * RIM, :]
            north[...] = sibling_rim[0 : 2 * RIM, :]

        @pl.when(jnp.logical_not(even))
        def _():
            south[...] = sibling_rim[0 : 2 * RIM, :]
            north[...] = other_rim[0 : 2 * RIM, :]

        @pl.when(on_top)
        def _():
            flipped = LANES - 1 - lane
            for half in range(2):
                for block in range(RIM // 8):
                    rows = other_rim[pl.ds((1 - half) * RIM + block * 8, 8), :]
                    north[pl.ds(half * RIM + block * 8, 8), :] = jnp.take_along_axis(
                        rows, flipped, axis=1, mode="promise_in_bounds"
                    )

    set_rims(from_sibling_ref, from_other_ref, from_south_ref, top_ref)
    set_rims(static_sibling_ref, static_other_ref, static_south_ref, static_top_ref)

    def block_step(block, carry):
        at = pl.multiple_of(block * 8, 8)
        below = pl.multiple_of(jnp.maximum(block - 1, 0) * 8, 8)
        above = pl.multiple_of(jnp.minimum(block + 1, ROWS // 8 - 1) * 8, 8)
        is_first, is_last = block == 0, block == ROWS // 8 - 1
        rows = pl.ds(at, 8)

        def halves(load):
            return [load(rows, slice(0, LANES)), load(rows, slice(LANES, 2 * LANES))]

        def to_west_of(parts, rim):
            low = jnp.where(last_lane, rim, parts[0])
            high = jnp.where(last_lane, parts[0], parts[1])
            return [pltpu.roll(low, 1, axis=1), pltpu.roll(high, 1, axis=1)]

        def to_east_of(parts, rim):
            low = jnp.where(first_lane, parts[1], parts[0])
            high = jnp.where(first_lane, rim, parts[1])
            return [
                pltpu.roll(low, LANES - 1, axis=1),
                pltpu.roll(high, LANES - 1, axis=1),
            ]

        def to_south_of(load, parts, rim_ref, channel):
            found = []
            for half in range(2):
                lanes = slice(half * LANES, (half + 1) * LANES)
                rim = jnp.broadcast_to(
                    rim_ref[half * RIM + channel : half * RIM + channel + 1, :], (8, LANES)
                )
                near = jnp.where(is_first, rim, load(pl.ds(below, 8), lanes))
                found.append(pltpu.roll(jnp.where(last_row, near, parts[half]), 1, axis=0))
            return found

        def to_north_of(load, parts, rim_ref, channel):
            found = []
            for half in range(2):
                lanes = slice(half * LANES, (half + 1) * LANES)
                rim = jnp.broadcast_to(
                    rim_ref[half * RIM + channel : half * RIM + channel + 1, :], (8, LANES)
                )
                near = jnp.where(is_last, rim, load(pl.ds(above, 8), lanes))
                found.append(pltpu.roll(jnp.where(first_row, near, parts[half]), 7, axis=0))
            return found

        def west_rim(ref, channel):
            return pltpu.roll(ref[rows, :], (LANES - 1 - channel) % LANES, axis=1)

        def east_rim(ref, channel):
            shift = (LANES - channel) % LANES
            return pltpu.roll(ref[rows, :], shift, axis=1) if shift else ref[rows, :]

        def load_count(where, lanes):
            return count_ref[where, lanes].astype(F32)

        count = halves(load_count)
        sides = [
            to_east_of(count, east_rim(static_east_ref, COUNT_AT)),
            to_west_of(count, west_rim(static_west_ref, COUNT_AT)),
            to_north_of(load_count, count, static_top_ref, COUNT_AT),
            to_south_of(load_count, count, static_south_ref, COUNT_AT),
        ]
        shared = [[jnp.minimum(count[half], side[half]) for half in range(2)] for side in sides]
        closed = jnp.logical_and(jnp.logical_and(on_top, is_last), last_row)

        values = [[[None, None] for _ in range(NZ)] for _ in range(TRACERS)]
        for level in range(NZ):
            east = halves(lambda where, lanes: east_ref[level, where, lanes])
            west = to_west_of(east, west_rim(static_west_ref, CHANNELS + level))

            def load_north(where, lanes):
                return north_ref[level, where, lanes]

            north = halves(load_north)
            south = to_south_of(load_north, north, static_south_ref, CHANNELS + level)
            coefs = []
            for half in range(2):
                limit = float(level)
                up = jnp.where(closed, 0.0, north[half])
                open_e, open_w, open_n, open_s = [side[half] > limit for side in shared]

                def into(opened, speed):
                    return jnp.where(opened, DIFFUSE - jnp.minimum(speed, 0.0), 0.0)

                def away(opened, speed):
                    return jnp.where(opened, DIFFUSE + jnp.maximum(speed, 0.0), 0.0)

                from_e, lost_e = into(open_e, east[half]), away(open_e, east[half])
                from_w, lost_w = away(open_w, west[half]), into(open_w, west[half])
                from_n, lost_n = into(open_n, up), away(open_n, up)
                from_s, lost_s = away(open_s, south[half]), into(open_s, south[half])
                kept = 1.0 - ((lost_e + lost_w) + (lost_n + lost_s))
                coefs.append((kept, from_e, from_w, from_n, from_s))
            for tracer in range(TRACERS):
                channel = tracer * NZ + level

                def load_q(where, lanes):
                    return q_ref[channel, where, lanes]

                q = halves(load_q)
                q_e = to_east_of(q, east_rim(from_east_ref, channel))
                q_w = to_west_of(q, west_rim(from_west_ref, channel))
                q_n = to_north_of(load_q, q, top_ref, channel)
                q_s = to_south_of(load_q, q, from_south_ref, channel)
                for half in range(2):
                    kept, from_e, from_w, from_n, from_s = coefs[half]
                    values[tracer][level][half] = (
                        kept * q[half]
                        + (from_e * q_e[half] + from_w * q_w[half])
                        + (from_n * q_n[half] + from_s * q_s[half])
                    )
        for half in range(2):
            lanes = slice(half * LANES, (half + 1) * LANES)
            sides_here = [[values[t][k][half] for k in range(NZ)] for t in range(TRACERS)]
            surface = count[half] > 0.0
            if forced:
                sides_here.append([jnp.where(surface, 1.0, 0.0)] + [None] * (NZ - 1))
            else:
                for tracer in range(TRACERS):
                    forcing = jnp.where(surface, forcing_ref[tracer, rows, lanes], 0.0)
                    sides_here[tracer][0] = sides_here[tracer][0] + forcing
            ratios = []
            partials = [[] for _ in sides_here]
            for level in range(NZ):
                thickness = 1.0 + level / NZ
                upper = lower = None
                if level >= 1:
                    mix = mix_ref[level - 1, rows, lanes]
                    upper = jnp.where(count[half] > float(level), mix * (1.0 / thickness), 0.0)
                if level <= NZ - 2:
                    mix = mix_ref[level, rows, lanes]
                    lower = jnp.where(
                        count[half] > float(level + 1), mix * (1.0 / thickness), 0.0
                    )
                if upper is None:
                    pivot = 1.0 + lower
                elif lower is None:
                    pivot = 1.0 + upper - upper * ratios[-1]
                else:
                    pivot = 1.0 + upper + lower - upper * ratios[-1]
                inverse = 1.0 / pivot
                if lower is not None:
                    ratios.append(lower * inverse)
                for side, partial in zip(sides_here, partials, strict=True):
                    right = side[level]
                    if level >= 1:
                        carried = upper * partial[-1]
                        right = carried if right is None else right + carried
                    partial.append(right * inverse)
            for index, partial in enumerate(partials):
                solved = partial[-1]
                for level in range(NZ - 1, -1, -1):
                    if level < NZ - 1:
                        solved = partial[level] + ratios[level] * solved
                    if index < TRACERS:
                        out_ref[index * NZ + level, rows, lanes] = solved
                    else:
                        gain_ref[level, rows, lanes] = solved
        if not forced:
            block_copy(block).start()
        return carry

    def block_copy(block):
        rows = pl.ds(pl.multiple_of(block * 8, 8), 8)
        return pltpu.make_async_copy(out_ref.at[:, rows, :], out_hbm.at[:, rows, :], sems.at[block])

    lax.fori_loop(0, ROWS // 8, block_step, 0)
    if not forced:
        for block in range(ROWS // 8):
            block_copy(block).wait()


def land_kernel(slots, own_slot, reset, *refs):
    operand_refs, refs = refs[:-9], refs[-9:]
    if own_slot:
        own, operand_refs = operand_refs[:4], operand_refs[4:]
    here = lax.axis_index("gy")
    helps = among(here, HELPED_BY)
    if reset is not None:
        start_ref = operand_refs[-1]
    total_ref, lists_ref, columns_ref, cells_ref = refs[:4]
    high_ref, low_ref, high_hot_ref, low_hot_ref, weights_ref = refs[4:]
    largest = jnp.zeros((8, LANES), F32)
    row_number = lax.broadcasted_iota(jnp.int32, (SLOT_ROWS, LANES), 0).astype(F32) + 1.0
    ends = []

    def unpack(slot):
        source, target, weight = weights_ref[0], weights_ref[1], weights_ref[2]
        rows = pl.ds(slot * SLOT_ROWS, SLOT_ROWS)
        source_row = jnp.floor(source * (1.0 / LANES))
        target_row = jnp.floor(target * (1.0 / COLUMNS))
        columns_ref[rows, :] = (source - source_row * LANES).astype(jnp.int32)
        lists_ref[0, rows, :] = source_row
        lists_ref[1, rows, :] = target_row
        lists_ref[2, rows, :] = target - target_row * COLUMNS
        lists_ref[3, rows, :] = weight
        return jnp.max(jnp.where(weight != 0.0, row_number, 0.0)).astype(jnp.int32)

    if own_slot:
        tile = here if reset else chosen(here, HELPED_BY, here)
        rows = pl.ds(pl.multiple_of(tile * SLOT_ROWS, SLOT_ROWS), SLOT_ROWS)
        for kind in range(3):
            part = own[kind][rows, :].astype(F32)
            if kind == 2 and reset:
                part = jnp.where(helps, part, 0.0)
            weights_ref[kind] = part
        ends.append(unpack(0))
        for field in range(FIELDS):
            largest = jnp.maximum(largest, jnp.abs(own[3][field, 0:8, :]))
            largest = jnp.maximum(largest, jnp.abs(own[3][field, 8:16, :]))
            for row in range(ATMOS_ROWS):
                cells_ref[0, row, field : field + 1, :] = own[3][field, row : row + 1, :]
    count = own_slot + len(slots)
    for slot, (operand, list_at, cells_at, only) in enumerate(slots, own_slot):
        ref = operand_refs[operand]
        for kind in range(3):
            rows = pl.ds(list_at + kind * SLOT_ROWS, SLOT_ROWS)
            part = ref[rows, :]
            if kind == 2 and only is not None:
                part = jnp.where(helps == only, part, 0.0)
            weights_ref[kind] = part
        ends.append(unpack(slot))
        for row in range(ATMOS_ROWS):
            cells = ref[pl.ds(cells_at + row * FIELDS, FIELDS), :]
            cells_ref[slot, row] = cells
            largest = jnp.maximum(largest, jnp.abs(cells))
    scale = LOW_TOP / jnp.maximum(jnp.max(largest), 1e-30)
    unscale = 1.0 / scale

    spare = count * SLOT_ROWS
    lists_ref[:, spare : spare + 8, :] = jnp.zeros((4, 8, LANES), F32)
    columns_ref[spare : spare + 8, :] = jnp.zeros((8, LANES), jnp.int32)
    firsts = [jnp.int32(0)]
    for end in ends:
        firsts.append(firsts[-1] + end)
    live = firsts.pop()

    def row_of(place):
        shift = jnp.int32(0)
        for slot in range(1, count):
            shift = jnp.where(place >= firsts[slot], slot * SLOT_ROWS - firsts[slot], shift)
        return jnp.where(place < live, place + shift, spare)

    if reset is None:
        total_ref[...] = jnp.zeros_like(total_ref)
    elif reset:

        @pl.when(helps)
        def _():
            total_ref[...] = jnp.zeros_like(total_ref)

        @pl.when(jnp.logical_not(helps))
        def _():
            total_ref[...] = start_ref[...]
    else:
        total_ref[...] = start_ref[...]
    ones, zeros = jnp.ones((), BF16), jnp.zeros((), BF16)
    iota = lax.broadcasted_iota(jnp.int32, (COLUMNS, LANES), 0).astype(F32).astype(BF16)

    def hot(values, height):
        line = jnp.broadcast_to(values, (16, LANES)).astype(BF16)
        return [jnp.where(line == iota[at : at + 16], ones, zeros) for at in range(0, height, 16)]

    def chunk(place, entries):
        for entry in range(entries):
            at = row_of(place + entry)
            one = pl.ds(at, 1)
            slot = jnp.minimum(lax.div(at, SLOT_ROWS), count - 1)
            lanes = slice(entry * LANES, (entry + 1) * LANES)
            row_here = jnp.broadcast_to(lists_ref[0, one, :], (FIELDS, LANES))
            column_here = jnp.broadcast_to(columns_ref[one, :], (FIELDS, LANES))
            picked = jnp.zeros((FIELDS, LANES), F32)
            for row in range(ATMOS_ROWS):
                found_here = jnp.take_along_axis(
                    cells_ref[slot, row], column_here, axis=1, mode="promise_in_bounds"
                )
                picked = jnp.where(row_here == float(row), found_here, picked)
            weighted = picked * lists_ref[3, one, :]
            high = weighted.astype(BF16).astype(F32)
            low = (weighted - high) * scale
            row_hot = hot(lists_ref[1, one, :], ROWS)
            for field in range(FIELDS):
                first = field * ROWS
                line = jnp.broadcast_to(high[field : field + 1, :], (16, LANES)).astype(BF16)
                for part in range(4):
                    high_ref[first + part * 16 : first + part * 16 + 16, lanes] = line * row_hot[part]
                line = jnp.broadcast_to(low[field : field + 1, :], (16, LANES)).astype(BF16)
                for part in range(2):
                    both = [line * row_hot[2 * part], line * row_hot[2 * part + 1]]
                    low_ref[first + part * 32 : first + part * 32 + 32, lanes] = jnp.concatenate(
                        both, axis=0
                    ).astype(F8)
            column_hot = hot(lists_ref[2, one, :], COLUMNS)
            for part in range(COLUMNS // 16):
                high_hot_ref[part * 16 : part * 16 + 16, lanes] = column_hot[part]
            for part in range(COLUMNS // 32):
                low_hot_ref[part * 32 : part * 32 + 32, lanes] = jnp.concatenate(
                    column_hot[2 * part : 2 * part + 2], axis=0
                ).astype(F8)
        over_entries = (((1,), (1,)), ((), ()))
        used = slice(0, entries * LANES)
        total_ref[...] += lax.dot_general(
            high_ref[:, used], high_hot_ref[:, used], over_entries, preferred_element_type=F32
        ) + unscale * lax.dot_general(
            low_ref[:, used], low_hot_ref[:, used], over_entries, preferred_element_type=F32
        )

    def chunk_step(at, carry):
        chunk(at * CHUNK_ROWS, CHUNK_ROWS)
        return carry

    half = CHUNK_ROWS // 2
    wholes = lax.div(live + (half - 1), CHUNK_ROWS)
    lax.fori_loop(0, wholes, chunk_step, 0)

    @pl.when(live > wholes * CHUNK_ROWS)
    def _():
        chunk(wholes * CHUNK_ROWS, half)


def finish_kernel(
    total_ref,
    helped_ref,
    solved_ref,
    gain_ref,
    result_ref,
    flux_ref,
    forcing_ref,
    to_east_ref,
    to_west_ref,
    sibling_ref,
    other_ref,
):
    def block_step(block, carry):
        rows = pl.ds(pl.multiple_of(block * 8, 8), 8)
        flux = []
        for field in range(FIELDS):
            from_rows = pl.ds(pl.multiple_of(field * ROWS + block * 8, 8), 8)
            value = total_ref[from_rows, :] + helped_ref[from_rows, :]
            flux_ref[field, rows, :] = value
            flux.append(value)
        heat = flux[0] + flux[1] + flux[2] + flux[3] + flux[4]
        salt = flux[7] - flux[5] - flux[6]
        forcing_ref[0, rows, :] = heat
        forcing_ref[1, rows, :] = salt
        for level in range(NZ):
            gain = gain_ref[level, rows, :]
            for tracer, forcing in enumerate((heat, salt)):
                channel = tracer * NZ + level
                result_ref[channel, rows, :] = solved_ref[channel, rows, :] + forcing * gain
        return carry

    lax.fori_loop(0, ROWS // 8, block_step, 0)
    pack_columns(
        lambda channel, row: (result_ref[channel, pl.ds(row, 8), LANES:], LANES - 1),
        range(CHANNELS),
        to_east_ref,
    )
    pack_columns(
        lambda channel, row: (result_ref[channel, pl.ds(row, 8), :LANES], 0),
        range(CHANNELS),
        to_west_ref,
    )
    pack_rows(
        lambda channel: result_ref[channel, ROWS - 1 : ROWS, :],
        lambda channel: result_ref[channel, 0:1, :],
        range(CHANNELS),
        sibling_ref,
        other_ref,
    )


EASTWARD = [(i, (i + 1) % GX) for i in range(GX)]
WESTWARD = [((i + 1) % GX, i) for i in range(GX)]
SIBLINGS = [(y, y ^ 1) for y in range(GY)]
OTHERS = [
    (x * GY + y, x * GY + (y + 1 if y % 2 else y - 1)) for x in range(GX) for y in range(1, GY - 1)
] + [(x * GY + GY - 1, (GX - 1 - x) * GY + GY - 1) for x in range(GX)]


def exchange(to_east, to_west, sibling, other):
    return (
        lax.ppermute(to_east, "gx", EASTWARD),
        lax.ppermute(to_west, "gx", WESTWARD),
        lax.ppermute(sibling, "gy", SIBLINGS),
        lax.ppermute(other, ("gx", "gy"), OTHERS),
    )


def land(operands, slots, own_slot, reset):
    count = own_slot + len(slots)
    (total,) = call(
        functools.partial(land_kernel, slots, own_slot, reset),
        [(FIELDS * ROWS, COLUMNS)],
        operands,
        [
            pltpu.VMEM((4, count * SLOT_ROWS + 8, LANES), F32),
            pltpu.VMEM((count * SLOT_ROWS + 8, LANES), jnp.int32),
            pltpu.VMEM((count, ATMOS_ROWS, FIELDS, LANES), F32),
            pltpu.VMEM((FIELDS * ROWS, CHUNK), BF16),
            pltpu.VMEM((FIELDS * ROWS, CHUNK), F8),
            pltpu.VMEM((COLUMNS, CHUNK), BF16),
            pltpu.VMEM((COLUMNS, CHUNK), F8),
            pltpu.VMEM((3, SLOT_ROWS, LANES), F32),
        ],
        moved=100_000,
    )
    return total


def local(
    tracers,
    east_speed,
    north_speed,
    vertical_mix,
    level_count,
    atmosphere_flux,
    intersection_source,
    intersection_target,
    intersection_weight,
):
    q = tracers.reshape(CHANNELS, ROWS, COLUMNS)
    statics = [east_speed, north_speed, level_count, vertical_mix]
    lists = [intersection_source, intersection_target, intersection_weight, atmosphere_flux]
    column_rim, row_rim = (ROWS, LANES), (2 * RIM, LANES)
    both = (2 * RIM + LIST + PAYLOAD, LANES)
    steps = len(ENTRY_STEPS)
    packed = call(
        pack_kernel,
        [column_rim, column_rim, both, both] + [(PAYLOAD, LANES)] * steps,
        [q, *statics[:3], *lists],
        [
            *[pltpu.VMEM(part.shape, part.dtype) for part in (q, *statics[:3], *lists)],
            pltpu.VMEM((ATMOS, LANES), F32),
            pltpu.SemaphoreType.DMA((8,)),
        ],
        in_hbm=True,
    )
    entries = [
        lax.ppermute(part, "gy", list(pairs))
        for part, pairs in zip(packed[4:], ENTRY_STEPS, strict=True)
    ]
    rims = exchange(*packed[:4])
    first, second, cells = 2 * RIM, 2 * RIM + LIST, 2 * RIM + 2 * LIST
    most = land([*lists, rims[2]], ((0, first, cells, None),), 1, None)
    partial = land(
        [rims[3], *entries, most], ((0, first, cells, None), (1, 0, LIST, True)), 0, False
    )
    helped = lax.ppermute(partial, "gy", list(DENSE))
    total = land(
        [*lists, rims[2], rims[3], *entries, partial],
        ((0, second, cells, None), (1, second, cells, None), (2, 0, LIST, False))
        + tuple((2 + step, 0, LIST, None) for step in range(1, steps)),
        1,
        True,
    )
    rim_scratch = [pltpu.VMEM(row_rim, F32)] * 4
    solved, gain = call(
        functools.partial(step_kernel, True),
        [q.shape, east_speed.shape],
        [q, *rims, *rims, *statics, partial],
        rim_scratch,
        moved=8_000_000,
    )
    result, flux, forcing, *out_rims = call(
        finish_kernel,
        [q.shape, (FIELDS, ROWS, COLUMNS), (TRACERS, ROWS, COLUMNS)]
        + [column_rim, column_rim, row_rim, row_rim],
        [total, helped, solved, gain],
    )
    second_rims = exchange(*out_rims)
    (result,) = call(
        functools.partial(step_kernel, False),
        [q.shape],
        [result, *second_rims, *rims, *statics, forcing],
        [pltpu.VMEM(q.shape, F32), pltpu.SemaphoreType.DMA((ROWS // 8,)), *rim_scratch],
        moved=8_000_000,
        out_hbm=True,
    )
    return result.reshape(tracers.shape), flux


def solution(mesh):
    in_specs = (
        P(None, None, "gy", "gx"),
        P(None, "gy", "gx"),
        P(None, "gy", "gx"),
        P(None, "gy", "gx"),
        P("gy", "gx"),
        P(None, "gy", "gx"),
        P("gy", "gx"),
        P("gy", "gx"),
        P("gy", "gx"),
    )
    out_specs = (P(None, None, "gy", "gx"), P(None, "gy", "gx"))
    return jax.shard_map(local, mesh=mesh, in_specs=in_specs, out_specs=out_specs, check_vma=False)
```

```python
import functools

import jax
import jax.numpy as jnp
from jax import lax
from jax.experimental import pallas as pl
from jax.experimental.pallas import tpu as pltpu
from jax.sharding import PartitionSpec as P

DIFFUSE = 0.05
FIELDS = 8
TRACERS = 2
NZ = 8
ROWS = 64
COLUMNS = 256
LANES = 128
GX = 8
GY = 16
SLOT_ROWS = 32
ATMOS_ROWS = 16
HELPED_BY = {12: GY - 2, 11: GY - 1}
DENSE = ((12, GY - 2), (11, GY - 1))
SENT_AWAY = 13
ENTRY_STEPS = (
    ((7, GY - 2), (8, GY - 1), (10, 12), (9, 11)),
    ((8, GY - 2), (7, GY - 1)),
    ((9, GY - 2), (13, GY - 1)),
)
CHANNELS = TRACERS * NZ
COUNT_AT = 24
RIM = 32
LIST = 3 * SLOT_ROWS
ATMOS = FIELDS * ATMOS_ROWS
PAYLOAD = LIST + ATMOS
CHUNK_ROWS = 16
CHUNK = CHUNK_ROWS * LANES
VMEM_LIMIT = 48 * 1024 * 1024
PACK_LIMIT = 63 * 1024 * 1024
F32 = jnp.float32
BF16 = jnp.bfloat16
F8 = jnp.float8_e4m3fn
LOW_TOP = 65536.0


def call(
    kernel, out_shapes, operands, scratch=(), flops=0, moved=4_000_000, in_hbm=False, out_hbm=False
):
    place = pltpu.HBM if in_hbm else pltpu.VMEM
    out_place = pl.ANY if out_hbm else pltpu.VMEM
    return pl.pallas_call(
        kernel,
        out_shape=[jax.ShapeDtypeStruct(shape, F32) for shape in out_shapes],
        in_specs=[pl.BlockSpec(memory_space=place) for _ in operands],
        out_specs=[pl.BlockSpec(memory_space=out_place) for _ in out_shapes],
        scratch_shapes=list(scratch),
        compiler_params=pltpu.CompilerParams(vmem_limit_bytes=PACK_LIMIT if in_hbm else VMEM_LIMIT),
        cost_estimate=pl.CostEstimate(flops=flops, bytes_accessed=moved, transcendentals=0),
    )(*operands)


def pack_columns(pick, channels, out_ref):
    lane = lax.broadcasted_iota(jnp.int32, (8, LANES), 1)
    for block in range(ROWS // 8):
        tile = jnp.zeros((8, LANES), F32)
        for channel in channels:
            value, at = pick(channel, block * 8)
            shift = (channel - at) % LANES
            moved = pltpu.roll(value, shift, axis=1) if shift else value
            tile = jnp.where(lane == channel, moved, tile)
        out_ref[pl.ds(block * 8, 8), :] = tile


def pack_row(value, channel, out_ref):
    out_ref[pl.ds(channel, 1), :] = value[:, :LANES]
    out_ref[pl.ds(RIM + channel, 1), :] = value[:, LANES:]


def is_even():
    return lax.rem(lax.axis_index("gy"), 2) == 0


def pack_rows(top_of, bottom_of, channels, sibling_ref, other_ref):
    even = is_even()
    zeros = jnp.zeros((2 * RIM, LANES), F32)
    sibling_ref[0 : 2 * RIM, :] = zeros
    other_ref[0 : 2 * RIM, :] = zeros
    for channel in channels:
        top, bottom = top_of(channel), bottom_of(channel)
        pack_row(jnp.where(even, top, bottom), channel, sibling_ref)
        pack_row(jnp.where(even, bottom, top), channel, other_ref)


def chosen(here, table, default):
    for key, value in table.items():
        default = jnp.where(here == key, value, default)
    return default


def among(here, table):
    return functools.reduce(jnp.logical_or, [here == key for key in table])


def list_into(lists, out_ref, at, tile, valid=None):
    rows = pl.ds(pl.multiple_of(tile * SLOT_ROWS, SLOT_ROWS), SLOT_ROWS)
    for kind, ref in enumerate(lists):
        part = ref[rows, :].astype(F32)
        if kind == 2 and valid is not None:
            part = jnp.where(valid, part, 0.0)
        out_ref[at + kind * SLOT_ROWS : at + (kind + 1) * SLOT_ROWS, :] = part


def pack_kernel(*refs):
    steps = len(ENTRY_STEPS)
    froms, refs = refs[:8], refs[8:]
    (to_east_ref, to_west_ref, sibling_ref, other_ref, fold_ref), refs = refs[:5], refs[5:]
    entry_refs, intos, (cells_ref, sems) = refs[:steps], refs[steps:-2], refs[-2:]
    tracers_ref, east_ref, north_ref, count_ref, source_ref, target_ref, weight_ref, atmos_ref = intos
    copies = [
        pltpu.make_async_copy(array, into, sems.at[n])
        for n, (array, into) in enumerate(zip(froms, intos, strict=True))
    ]
    for copy in copies:
        copy.start()
    for copy in copies[4:]:
        copy.wait()
    here = lax.axis_index("gy")
    even = is_even()
    lists = (source_ref, target_ref, weight_ref)
    for field in range(FIELDS):
        for row in range(ATMOS_ROWS):
            to = row * FIELDS + field
            cells_ref[to : to + 1, :] = atmos_ref[field, row : row + 1, :]
    cells = cells_ref[...]
    for pairs, out_ref in zip(ENTRY_STEPS, entry_refs, strict=True):
        wanted = {source: HELPED_BY.get(to, to) for source, to in pairs}
        list_into(lists, out_ref, 0, chosen(here, wanted, here))
        out_ref[LIST:PAYLOAD, :] = cells
    partner = here ^ 1
    list_into(lists, sibling_ref, 2 * RIM, chosen(partner, HELPED_BY, partner))
    list_into(lists, sibling_ref, 2 * RIM + LIST, partner, among(partner, HELPED_BY))
    sibling_ref[2 * RIM + 2 * LIST :, :] = cells
    away = jnp.clip(jnp.where(even, here - 1, here + 1), 0, GY - 1)
    below_top = here != GY - 1
    helped = jnp.logical_and(below_top, among(away, HELPED_BY))
    list_into(lists, other_ref, 2 * RIM, chosen(away, HELPED_BY, away), helped)
    direct = jnp.logical_and(below_top, here != SENT_AWAY)
    list_into(lists, other_ref, 2 * RIM + LIST, away, direct)
    other_ref[2 * RIM + 2 * LIST :, :] = cells

    for copy in copies[:4]:
        copy.wait()

    def east_column(channel, row):
        rows = pl.ds(row, 8)
        if channel < CHANNELS:
            return tracers_ref[channel, rows, LANES:], LANES - 1
        if channel < COUNT_AT:
            return east_ref[channel - CHANNELS, rows, LANES:], LANES - 1
        return count_ref[rows, LANES:].astype(F32), LANES - 1

    def west_column(channel, row):
        rows = pl.ds(row, 8)
        if channel < CHANNELS:
            return tracers_ref[channel, rows, :LANES], 0
        return count_ref[rows, :LANES].astype(F32), 0

    pack_columns(east_column, [*range(CHANNELS + NZ), COUNT_AT], to_east_ref)
    pack_columns(west_column, [*range(CHANNELS), COUNT_AT], to_west_ref)

    def top_of(channel):
        if channel < CHANNELS:
            return tracers_ref[channel, ROWS - 1 : ROWS, :]
        if channel < COUNT_AT:
            return north_ref[channel - CHANNELS, ROWS - 1 : ROWS, :]
        return count_ref[ROWS - 1 : ROWS, :].astype(F32)

    def bottom_of(channel):
        if channel < CHANNELS:
            return tracers_ref[channel, 0:1, :]
        if channel < COUNT_AT:
            return jnp.zeros((1, COLUMNS), F32)
        return count_ref[0:1, :].astype(F32)

    pack_rows(top_of, bottom_of, range(COUNT_AT + 1), sibling_ref, other_ref)
    fold_ref[...] = other_ref[0 : 2 * RIM, :]


def step_kernel(
    forced,
    q_ref,
    from_west_ref,
    from_east_ref,
    from_sibling_ref,
    from_other_ref,
    from_fold_ref,
    static_west_ref,
    static_east_ref,
    static_sibling_ref,
    static_other_ref,
    static_fold_ref,
    east_ref,
    north_ref,
    count_ref,
    mix_ref,
    *more_refs,
):
    if forced:
        out_ref, gain_ref = more_refs[-6:-4]
    else:
        forcing_ref, out_hbm, out_ref, sems = more_refs[:4]
    from_south_ref, top_ref, static_south_ref, static_top_ref = more_refs[-4:]
    even = is_even()
    on_top = lax.axis_index("gy") == GY - 1
    lane = lax.broadcasted_iota(jnp.int32, (8, LANES), 1)
    row = lax.broadcasted_iota(jnp.int32, (8, LANES), 0)
    first_lane, last_lane = lane == 0, lane == LANES - 1
    first_row, last_row = row == 0, row == 7

    def set_rims(sibling_rim, other_rim, fold_rim, south, north):
        @pl.when(even)
        def _():
            south[...] = other_rim[0 : 2 * RIM, :]
            north[...] = sibling_rim[0 : 2 * RIM, :]

        @pl.when(jnp.logical_not(even))
        def _():
            south[...] = sibling_rim[0 : 2 * RIM, :]
            north[...] = other_rim[0 : 2 * RIM, :]

        @pl.when(on_top)
        def _():
            flipped = LANES - 1 - lane
            for half in range(2):
                for block in range(RIM // 8):
                    rows = fold_rim[pl.ds((1 - half) * RIM + block * 8, 8), :]
                    north[pl.ds(half * RIM + block * 8, 8), :] = jnp.take_along_axis(
                        rows, flipped, axis=1, mode="promise_in_bounds"
                    )

    set_rims(from_sibling_ref, from_other_ref, from_fold_ref, from_south_ref, top_ref)
    set_rims(
        static_sibling_ref, static_other_ref, static_fold_ref, static_south_ref, static_top_ref
    )

    def block_step(block, carry):
        at = pl.multiple_of(block * 8, 8)
        below = pl.multiple_of(jnp.maximum(block - 1, 0) * 8, 8)
        above = pl.multiple_of(jnp.minimum(block + 1, ROWS // 8 - 1) * 8, 8)
        is_first, is_last = block == 0, block == ROWS // 8 - 1
        rows = pl.ds(at, 8)

        def halves(load):
            return [load(rows, slice(0, LANES)), load(rows, slice(LANES, 2 * LANES))]

        def to_west_of(parts, rim):
            low = jnp.where(last_lane, rim, parts[0])
            high = jnp.where(last_lane, parts[0], parts[1])
            return [pltpu.roll(low, 1, axis=1), pltpu.roll(high, 1, axis=1)]

        def to_east_of(parts, rim):
            low = jnp.where(first_lane, parts[1], parts[0])
            high = jnp.where(first_lane, rim, parts[1])
            return [
                pltpu.roll(low, LANES - 1, axis=1),
                pltpu.roll(high, LANES - 1, axis=1),
            ]

        def to_south_of(load, parts, rim_ref, channel):
            found = []
            for half in range(2):
                lanes = slice(half * LANES, (half + 1) * LANES)
                rim = jnp.broadcast_to(
                    rim_ref[half * RIM + channel : half * RIM + channel + 1, :], (8, LANES)
                )
                near = jnp.where(is_first, rim, load(pl.ds(below, 8), lanes))
                found.append(pltpu.roll(jnp.where(last_row, near, parts[half]), 1, axis=0))
            return found

        def to_north_of(load, parts, rim_ref, channel):
            found = []
            for half in range(2):
                lanes = slice(half * LANES, (half + 1) * LANES)
                rim = jnp.broadcast_to(
                    rim_ref[half * RIM + channel : half * RIM + channel + 1, :], (8, LANES)
                )
                near = jnp.where(is_last, rim, load(pl.ds(above, 8), lanes))
                found.append(pltpu.roll(jnp.where(first_row, near, parts[half]), 7, axis=0))
            return found

        def west_rim(ref, channel):
            return pltpu.roll(ref[rows, :], (LANES - 1 - channel) % LANES, axis=1)

        def east_rim(ref, channel):
            shift = (LANES - channel) % LANES
            return pltpu.roll(ref[rows, :], shift, axis=1) if shift else ref[rows, :]

        def load_count(where, lanes):
            return count_ref[where, lanes].astype(F32)

        count = halves(load_count)
        sides = [
            to_east_of(count, east_rim(static_east_ref, COUNT_AT)),
            to_west_of(count, west_rim(static_west_ref, COUNT_AT)),
            to_north_of(load_count, count, static_top_ref, COUNT_AT),
            to_south_of(load_count, count, static_south_ref, COUNT_AT),
        ]
        shared = [[jnp.minimum(count[half], side[half]) for half in range(2)] for side in sides]
        closed = jnp.logical_and(jnp.logical_and(on_top, is_last), last_row)

        values = [[[None, None] for _ in range(NZ)] for _ in range(TRACERS)]
        for level in range(NZ):
            east = halves(lambda where, lanes: east_ref[level, where, lanes])
            west = to_west_of(east, west_rim(static_west_ref, CHANNELS + level))

            def load_north(where, lanes):
                return north_ref[level, where, lanes]

            north = halves(load_north)
            south = to_south_of(load_north, north, static_south_ref, CHANNELS + level)
            coefs = []
            for half in range(2):
                limit = float(level)
                up = jnp.where(closed, 0.0, north[half])
                open_e, open_w, open_n, open_s = [side[half] > limit for side in shared]

                def into(opened, speed):
                    return jnp.where(opened, DIFFUSE - jnp.minimum(speed, 0.0), 0.0)

                def away(opened, speed):
                    return jnp.where(opened, DIFFUSE + jnp.maximum(speed, 0.0), 0.0)

                from_e, lost_e = into(open_e, east[half]), away(open_e, east[half])
                from_w, lost_w = away(open_w, west[half]), into(open_w, west[half])
                from_n, lost_n = into(open_n, up), away(open_n, up)
                from_s, lost_s = away(open_s, south[half]), into(open_s, south[half])
                kept = 1.0 - ((lost_e + lost_w) + (lost_n + lost_s))
                coefs.append((kept, from_e, from_w, from_n, from_s))
            for tracer in range(TRACERS):
                channel = tracer * NZ + level

                def load_q(where, lanes):
                    return q_ref[channel, where, lanes]

                q = halves(load_q)
                q_e = to_east_of(q, east_rim(from_east_ref, channel))
                q_w = to_west_of(q, west_rim(from_west_ref, channel))
                q_n = to_north_of(load_q, q, top_ref, channel)
                q_s = to_south_of(load_q, q, from_south_ref, channel)
                for half in range(2):
                    kept, from_e, from_w, from_n, from_s = coefs[half]
                    values[tracer][level][half] = (
                        kept * q[half]
                        + (from_e * q_e[half] + from_w * q_w[half])
                        + (from_n * q_n[half] + from_s * q_s[half])
                    )
        for half in range(2):
            lanes = slice(half * LANES, (half + 1) * LANES)
            sides_here = [[values[t][k][half] for k in range(NZ)] for t in range(TRACERS)]
            surface = count[half] > 0.0
            if forced:
                sides_here.append([jnp.where(surface, 1.0, 0.0)] + [None] * (NZ - 1))
            else:
                for tracer in range(TRACERS):
                    forcing = jnp.where(surface, forcing_ref[tracer, rows, lanes], 0.0)
                    sides_here[tracer][0] = sides_here[tracer][0] + forcing
            ratios = []
            partials = [[] for _ in sides_here]
            for level in range(NZ):
                thickness = 1.0 + level / NZ
                upper = lower = None
                if level >= 1:
                    mix = mix_ref[level - 1, rows, lanes]
                    upper = jnp.where(count[half] > float(level), mix * (1.0 / thickness), 0.0)
                if level <= NZ - 2:
                    mix = mix_ref[level, rows, lanes]
                    lower = jnp.where(
                        count[half] > float(level + 1), mix * (1.0 / thickness), 0.0
                    )
                if upper is None:
                    pivot = 1.0 + lower
                elif lower is None:
                    pivot = 1.0 + upper - upper * ratios[-1]
                else:
                    pivot = 1.0 + upper + lower - upper * ratios[-1]
                inverse = 1.0 / pivot
                if lower is not None:
                    ratios.append(lower * inverse)
                for side, partial in zip(sides_here, partials, strict=True):
                    right = side[level]
                    if level >= 1:
                        carried = upper * partial[-1]
                        right = carried if right is None else right + carried
                    partial.append(right * inverse)
            for index, partial in enumerate(partials):
                solved = partial[-1]
                for level in range(NZ - 1, -1, -1):
                    if level < NZ - 1:
                        solved = partial[level] + ratios[level] * solved
                    if index < TRACERS:
                        out_ref[index * NZ + level, rows, lanes] = solved
                    else:
                        gain_ref[level, rows, lanes] = solved
        if not forced:
            block_copy(block).start()
        return carry

    def block_copy(block):
        rows = pl.ds(pl.multiple_of(block * 8, 8), 8)
        return pltpu.make_async_copy(out_ref.at[:, rows, :], out_hbm.at[:, rows, :], sems.at[block])

    lax.fori_loop(0, ROWS // 8, block_step, 0)
    if not forced:
        for block in range(ROWS // 8):
            block_copy(block).wait()


def land_kernel(slots, own_slot, reset, *refs):
    operand_refs, refs = refs[:-9], refs[-9:]
    if own_slot:
        own, operand_refs = operand_refs[:4], operand_refs[4:]
    here = lax.axis_index("gy")
    helps = among(here, HELPED_BY)
    if reset is not None:
        start_ref = operand_refs[-1]
    total_ref, lists_ref, columns_ref, cells_ref = refs[:4]
    high_ref, low_ref, high_hot_ref, low_hot_ref, weights_ref = refs[4:]
    largest = jnp.zeros((8, LANES), F32)
    row_number = lax.broadcasted_iota(jnp.int32, (SLOT_ROWS, LANES), 0).astype(F32) + 1.0
    ends = []

    def unpack(slot):
        source, target, weight = weights_ref[0], weights_ref[1], weights_ref[2]
        rows = pl.ds(slot * SLOT_ROWS, SLOT_ROWS)
        source_row = jnp.floor(source * (1.0 / LANES))
        target_row = jnp.floor(target * (1.0 / COLUMNS))
        columns_ref[rows, :] = (source - source_row * LANES).astype(jnp.int32)
        lists_ref[0, rows, :] = source_row
        lists_ref[1, rows, :] = target_row
        lists_ref[2, rows, :] = target - target_row * COLUMNS
        lists_ref[3, rows, :] = weight
        return jnp.max(jnp.where(weight != 0.0, row_number, 0.0)).astype(jnp.int32)

    if own_slot:
        tile = here if reset else chosen(here, HELPED_BY, here)
        rows = pl.ds(pl.multiple_of(tile * SLOT_ROWS, SLOT_ROWS), SLOT_ROWS)
        for kind in range(3):
            part = own[kind][rows, :].astype(F32)
            if kind == 2 and reset:
                part = jnp.where(helps, part, 0.0)
            weights_ref[kind] = part
        ends.append(unpack(0))
        for field in range(FIELDS):
            largest = jnp.maximum(largest, jnp.abs(own[3][field, 0:8, :]))
            largest = jnp.maximum(largest, jnp.abs(own[3][field, 8:16, :]))
            for row in range(ATMOS_ROWS):
                cells_ref[0, row, field : field + 1, :] = own[3][field, row : row + 1, :]
    count = own_slot + len(slots)
    for slot, (operand, list_at, cells_at, only) in enumerate(slots, own_slot):
        ref = operand_refs[operand]
        for kind in range(3):
            rows = pl.ds(list_at + kind * SLOT_ROWS, SLOT_ROWS)
            part = ref[rows, :]
            if kind == 2 and only is not None:
                part = jnp.where(helps == only, part, 0.0)
            weights_ref[kind] = part
        ends.append(unpack(slot))
        for row in range(ATMOS_ROWS):
            cells = ref[pl.ds(cells_at + row * FIELDS, FIELDS), :]
            cells_ref[slot, row] = cells
            largest = jnp.maximum(largest, jnp.abs(cells))
    scale = LOW_TOP / jnp.maximum(jnp.max(largest), 1e-30)
    unscale = 1.0 / scale

    spare = count * SLOT_ROWS
    lists_ref[:, spare : spare + 8, :] = jnp.zeros((4, 8, LANES), F32)
    columns_ref[spare : spare + 8, :] = jnp.zeros((8, LANES), jnp.int32)
    firsts = [jnp.int32(0)]
    for end in ends:
        firsts.append(firsts[-1] + end)
    live = firsts.pop()

    def row_of(place):
        shift = jnp.int32(0)
        for slot in range(1, count):
            shift = jnp.where(place >= firsts[slot], slot * SLOT_ROWS - firsts[slot], shift)
        return jnp.where(place < live, place + shift, spare)

    if reset is None:
        total_ref[...] = jnp.zeros_like(total_ref)
    elif reset:

        @pl.when(helps)
        def _():
            total_ref[...] = jnp.zeros_like(total_ref)

        @pl.when(jnp.logical_not(helps))
        def _():
            total_ref[...] = start_ref[...]
    else:
        total_ref[...] = start_ref[...]
    ones, zeros = jnp.ones((), BF16), jnp.zeros((), BF16)
    iota = lax.broadcasted_iota(jnp.int32, (COLUMNS, LANES), 0).astype(F32).astype(BF16)

    def hot(values, height):
        line = jnp.broadcast_to(values, (16, LANES)).astype(BF16)
        return [jnp.where(line == iota[at : at + 16], ones, zeros) for at in range(0, height, 16)]

    def chunk(place, entries):
        for entry in range(entries):
            at = row_of(place + entry)
            one = pl.ds(at, 1)
            slot = jnp.minimum(lax.div(at, SLOT_ROWS), count - 1)
            lanes = slice(entry * LANES, (entry + 1) * LANES)
            row_here = jnp.broadcast_to(lists_ref[0, one, :], (FIELDS, LANES))
            column_here = jnp.broadcast_to(columns_ref[one, :], (FIELDS, LANES))
            picked = jnp.zeros((FIELDS, LANES), F32)
            for row in range(ATMOS_ROWS):
                found_here = jnp.take_along_axis(
                    cells_ref[slot, row], column_here, axis=1, mode="promise_in_bounds"
                )
                picked = jnp.where(row_here == float(row), found_here, picked)
            weighted = picked * lists_ref[3, one, :]
            high = weighted.astype(BF16).astype(F32)
            low = (weighted - high) * scale
            row_hot = hot(lists_ref[1, one, :], ROWS)
            for field in range(FIELDS):
                first = field * ROWS
                line = jnp.broadcast_to(high[field : field + 1, :], (16, LANES)).astype(BF16)
                for part in range(4):
                    high_ref[first + part * 16 : first + part * 16 + 16, lanes] = line * row_hot[part]
                line = jnp.broadcast_to(low[field : field + 1, :], (16, LANES)).astype(BF16)
                for part in range(2):
                    both = [line * row_hot[2 * part], line * row_hot[2 * part + 1]]
                    low_ref[first + part * 32 : first + part * 32 + 32, lanes] = jnp.concatenate(
                        both, axis=0
                    ).astype(F8)
            column_hot = hot(lists_ref[2, one, :], COLUMNS)
            for part in range(COLUMNS // 16):
                high_hot_ref[part * 16 : part * 16 + 16, lanes] = column_hot[part]
            for part in range(COLUMNS // 32):
                low_hot_ref[part * 32 : part * 32 + 32, lanes] = jnp.concatenate(
                    column_hot[2 * part : 2 * part + 2], axis=0
                ).astype(F8)
        over_entries = (((1,), (1,)), ((), ()))
        used = slice(0, entries * LANES)
        total_ref[...] += lax.dot_general(
            high_ref[:, used], high_hot_ref[:, used], over_entries, preferred_element_type=F32
        ) + unscale * lax.dot_general(
            low_ref[:, used], low_hot_ref[:, used], over_entries, preferred_element_type=F32
        )

    def chunk_step(at, carry):
        chunk(at * CHUNK_ROWS, CHUNK_ROWS)
        return carry

    half = CHUNK_ROWS // 2
    wholes = lax.div(live + (half - 1), CHUNK_ROWS)
    lax.fori_loop(0, wholes, chunk_step, 0)

    @pl.when(live > wholes * CHUNK_ROWS)
    def _():
        chunk(wholes * CHUNK_ROWS, half)


def finish_kernel(
    total_ref,
    helped_ref,
    solved_ref,
    gain_ref,
    result_ref,
    flux_ref,
    forcing_ref,
    to_east_ref,
    to_west_ref,
    sibling_ref,
    other_ref,
):
    def block_step(block, carry):
        rows = pl.ds(pl.multiple_of(block * 8, 8), 8)
        flux = []
        for field in range(FIELDS):
            from_rows = pl.ds(pl.multiple_of(field * ROWS + block * 8, 8), 8)
            value = total_ref[from_rows, :] + helped_ref[from_rows, :]
            flux_ref[field, rows, :] = value
            flux.append(value)
        heat = flux[0] + flux[1] + flux[2] + flux[3] + flux[4]
        salt = flux[7] - flux[5] - flux[6]
        forcing_ref[0, rows, :] = heat
        forcing_ref[1, rows, :] = salt
        for level in range(NZ):
            gain = gain_ref[level, rows, :]
            for tracer, forcing in enumerate((heat, salt)):
                channel = tracer * NZ + level
                result_ref[channel, rows, :] = solved_ref[channel, rows, :] + forcing * gain
        return carry

    lax.fori_loop(0, ROWS // 8, block_step, 0)
    pack_columns(
        lambda channel, row: (result_ref[channel, pl.ds(row, 8), LANES:], LANES - 1),
        range(CHANNELS),
        to_east_ref,
    )
    pack_columns(
        lambda channel, row: (result_ref[channel, pl.ds(row, 8), :LANES], 0),
        range(CHANNELS),
        to_west_ref,
    )
    pack_rows(
        lambda channel: result_ref[channel, ROWS - 1 : ROWS, :],
        lambda channel: result_ref[channel, 0:1, :],
        range(CHANNELS),
        sibling_ref,
        other_ref,
    )


EASTWARD = [(i, (i + 1) % GX) for i in range(GX)]
WESTWARD = [((i + 1) % GX, i) for i in range(GX)]
SIBLINGS = [(y, y ^ 1) for y in range(GY)]
OTHERS = [
    (x * GY + y, x * GY + (y + 1 if y % 2 else y - 1)) for x in range(GX) for y in range(1, GY - 1)
]
FOLD = [(x * GY + GY - 1, (GX - 1 - x) * GY + GY - 1) for x in range(GX)]


def exchange(to_east, to_west, sibling, other, fold=None):
    if fold is None:
        others = lax.ppermute(other, ("gx", "gy"), OTHERS + FOLD)
        folded = others
    else:
        others = lax.ppermute(other, ("gx", "gy"), OTHERS)
        folded = lax.ppermute(fold, ("gx", "gy"), FOLD)
    return (
        lax.ppermute(to_east, "gx", EASTWARD),
        lax.ppermute(to_west, "gx", WESTWARD),
        lax.ppermute(sibling, "gy", SIBLINGS),
        others,
        folded,
    )


def land(operands, slots, own_slot, reset):
    count = own_slot + len(slots)
    (total,) = call(
        functools.partial(land_kernel, slots, own_slot, reset),
        [(FIELDS * ROWS, COLUMNS)],
        operands,
        [
            pltpu.VMEM((4, count * SLOT_ROWS + 8, LANES), F32),
            pltpu.VMEM((count * SLOT_ROWS + 8, LANES), jnp.int32),
            pltpu.VMEM((count, ATMOS_ROWS, FIELDS, LANES), F32),
            pltpu.VMEM((FIELDS * ROWS, CHUNK), BF16),
            pltpu.VMEM((FIELDS * ROWS, CHUNK), F8),
            pltpu.VMEM((COLUMNS, CHUNK), BF16),
            pltpu.VMEM((COLUMNS, CHUNK), F8),
            pltpu.VMEM((3, SLOT_ROWS, LANES), F32),
        ],
        moved=100_000,
    )
    return total


def local(
    tracers,
    east_speed,
    north_speed,
    vertical_mix,
    level_count,
    atmosphere_flux,
    intersection_source,
    intersection_target,
    intersection_weight,
):
    q = tracers.reshape(CHANNELS, ROWS, COLUMNS)
    statics = [east_speed, north_speed, level_count, vertical_mix]
    lists = [intersection_source, intersection_target, intersection_weight, atmosphere_flux]
    column_rim, row_rim = (ROWS, LANES), (2 * RIM, LANES)
    both = (2 * RIM + LIST + PAYLOAD, LANES)
    steps = len(ENTRY_STEPS)
    packed = call(
        pack_kernel,
        [column_rim, column_rim, both, both, row_rim] + [(PAYLOAD, LANES)] * steps,
        [q, *statics[:3], *lists],
        [
            *[pltpu.VMEM(part.shape, part.dtype) for part in (q, *statics[:3], *lists)],
            pltpu.VMEM((ATMOS, LANES), F32),
            pltpu.SemaphoreType.DMA((8,)),
        ],
        in_hbm=True,
    )
    entries = [
        lax.ppermute(part, "gy", list(pairs))
        for part, pairs in zip(packed[5:], ENTRY_STEPS, strict=True)
    ]
    rims = exchange(*packed[:5])
    first, second, cells = 2 * RIM, 2 * RIM + LIST, 2 * RIM + 2 * LIST
    most = land([*lists, rims[2]], ((0, first, cells, None),), 1, None)
    partial = land(
        [rims[3], *entries, most], ((0, first, cells, None), (1, 0, LIST, True)), 0, False
    )
    helped = lax.ppermute(partial, "gy", list(DENSE))
    total = land(
        [*lists, rims[2], rims[3], *entries, partial],
        ((0, second, cells, None), (1, second, cells, None), (2, 0, LIST, False))
        + tuple((2 + step, 0, LIST, None) for step in range(1, steps)),
        1,
        True,
    )
    rim_scratch = [pltpu.VMEM(row_rim, F32)] * 4
    solved, gain = call(
        functools.partial(step_kernel, True),
        [q.shape, east_speed.shape],
        [q, *rims, *rims, *statics, partial],
        rim_scratch,
        moved=8_000_000,
    )
    result, flux, forcing, *out_rims = call(
        finish_kernel,
        [q.shape, (FIELDS, ROWS, COLUMNS), (TRACERS, ROWS, COLUMNS)]
        + [column_rim, column_rim, row_rim, row_rim],
        [total, helped, solved, gain],
    )
    second_rims = exchange(*out_rims)
    (result,) = call(
        functools.partial(step_kernel, False),
        [q.shape],
        [result, *second_rims, *rims, *statics, forcing],
        [pltpu.VMEM(q.shape, F32), pltpu.SemaphoreType.DMA((ROWS // 8,)), *rim_scratch],
        moved=8_000_000,
        out_hbm=True,
    )
    return result.reshape(tracers.shape), flux


def solution(mesh):
    in_specs = (
        P(None, None, "gy", "gx"),
        P(None, "gy", "gx"),
        P(None, "gy", "gx"),
        P(None, "gy", "gx"),
        P("gy", "gx"),
        P(None, "gy", "gx"),
        P("gy", "gx"),
        P("gy", "gx"),
        P("gy", "gx"),
    )
    out_specs = (P(None, None, "gy", "gx"), P(None, "gy", "gx"))
    return jax.shard_map(local, mesh=mesh, in_specs=in_specs, out_specs=out_specs, check_vma=False)
```

```python
import functools

import jax
import jax.numpy as jnp
from jax import lax
from jax.experimental import pallas as pl
from jax.experimental.pallas import tpu as pltpu
from jax.sharding import PartitionSpec as P

DIFFUSE = 0.05
FIELDS = 8
TRACERS = 2
NZ = 8
ROWS = 64
COLUMNS = 256
LANES = 128
GX = 8
GY = 16
SLOT_ROWS = 32
ATMOS_ROWS = 16
HELPED_BY = {12: GY - 2, 11: GY - 1}
DENSE = ((12, GY - 2), (11, GY - 1))
SENT_AWAY = 13
ENTRY_STEPS = (
    ((7, GY - 2), (8, GY - 1), (10, 12), (9, 11)),
    ((8, GY - 2), (7, GY - 1)),
    ((9, GY - 2), (13, GY - 1)),
)
CHANNELS = TRACERS * NZ
COUNT_AT = 24
RIM = 32
LIST = 3 * SLOT_ROWS
ATMOS = FIELDS * ATMOS_ROWS
PAYLOAD = LIST + ATMOS
CHUNK_ROWS = 16
CHUNK = CHUNK_ROWS * LANES
VMEM_LIMIT = 48 * 1024 * 1024
PACK_LIMIT = 63 * 1024 * 1024
F32 = jnp.float32
BF16 = jnp.bfloat16
F8 = jnp.float8_e4m3fn
LOW_TOP = 65536.0


def call(
    kernel, out_shapes, operands, scratch=(), flops=0, moved=4_000_000, in_hbm=False, out_hbm=False
):
    place = pltpu.HBM if in_hbm else pltpu.VMEM
    out_place = pl.ANY if out_hbm else pltpu.VMEM
    return pl.pallas_call(
        kernel,
        out_shape=[jax.ShapeDtypeStruct(shape, F32) for shape in out_shapes],
        in_specs=[pl.BlockSpec(memory_space=place) for _ in operands],
        out_specs=[pl.BlockSpec(memory_space=out_place) for _ in out_shapes],
        scratch_shapes=list(scratch),
        compiler_params=pltpu.CompilerParams(vmem_limit_bytes=PACK_LIMIT if in_hbm else VMEM_LIMIT),
        cost_estimate=pl.CostEstimate(flops=flops, bytes_accessed=moved, transcendentals=0),
    )(*operands)


def is_odd_column():
    return lax.rem(lax.axis_index("gx"), 2) == 1


def pack_columns(east_of, east_channels, west_of, west_channels, far_ref, near_ref):
    odd = is_odd_column()
    lane = lax.broadcasted_iota(jnp.int32, (8, LANES), 1)
    for block in range(ROWS // 8):
        tiles = []
        for pick, channels in ((east_of, east_channels), (west_of, west_channels)):
            tile = jnp.zeros((8, LANES), F32)
            for channel in channels:
                value, at = pick(channel, block * 8)
                shift = (channel - at) % LANES
                moved = pltpu.roll(value, shift, axis=1) if shift else value
                tile = jnp.where(lane == channel, moved, tile)
            tiles.append(tile)
        east, west = tiles
        far_ref[pl.ds(block * 8, 8), :] = jnp.where(odd, east, west)
        near_ref[pl.ds(block * 8, 8), :] = jnp.where(odd, west, east)


def pack_row(value, channel, out_ref):
    out_ref[pl.ds(channel, 1), :] = value[:, :LANES]
    out_ref[pl.ds(RIM + channel, 1), :] = value[:, LANES:]


def is_even():
    return lax.rem(lax.axis_index("gy"), 2) == 0


def pack_rows(top_of, bottom_of, channels, sibling_ref, other_ref):
    even = is_even()
    zeros = jnp.zeros((2 * RIM, LANES), F32)
    sibling_ref[0 : 2 * RIM, :] = zeros
    other_ref[0 : 2 * RIM, :] = zeros
    for channel in channels:
        top, bottom = top_of(channel), bottom_of(channel)
        pack_row(jnp.where(even, top, bottom), channel, sibling_ref)
        pack_row(jnp.where(even, bottom, top), channel, other_ref)


def chosen(here, table, default):
    for key, value in table.items():
        default = jnp.where(here == key, value, default)
    return default


def among(here, table):
    return functools.reduce(jnp.logical_or, [here == key for key in table])


def list_into(lists, out_ref, at, tile, valid=None):
    rows = pl.ds(pl.multiple_of(tile * SLOT_ROWS, SLOT_ROWS), SLOT_ROWS)
    for kind, ref in enumerate(lists):
        part = ref[rows, :].astype(F32)
        if kind == 2 and valid is not None:
            part = jnp.where(valid, part, 0.0)
        out_ref[at + kind * SLOT_ROWS : at + (kind + 1) * SLOT_ROWS, :] = part


def pack_kernel(*refs):
    steps = len(ENTRY_STEPS)
    froms, refs = refs[:8], refs[8:]
    (to_far_ref, to_near_ref, sibling_ref, other_ref, fold_ref), refs = refs[:5], refs[5:]
    entry_refs, intos, (cells_ref, sems) = refs[:steps], refs[steps:-2], refs[-2:]
    tracers_ref, east_ref, north_ref, count_ref, source_ref, target_ref, weight_ref, atmos_ref = intos
    copies = [
        pltpu.make_async_copy(array, into, sems.at[n])
        for n, (array, into) in enumerate(zip(froms, intos, strict=True))
    ]
    for copy in copies:
        copy.start()
    for copy in copies[4:]:
        copy.wait()
    here = lax.axis_index("gy")
    even = is_even()
    lists = (source_ref, target_ref, weight_ref)
    for field in range(FIELDS):
        for row in range(ATMOS_ROWS):
            to = row * FIELDS + field
            cells_ref[to : to + 1, :] = atmos_ref[field, row : row + 1, :]
    cells = cells_ref[...]
    for pairs, out_ref in zip(ENTRY_STEPS, entry_refs, strict=True):
        wanted = {source: HELPED_BY.get(to, to) for source, to in pairs}
        list_into(lists, out_ref, 0, chosen(here, wanted, here))
        out_ref[LIST:PAYLOAD, :] = cells
    partner = here ^ 1
    list_into(lists, sibling_ref, 2 * RIM, chosen(partner, HELPED_BY, partner))
    list_into(lists, sibling_ref, 2 * RIM + LIST, partner, among(partner, HELPED_BY))
    sibling_ref[2 * RIM + 2 * LIST :, :] = cells
    away = jnp.clip(jnp.where(even, here - 1, here + 1), 0, GY - 1)
    below_top = here != GY - 1
    helped = jnp.logical_and(below_top, among(away, HELPED_BY))
    list_into(lists, other_ref, 2 * RIM, chosen(away, HELPED_BY, away), helped)
    direct = jnp.logical_and(below_top, here != SENT_AWAY)
    list_into(lists, other_ref, 2 * RIM + LIST, away, direct)
    other_ref[2 * RIM + 2 * LIST :, :] = cells

    for copy in copies[:4]:
        copy.wait()

    def east_column(channel, row):
        rows = pl.ds(row, 8)
        if channel < CHANNELS:
            return tracers_ref[channel, rows, LANES:], LANES - 1
        if channel < COUNT_AT:
            return east_ref[channel - CHANNELS, rows, LANES:], LANES - 1
        return count_ref[rows, LANES:].astype(F32), LANES - 1

    def west_column(channel, row):
        rows = pl.ds(row, 8)
        if channel < CHANNELS:
            return tracers_ref[channel, rows, :LANES], 0
        return count_ref[rows, :LANES].astype(F32), 0

    pack_columns(
        east_column,
        [*range(CHANNELS + NZ), COUNT_AT],
        west_column,
        [*range(CHANNELS), COUNT_AT],
        to_far_ref,
        to_near_ref,
    )

    def top_of(channel):
        if channel < CHANNELS:
            return tracers_ref[channel, ROWS - 1 : ROWS, :]
        if channel < COUNT_AT:
            return north_ref[channel - CHANNELS, ROWS - 1 : ROWS, :]
        return count_ref[ROWS - 1 : ROWS, :].astype(F32)

    def bottom_of(channel):
        if channel < CHANNELS:
            return tracers_ref[channel, 0:1, :]
        if channel < COUNT_AT:
            return jnp.zeros((1, COLUMNS), F32)
        return count_ref[0:1, :].astype(F32)

    pack_rows(top_of, bottom_of, range(COUNT_AT + 1), sibling_ref, other_ref)
    fold_ref[...] = other_ref[0 : 2 * RIM, :]


def step_kernel(
    forced,
    q_ref,
    from_far_ref,
    from_near_ref,
    from_sibling_ref,
    from_other_ref,
    from_fold_ref,
    static_far_ref,
    static_near_ref,
    static_sibling_ref,
    static_other_ref,
    static_fold_ref,
    east_ref,
    north_ref,
    count_ref,
    mix_ref,
    *more_refs,
):
    if forced:
        out_ref, gain_ref = more_refs[-10:-8]
    else:
        forcing_ref, out_hbm, out_ref, sems = more_refs[:4]
    from_south_ref, top_ref, static_south_ref, static_top_ref = more_refs[-8:-4]
    from_west_ref, from_east_ref, static_west_ref, static_east_ref = more_refs[-4:]
    odd = is_odd_column()
    from_west_ref[...] = jnp.where(odd, from_near_ref[...], from_far_ref[...])
    from_east_ref[...] = jnp.where(odd, from_far_ref[...], from_near_ref[...])
    static_west_ref[...] = jnp.where(odd, static_near_ref[...], static_far_ref[...])
    static_east_ref[...] = jnp.where(odd, static_far_ref[...], static_near_ref[...])
    even = is_even()
    on_top = lax.axis_index("gy") == GY - 1
    lane = lax.broadcasted_iota(jnp.int32, (8, LANES), 1)
    row = lax.broadcasted_iota(jnp.int32, (8, LANES), 0)
    first_lane, last_lane = lane == 0, lane == LANES - 1
    first_row, last_row = row == 0, row == 7

    def set_rims(sibling_rim, other_rim, fold_rim, south, north):
        @pl.when(even)
        def _():
            south[...] = other_rim[0 : 2 * RIM, :]
            north[...] = sibling_rim[0 : 2 * RIM, :]

        @pl.when(jnp.logical_not(even))
        def _():
            south[...] = sibling_rim[0 : 2 * RIM, :]
            north[...] = other_rim[0 : 2 * RIM, :]

        @pl.when(on_top)
        def _():
            flipped = LANES - 1 - lane
            for half in range(2):
                for block in range(RIM // 8):
                    rows = fold_rim[pl.ds((1 - half) * RIM + block * 8, 8), :]
                    north[pl.ds(half * RIM + block * 8, 8), :] = jnp.take_along_axis(
                        rows, flipped, axis=1, mode="promise_in_bounds"
                    )

    set_rims(from_sibling_ref, from_other_ref, from_fold_ref, from_south_ref, top_ref)
    set_rims(
        static_sibling_ref, static_other_ref, static_fold_ref, static_south_ref, static_top_ref
    )

    def block_step(block, carry):
        at = pl.multiple_of(block * 8, 8)
        below = pl.multiple_of(jnp.maximum(block - 1, 0) * 8, 8)
        above = pl.multiple_of(jnp.minimum(block + 1, ROWS // 8 - 1) * 8, 8)
        is_first, is_last = block == 0, block == ROWS // 8 - 1
        rows = pl.ds(at, 8)

        def halves(load):
            return [load(rows, slice(0, LANES)), load(rows, slice(LANES, 2 * LANES))]

        def to_west_of(parts, rim):
            low = jnp.where(last_lane, rim, parts[0])
            high = jnp.where(last_lane, parts[0], parts[1])
            return [pltpu.roll(low, 1, axis=1), pltpu.roll(high, 1, axis=1)]

        def to_east_of(parts, rim):
            low = jnp.where(first_lane, parts[1], parts[0])
            high = jnp.where(first_lane, rim, parts[1])
            return [
                pltpu.roll(low, LANES - 1, axis=1),
                pltpu.roll(high, LANES - 1, axis=1),
            ]

        def to_south_of(load, parts, rim_ref, channel):
            found = []
            for half in range(2):
                lanes = slice(half * LANES, (half + 1) * LANES)
                rim = jnp.broadcast_to(
                    rim_ref[half * RIM + channel : half * RIM + channel + 1, :], (8, LANES)
                )
                near = jnp.where(is_first, rim, load(pl.ds(below, 8), lanes))
                found.append(pltpu.roll(jnp.where(last_row, near, parts[half]), 1, axis=0))
            return found

        def to_north_of(load, parts, rim_ref, channel):
            found = []
            for half in range(2):
                lanes = slice(half * LANES, (half + 1) * LANES)
                rim = jnp.broadcast_to(
                    rim_ref[half * RIM + channel : half * RIM + channel + 1, :], (8, LANES)
                )
                near = jnp.where(is_last, rim, load(pl.ds(above, 8), lanes))
                found.append(pltpu.roll(jnp.where(first_row, near, parts[half]), 7, axis=0))
            return found

        def west_rim(ref, channel):
            return pltpu.roll(ref[rows, :], (LANES - 1 - channel) % LANES, axis=1)

        def east_rim(ref, channel):
            shift = (LANES - channel) % LANES
            return pltpu.roll(ref[rows, :], shift, axis=1) if shift else ref[rows, :]

        def load_count(where, lanes):
            return count_ref[where, lanes].astype(F32)

        count = halves(load_count)
        sides = [
            to_east_of(count, east_rim(static_east_ref, COUNT_AT)),
            to_west_of(count, west_rim(static_west_ref, COUNT_AT)),
            to_north_of(load_count, count, static_top_ref, COUNT_AT),
            to_south_of(load_count, count, static_south_ref, COUNT_AT),
        ]
        shared = [[jnp.minimum(count[half], side[half]) for half in range(2)] for side in sides]
        closed = jnp.logical_and(jnp.logical_and(on_top, is_last), last_row)

        values = [[[None, None] for _ in range(NZ)] for _ in range(TRACERS)]
        for level in range(NZ):
            east = halves(lambda where, lanes: east_ref[level, where, lanes])
            west = to_west_of(east, west_rim(static_west_ref, CHANNELS + level))

            def load_north(where, lanes):
                return north_ref[level, where, lanes]

            north = halves(load_north)
            south = to_south_of(load_north, north, static_south_ref, CHANNELS + level)
            coefs = []
            for half in range(2):
                limit = float(level)
                up = jnp.where(closed, 0.0, north[half])
                open_e, open_w, open_n, open_s = [side[half] > limit for side in shared]

                def into(opened, speed):
                    return jnp.where(opened, DIFFUSE - jnp.minimum(speed, 0.0), 0.0)

                def away(opened, speed):
                    return jnp.where(opened, DIFFUSE + jnp.maximum(speed, 0.0), 0.0)

                from_e, lost_e = into(open_e, east[half]), away(open_e, east[half])
                from_w, lost_w = away(open_w, west[half]), into(open_w, west[half])
                from_n, lost_n = into(open_n, up), away(open_n, up)
                from_s, lost_s = away(open_s, south[half]), into(open_s, south[half])
                kept = 1.0 - ((lost_e + lost_w) + (lost_n + lost_s))
                coefs.append((kept, from_e, from_w, from_n, from_s))
            for tracer in range(TRACERS):
                channel = tracer * NZ + level

                def load_q(where, lanes):
                    return q_ref[channel, where, lanes]

                q = halves(load_q)
                q_e = to_east_of(q, east_rim(from_east_ref, channel))
                q_w = to_west_of(q, west_rim(from_west_ref, channel))
                q_n = to_north_of(load_q, q, top_ref, channel)
                q_s = to_south_of(load_q, q, from_south_ref, channel)
                for half in range(2):
                    kept, from_e, from_w, from_n, from_s = coefs[half]
                    values[tracer][level][half] = (
                        kept * q[half]
                        + (from_e * q_e[half] + from_w * q_w[half])
                        + (from_n * q_n[half] + from_s * q_s[half])
                    )
        for half in range(2):
            lanes = slice(half * LANES, (half + 1) * LANES)
            sides_here = [[values[t][k][half] for k in range(NZ)] for t in range(TRACERS)]
            surface = count[half] > 0.0
            if forced:
                sides_here.append([jnp.where(surface, 1.0, 0.0)] + [None] * (NZ - 1))
            else:
                for tracer in range(TRACERS):
                    forcing = jnp.where(surface, forcing_ref[tracer, rows, lanes], 0.0)
                    sides_here[tracer][0] = sides_here[tracer][0] + forcing
            ratios = []
            partials = [[] for _ in sides_here]
            for level in range(NZ):
                thickness = 1.0 + level / NZ
                upper = lower = None
                if level >= 1:
                    mix = mix_ref[level - 1, rows, lanes]
                    upper = jnp.where(count[half] > float(level), mix * (1.0 / thickness), 0.0)
                if level <= NZ - 2:
                    mix = mix_ref[level, rows, lanes]
                    lower = jnp.where(
                        count[half] > float(level + 1), mix * (1.0 / thickness), 0.0
                    )
                if upper is None:
                    pivot = 1.0 + lower
                elif lower is None:
                    pivot = 1.0 + upper - upper * ratios[-1]
                else:
                    pivot = 1.0 + upper + lower - upper * ratios[-1]
                inverse = 1.0 / pivot
                if lower is not None:
                    ratios.append(lower * inverse)
                for side, partial in zip(sides_here, partials, strict=True):
                    right = side[level]
                    if level >= 1:
                        carried = upper * partial[-1]
                        right = carried if right is None else right + carried
                    partial.append(right * inverse)
            for index, partial in enumerate(partials):
                solved = partial[-1]
                for level in range(NZ - 1, -1, -1):
                    if level < NZ - 1:
                        solved = partial[level] + ratios[level] * solved
                    if index < TRACERS:
                        out_ref[index * NZ + level, rows, lanes] = solved
                    else:
                        gain_ref[level, rows, lanes] = solved
        if not forced:
            block_copy(block).start()
        return carry

    def block_copy(block):
        rows = pl.ds(pl.multiple_of(block * 8, 8), 8)
        return pltpu.make_async_copy(out_ref.at[:, rows, :], out_hbm.at[:, rows, :], sems.at[block])

    lax.fori_loop(0, ROWS // 8, block_step, 0)
    if not forced:
        for block in range(ROWS // 8):
            block_copy(block).wait()


def land_kernel(slots, own_slot, reset, *refs):
    operand_refs, refs = refs[:-9], refs[-9:]
    if own_slot:
        own, operand_refs = operand_refs[:4], operand_refs[4:]
    here = lax.axis_index("gy")
    helps = among(here, HELPED_BY)
    if reset is not None:
        start_ref = operand_refs[-1]
    total_ref, lists_ref, columns_ref, cells_ref = refs[:4]
    high_ref, low_ref, high_hot_ref, low_hot_ref, weights_ref = refs[4:]
    largest = jnp.zeros((8, LANES), F32)
    row_number = lax.broadcasted_iota(jnp.int32, (SLOT_ROWS, LANES), 0).astype(F32) + 1.0
    ends = []

    def unpack(slot):
        source, target, weight = weights_ref[0], weights_ref[1], weights_ref[2]
        rows = pl.ds(slot * SLOT_ROWS, SLOT_ROWS)
        source_row = jnp.floor(source * (1.0 / LANES))
        target_row = jnp.floor(target * (1.0 / COLUMNS))
        columns_ref[rows, :] = (source - source_row * LANES).astype(jnp.int32)
        lists_ref[0, rows, :] = source_row
        lists_ref[1, rows, :] = target_row
        lists_ref[2, rows, :] = target - target_row * COLUMNS
        lists_ref[3, rows, :] = weight
        return jnp.max(jnp.where(weight != 0.0, row_number, 0.0)).astype(jnp.int32)

    if own_slot:
        tile = here if reset else chosen(here, HELPED_BY, here)
        rows = pl.ds(pl.multiple_of(tile * SLOT_ROWS, SLOT_ROWS), SLOT_ROWS)
        for kind in range(3):
            part = own[kind][rows, :].astype(F32)
            if kind == 2 and reset:
                part = jnp.where(helps, part, 0.0)
            weights_ref[kind] = part
        ends.append(unpack(0))
        for field in range(FIELDS):
            largest = jnp.maximum(largest, jnp.abs(own[3][field, 0:8, :]))
            largest = jnp.maximum(largest, jnp.abs(own[3][field, 8:16, :]))
            for row in range(ATMOS_ROWS):
                cells_ref[0, row, field : field + 1, :] = own[3][field, row : row + 1, :]
    count = own_slot + len(slots)
    for slot, (operand, list_at, cells_at, only) in enumerate(slots, own_slot):
        ref = operand_refs[operand]
        for kind in range(3):
            rows = pl.ds(list_at + kind * SLOT_ROWS, SLOT_ROWS)
            part = ref[rows, :]
            if kind == 2 and only is not None:
                part = jnp.where(helps == only, part, 0.0)
            weights_ref[kind] = part
        ends.append(unpack(slot))
        for row in range(ATMOS_ROWS):
            cells = ref[pl.ds(cells_at + row * FIELDS, FIELDS), :]
            cells_ref[slot, row] = cells
            largest = jnp.maximum(largest, jnp.abs(cells))
    scale = LOW_TOP / jnp.maximum(jnp.max(largest), 1e-30)
    unscale = 1.0 / scale

    spare = count * SLOT_ROWS
    lists_ref[:, spare : spare + 8, :] = jnp.zeros((4, 8, LANES), F32)
    columns_ref[spare : spare + 8, :] = jnp.zeros((8, LANES), jnp.int32)
    firsts = [jnp.int32(0)]
    for end in ends:
        firsts.append(firsts[-1] + end)
    live = firsts.pop()

    def row_of(place):
        shift = jnp.int32(0)
        for slot in range(1, count):
            shift = jnp.where(place >= firsts[slot], slot * SLOT_ROWS - firsts[slot], shift)
        return jnp.where(place < live, place + shift, spare)

    if reset is None:
        total_ref[...] = jnp.zeros_like(total_ref)
    elif reset:

        @pl.when(helps)
        def _():
            total_ref[...] = jnp.zeros_like(total_ref)

        @pl.when(jnp.logical_not(helps))
        def _():
            total_ref[...] = start_ref[...]
    else:
        total_ref[...] = start_ref[...]
    ones, zeros = jnp.ones((), BF16), jnp.zeros((), BF16)
    iota = lax.broadcasted_iota(jnp.int32, (COLUMNS, LANES), 0).astype(F32).astype(BF16)

    def hot(values, height):
        line = jnp.broadcast_to(values, (16, LANES)).astype(BF16)
        return [jnp.where(line == iota[at : at + 16], ones, zeros) for at in range(0, height, 16)]

    def chunk(place, entries):
        for entry in range(entries):
            at = row_of(place + entry)
            one = pl.ds(at, 1)
            slot = jnp.minimum(lax.div(at, SLOT_ROWS), count - 1)
            lanes = slice(entry * LANES, (entry + 1) * LANES)
            row_here = jnp.broadcast_to(lists_ref[0, one, :], (FIELDS, LANES))
            column_here = jnp.broadcast_to(columns_ref[one, :], (FIELDS, LANES))
            picked = jnp.zeros((FIELDS, LANES), F32)
            for row in range(ATMOS_ROWS):
                found_here = jnp.take_along_axis(
                    cells_ref[slot, row], column_here, axis=1, mode="promise_in_bounds"
                )
                picked = jnp.where(row_here == float(row), found_here, picked)
            weighted = picked * lists_ref[3, one, :]
            high = weighted.astype(BF16).astype(F32)
            low = (weighted - high) * scale
            row_hot = hot(lists_ref[1, one, :], ROWS)
            for field in range(FIELDS):
                first = field * ROWS
                line = jnp.broadcast_to(high[field : field + 1, :], (16, LANES)).astype(BF16)
                for part in range(4):
                    high_ref[first + part * 16 : first + part * 16 + 16, lanes] = line * row_hot[part]
                line = jnp.broadcast_to(low[field : field + 1, :], (16, LANES)).astype(BF16)
                for part in range(2):
                    both = [line * row_hot[2 * part], line * row_hot[2 * part + 1]]
                    low_ref[first + part * 32 : first + part * 32 + 32, lanes] = jnp.concatenate(
                        both, axis=0
                    ).astype(F8)
            column_hot = hot(lists_ref[2, one, :], COLUMNS)
            for part in range(COLUMNS // 16):
                high_hot_ref[part * 16 : part * 16 + 16, lanes] = column_hot[part]
            for part in range(COLUMNS // 32):
                low_hot_ref[part * 32 : part * 32 + 32, lanes] = jnp.concatenate(
                    column_hot[2 * part : 2 * part + 2], axis=0
                ).astype(F8)
        over_entries = (((1,), (1,)), ((), ()))
        used = slice(0, entries * LANES)
        total_ref[...] += lax.dot_general(
            high_ref[:, used], high_hot_ref[:, used], over_entries, preferred_element_type=F32
        ) + unscale * lax.dot_general(
            low_ref[:, used], low_hot_ref[:, used], over_entries, preferred_element_type=F32
        )

    def chunk_step(at, carry):
        chunk(at * CHUNK_ROWS, CHUNK_ROWS)
        return carry

    half = CHUNK_ROWS // 2
    wholes = lax.div(live + (half - 1), CHUNK_ROWS)
    lax.fori_loop(0, wholes, chunk_step, 0)

    @pl.when(live > wholes * CHUNK_ROWS)
    def _():
        chunk(wholes * CHUNK_ROWS, half)


def finish_kernel(
    total_ref,
    helped_ref,
    solved_ref,
    gain_ref,
    result_ref,
    flux_ref,
    forcing_ref,
    to_far_ref,
    to_near_ref,
    sibling_ref,
    other_ref,
):
    def block_step(block, carry):
        rows = pl.ds(pl.multiple_of(block * 8, 8), 8)
        flux = []
        for field in range(FIELDS):
            from_rows = pl.ds(pl.multiple_of(field * ROWS + block * 8, 8), 8)
            value = total_ref[from_rows, :] + helped_ref[from_rows, :]
            flux_ref[field, rows, :] = value
            flux.append(value)
        heat = flux[0] + flux[1] + flux[2] + flux[3] + flux[4]
        salt = flux[7] - flux[5] - flux[6]
        forcing_ref[0, rows, :] = heat
        forcing_ref[1, rows, :] = salt
        for level in range(NZ):
            gain = gain_ref[level, rows, :]
            for tracer, forcing in enumerate((heat, salt)):
                channel = tracer * NZ + level
                result_ref[channel, rows, :] = solved_ref[channel, rows, :] + forcing * gain
        return carry

    lax.fori_loop(0, ROWS // 8, block_step, 0)
    pack_columns(
        lambda channel, row: (result_ref[channel, pl.ds(row, 8), LANES:], LANES - 1),
        range(CHANNELS),
        lambda channel, row: (result_ref[channel, pl.ds(row, 8), :LANES], 0),
        range(CHANNELS),
        to_far_ref,
        to_near_ref,
    )
    pack_rows(
        lambda channel: result_ref[channel, ROWS - 1 : ROWS, :],
        lambda channel: result_ref[channel, 0:1, :],
        range(CHANNELS),
        sibling_ref,
        other_ref,
    )


FAR = [(x, (x + 1 if x % 2 else x - 1) % GX) for x in range(GX)]
NEAR = [(x, (x - 1 if x % 2 else x + 1) % GX) for x in range(GX)]
SIBLINGS = [(y, y ^ 1) for y in range(GY)]
OTHERS = [
    (x * GY + y, x * GY + (y + 1 if y % 2 else y - 1)) for x in range(GX) for y in range(1, GY - 1)
]
FOLD = [(x * GY + GY - 1, (GX - 1 - x) * GY + GY - 1) for x in range(GX)]


def exchange(to_far, to_near, sibling, other, fold=None):
    if fold is None:
        others = lax.ppermute(other, ("gx", "gy"), OTHERS + FOLD)
        folded = others
    else:
        others = lax.ppermute(other, ("gx", "gy"), OTHERS)
        folded = lax.ppermute(fold, ("gx", "gy"), FOLD)
    return (
        lax.ppermute(to_far, "gx", FAR),
        lax.ppermute(to_near, "gx", NEAR),
        lax.ppermute(sibling, "gy", SIBLINGS),
        others,
        folded,
    )


def land(operands, slots, own_slot, reset):
    count = own_slot + len(slots)
    (total,) = call(
        functools.partial(land_kernel, slots, own_slot, reset),
        [(FIELDS * ROWS, COLUMNS)],
        operands,
        [
            pltpu.VMEM((4, count * SLOT_ROWS + 8, LANES), F32),
            pltpu.VMEM((count * SLOT_ROWS + 8, LANES), jnp.int32),
            pltpu.VMEM((count, ATMOS_ROWS, FIELDS, LANES), F32),
            pltpu.VMEM((FIELDS * ROWS, CHUNK), BF16),
            pltpu.VMEM((FIELDS * ROWS, CHUNK), F8),
            pltpu.VMEM((COLUMNS, CHUNK), BF16),
            pltpu.VMEM((COLUMNS, CHUNK), F8),
            pltpu.VMEM((3, SLOT_ROWS, LANES), F32),
        ],
        moved=100_000,
    )
    return total


def local(
    tracers,
    east_speed,
    north_speed,
    vertical_mix,
    level_count,
    atmosphere_flux,
    intersection_source,
    intersection_target,
    intersection_weight,
):
    q = tracers.reshape(CHANNELS, ROWS, COLUMNS)
    statics = [east_speed, north_speed, level_count, vertical_mix]
    lists = [intersection_source, intersection_target, intersection_weight, atmosphere_flux]
    column_rim, row_rim = (ROWS, LANES), (2 * RIM, LANES)
    both = (2 * RIM + LIST + PAYLOAD, LANES)
    steps = len(ENTRY_STEPS)
    packed = call(
        pack_kernel,
        [column_rim, column_rim, both, both, row_rim] + [(PAYLOAD, LANES)] * steps,
        [q, *statics[:3], *lists],
        [
            *[pltpu.VMEM(part.shape, part.dtype) for part in (q, *statics[:3], *lists)],
            pltpu.VMEM((ATMOS, LANES), F32),
            pltpu.SemaphoreType.DMA((8,)),
        ],
        in_hbm=True,
    )
    entries = [
        lax.ppermute(part, "gy", list(pairs))
        for part, pairs in zip(packed[5:], ENTRY_STEPS, strict=True)
    ]
    rims = exchange(*packed[:5])
    first, second, cells = 2 * RIM, 2 * RIM + LIST, 2 * RIM + 2 * LIST
    most = land([*lists, rims[2]], ((0, first, cells, None),), 1, None)
    partial = land(
        [rims[3], *entries, most], ((0, first, cells, None), (1, 0, LIST, True)), 0, False
    )
    helped = lax.ppermute(partial, "gy", list(DENSE))
    total = land(
        [*lists, rims[2], rims[3], *entries, partial],
        ((0, second, cells, None), (1, second, cells, None), (2, 0, LIST, False))
        + tuple((2 + step, 0, LIST, None) for step in range(1, steps)),
        1,
        True,
    )
    rim_scratch = [pltpu.VMEM(row_rim, F32)] * 4 + [pltpu.VMEM(column_rim, F32)] * 4
    solved, gain = call(
        functools.partial(step_kernel, True),
        [q.shape, east_speed.shape],
        [q, *rims, *rims, *statics, partial],
        rim_scratch,
        moved=8_000_000,
    )
    result, flux, forcing, *out_rims = call(
        finish_kernel,
        [q.shape, (FIELDS, ROWS, COLUMNS), (TRACERS, ROWS, COLUMNS)]
        + [column_rim, column_rim, row_rim, row_rim],
        [total, helped, solved, gain],
    )
    second_rims = exchange(*out_rims)
    (result,) = call(
        functools.partial(step_kernel, False),
        [q.shape],
        [result, *second_rims, *rims, *statics, forcing],
        [pltpu.VMEM(q.shape, F32), pltpu.SemaphoreType.DMA((ROWS // 8,)), *rim_scratch],
        moved=8_000_000,
        out_hbm=True,
    )
    return result.reshape(tracers.shape), flux


def solution(mesh):
    in_specs = (
        P(None, None, "gy", "gx"),
        P(None, "gy", "gx"),
        P(None, "gy", "gx"),
        P(None, "gy", "gx"),
        P("gy", "gx"),
        P(None, "gy", "gx"),
        P("gy", "gx"),
        P("gy", "gx"),
        P("gy", "gx"),
    )
    out_specs = (P(None, None, "gy", "gx"), P(None, "gy", "gx"))
    return jax.shard_map(local, mesh=mesh, in_specs=in_specs, out_specs=out_specs, check_vma=False)
```

```python
import functools

import jax
import jax.numpy as jnp
from jax import lax
from jax.experimental import pallas as pl
from jax.experimental.pallas import tpu as pltpu
from jax.sharding import PartitionSpec as P

DIFFUSE = 0.05
FIELDS = 8
TRACERS = 2
NZ = 8
ROWS = 64
COLUMNS = 256
LANES = 128
GX = 8
GY = 16
SLOT_ROWS = 32
ATMOS_ROWS = 16
HELPED_BY = {12: GY - 2, 11: GY - 1}
DENSE = ((12, GY - 2), (11, GY - 1))
SENT_AWAY = 13
ENTRY_STEPS = (
    ((7, GY - 2), (8, GY - 1), (10, 12), (9, 11)),
    ((8, GY - 2), (7, GY - 1)),
    ((9, GY - 2), (13, GY - 1)),
)
CHANNELS = TRACERS * NZ
COUNT_AT = 24
RIM = 32
LIST = 3 * SLOT_ROWS
ATMOS = FIELDS * ATMOS_ROWS
PAYLOAD = LIST + ATMOS
CHUNK_ROWS = 16
CHUNK = CHUNK_ROWS * LANES
VMEM_LIMIT = 48 * 1024 * 1024
PACK_LIMIT = 63 * 1024 * 1024
F32 = jnp.float32
BF16 = jnp.bfloat16
F8 = jnp.float8_e4m3fn
LOW_TOP = 65536.0


def call(
    kernel, out_shapes, operands, scratch=(), flops=0, moved=4_000_000, in_hbm=False, out_hbm=False
):
    place = pltpu.HBM if in_hbm else pltpu.VMEM
    out_place = pl.ANY if out_hbm else pltpu.VMEM
    return pl.pallas_call(
        kernel,
        out_shape=[jax.ShapeDtypeStruct(shape, F32) for shape in out_shapes],
        in_specs=[pl.BlockSpec(memory_space=place) for _ in operands],
        out_specs=[pl.BlockSpec(memory_space=out_place) for _ in out_shapes],
        scratch_shapes=list(scratch),
        compiler_params=pltpu.CompilerParams(vmem_limit_bytes=PACK_LIMIT if in_hbm else VMEM_LIMIT),
        cost_estimate=pl.CostEstimate(flops=flops, bytes_accessed=moved, transcendentals=0),
    )(*operands)


def is_odd_column():
    return lax.rem(lax.axis_index("gx"), 2) == 1


def pack_columns(east_of, east_channels, west_of, west_channels, far_ref, near_ref):
    odd = is_odd_column()
    lane = lax.broadcasted_iota(jnp.int32, (8, LANES), 1)
    for block in range(ROWS // 8):
        tiles = []
        for pick, channels in ((east_of, east_channels), (west_of, west_channels)):
            tile = jnp.zeros((8, LANES), F32)
            for channel in channels:
                value, at = pick(channel, block * 8)
                shift = (channel - at) % LANES
                moved = pltpu.roll(value, shift, axis=1) if shift else value
                tile = jnp.where(lane == channel, moved, tile)
            tiles.append(tile)
        east, west = tiles
        far_ref[pl.ds(block * 8, 8), :] = jnp.where(odd, east, west)
        near_ref[pl.ds(block * 8, 8), :] = jnp.where(odd, west, east)


def pack_row(value, channel, out_ref):
    out_ref[pl.ds(channel, 1), :] = value[:, :LANES]
    out_ref[pl.ds(RIM + channel, 1), :] = value[:, LANES:]


def is_even():
    return lax.rem(lax.axis_index("gy"), 2) == 0


def pack_rows(top_of, bottom_of, channels, sibling_ref, other_ref):
    even = is_even()
    zeros = jnp.zeros((2 * RIM, LANES), F32)
    sibling_ref[0 : 2 * RIM, :] = zeros
    other_ref[0 : 2 * RIM, :] = zeros
    for channel in channels:
        top, bottom = top_of(channel), bottom_of(channel)
        pack_row(jnp.where(even, top, bottom), channel, sibling_ref)
        pack_row(jnp.where(even, bottom, top), channel, other_ref)


def chosen(here, table, default):
    for key, value in table.items():
        default = jnp.where(here == key, value, default)
    return default


def among(here, table):
    return functools.reduce(jnp.logical_or, [here == key for key in table])


def list_into(lists, out_ref, at, tile, valid=None):
    rows = pl.ds(pl.multiple_of(tile * SLOT_ROWS, SLOT_ROWS), SLOT_ROWS)
    for kind, ref in enumerate(lists):
        part = ref[rows, :].astype(F32)
        if kind == 2 and valid is not None:
            part = jnp.where(valid, part, 0.0)
        out_ref[at + kind * SLOT_ROWS : at + (kind + 1) * SLOT_ROWS, :] = part


def pack_kernel(*refs):
    steps = len(ENTRY_STEPS)
    froms, refs = refs[:8], refs[8:]
    (to_far_ref, to_near_ref, sibling_ref, other_ref, fold_ref), refs = refs[:5], refs[5:]
    entry_refs, intos, (cells_ref, sems) = refs[:steps], refs[steps:-2], refs[-2:]
    tracers_ref, east_ref, north_ref, count_ref, source_ref, target_ref, weight_ref, atmos_ref = intos
    copies = [
        pltpu.make_async_copy(array, into, sems.at[n])
        for n, (array, into) in enumerate(zip(froms, intos, strict=True))
    ]
    for copy in copies:
        copy.start()
    for copy in copies[4:]:
        copy.wait()
    here = lax.axis_index("gy")
    even = is_even()
    lists = (source_ref, target_ref, weight_ref)
    for field in range(FIELDS):
        for row in range(ATMOS_ROWS):
            to = row * FIELDS + field
            cells_ref[to : to + 1, :] = atmos_ref[field, row : row + 1, :]
    cells = cells_ref[...]
    for pairs, out_ref in zip(ENTRY_STEPS, entry_refs, strict=True):
        wanted = {source: HELPED_BY.get(to, to) for source, to in pairs}
        list_into(lists, out_ref, 0, chosen(here, wanted, here))
        out_ref[LIST:PAYLOAD, :] = cells
    partner = here ^ 1
    list_into(lists, sibling_ref, 2 * RIM, chosen(partner, HELPED_BY, partner))
    list_into(lists, sibling_ref, 2 * RIM + LIST, partner, among(partner, HELPED_BY))
    sibling_ref[2 * RIM + 2 * LIST :, :] = cells
    away = jnp.clip(jnp.where(even, here - 1, here + 1), 0, GY - 1)
    below_top = here != GY - 1
    helped = jnp.logical_and(below_top, among(away, HELPED_BY))
    list_into(lists, other_ref, 2 * RIM, chosen(away, HELPED_BY, away), helped)
    direct = jnp.logical_and(below_top, here != SENT_AWAY)
    list_into(lists, other_ref, 2 * RIM + LIST, away, direct)
    other_ref[2 * RIM + 2 * LIST :, :] = cells

    for copy in copies[:4]:
        copy.wait()

    def east_column(channel, row):
        rows = pl.ds(row, 8)
        if channel < CHANNELS:
            return tracers_ref[channel, rows, LANES:], LANES - 1
        if channel < COUNT_AT:
            return east_ref[channel - CHANNELS, rows, LANES:], LANES - 1
        return count_ref[rows, LANES:].astype(F32), LANES - 1

    def west_column(channel, row):
        rows = pl.ds(row, 8)
        if channel < CHANNELS:
            return tracers_ref[channel, rows, :LANES], 0
        return count_ref[rows, :LANES].astype(F32), 0

    pack_columns(
        east_column,
        [*range(CHANNELS + NZ), COUNT_AT],
        west_column,
        [*range(CHANNELS), COUNT_AT],
        to_far_ref,
        to_near_ref,
    )

    def top_of(channel):
        if channel < CHANNELS:
            return tracers_ref[channel, ROWS - 1 : ROWS, :]
        if channel < COUNT_AT:
            return north_ref[channel - CHANNELS, ROWS - 1 : ROWS, :]
        return count_ref[ROWS - 1 : ROWS, :].astype(F32)

    def bottom_of(channel):
        if channel < CHANNELS:
            return tracers_ref[channel, 0:1, :]
        if channel < COUNT_AT:
            return jnp.zeros((1, COLUMNS), F32)
        return count_ref[0:1, :].astype(F32)

    pack_rows(top_of, bottom_of, range(COUNT_AT + 1), sibling_ref, other_ref)
    fold_ref[...] = other_ref[0 : 2 * RIM, :]


def step_kernel(
    forced,
    q_ref,
    from_far_ref,
    from_near_ref,
    from_sibling_ref,
    from_other_ref,
    from_fold_ref,
    static_far_ref,
    static_near_ref,
    static_sibling_ref,
    static_other_ref,
    static_fold_ref,
    east_ref,
    north_ref,
    count_ref,
    mix_ref,
    *more_refs,
):
    if forced:
        out_ref, gain_ref = more_refs[-10:-8]
    else:
        forcing_ref, out_hbm, out_ref, sems = more_refs[:4]
    from_south_ref, top_ref, static_south_ref, static_top_ref = more_refs[-8:-4]
    from_west_ref, from_east_ref, static_west_ref, static_east_ref = more_refs[-4:]
    odd = is_odd_column()
    from_west_ref[...] = jnp.where(odd, from_near_ref[...], from_far_ref[...])
    from_east_ref[...] = jnp.where(odd, from_far_ref[...], from_near_ref[...])
    static_west_ref[...] = jnp.where(odd, static_near_ref[...], static_far_ref[...])
    static_east_ref[...] = jnp.where(odd, static_far_ref[...], static_near_ref[...])
    even = is_even()
    on_top = lax.axis_index("gy") == GY - 1
    lane = lax.broadcasted_iota(jnp.int32, (8, LANES), 1)
    row = lax.broadcasted_iota(jnp.int32, (8, LANES), 0)
    first_lane, last_lane = lane == 0, lane == LANES - 1
    first_row, last_row = row == 0, row == 7

    def set_rims(sibling_rim, other_rim, fold_rim, south, north):
        @pl.when(even)
        def _():
            south[...] = other_rim[0 : 2 * RIM, :]
            north[...] = sibling_rim[0 : 2 * RIM, :]

        @pl.when(jnp.logical_not(even))
        def _():
            south[...] = sibling_rim[0 : 2 * RIM, :]
            north[...] = other_rim[0 : 2 * RIM, :]

        @pl.when(on_top)
        def _():
            flipped = LANES - 1 - lane
            for half in range(2):
                for block in range(RIM // 8):
                    rows = fold_rim[pl.ds((1 - half) * RIM + block * 8, 8), :]
                    north[pl.ds(half * RIM + block * 8, 8), :] = jnp.take_along_axis(
                        rows, flipped, axis=1, mode="promise_in_bounds"
                    )

    set_rims(from_sibling_ref, from_other_ref, from_fold_ref, from_south_ref, top_ref)
    set_rims(
        static_sibling_ref, static_other_ref, static_fold_ref, static_south_ref, static_top_ref
    )

    def block_step(block, carry):
        at = pl.multiple_of(block * 8, 8)
        below = pl.multiple_of(jnp.maximum(block - 1, 0) * 8, 8)
        above = pl.multiple_of(jnp.minimum(block + 1, ROWS // 8 - 1) * 8, 8)
        is_first, is_last = block == 0, block == ROWS // 8 - 1
        rows = pl.ds(at, 8)

        def halves(load):
            return [load(rows, slice(0, LANES)), load(rows, slice(LANES, 2 * LANES))]

        def to_west_of(parts, rim):
            low = jnp.where(last_lane, rim, parts[0])
            high = jnp.where(last_lane, parts[0], parts[1])
            return [pltpu.roll(low, 1, axis=1), pltpu.roll(high, 1, axis=1)]

        def to_east_of(parts, rim):
            low = jnp.where(first_lane, parts[1], parts[0])
            high = jnp.where(first_lane, rim, parts[1])
            return [
                pltpu.roll(low, LANES - 1, axis=1),
                pltpu.roll(high, LANES - 1, axis=1),
            ]

        def to_south_of(load, parts, rim_ref, channel):
            found = []
            for half in range(2):
                lanes = slice(half * LANES, (half + 1) * LANES)
                rim = jnp.broadcast_to(
                    rim_ref[half * RIM + channel : half * RIM + channel + 1, :], (8, LANES)
                )
                near = jnp.where(is_first, rim, load(pl.ds(below, 8), lanes))
                found.append(pltpu.roll(jnp.where(last_row, near, parts[half]), 1, axis=0))
            return found

        def to_north_of(load, parts, rim_ref, channel):
            found = []
            for half in range(2):
                lanes = slice(half * LANES, (half + 1) * LANES)
                rim = jnp.broadcast_to(
                    rim_ref[half * RIM + channel : half * RIM + channel + 1, :], (8, LANES)
                )
                near = jnp.where(is_last, rim, load(pl.ds(above, 8), lanes))
                found.append(pltpu.roll(jnp.where(first_row, near, parts[half]), 7, axis=0))
            return found

        def west_rim(ref, channel):
            return pltpu.roll(ref[rows, :], (LANES - 1 - channel) % LANES, axis=1)

        def east_rim(ref, channel):
            shift = (LANES - channel) % LANES
            return pltpu.roll(ref[rows, :], shift, axis=1) if shift else ref[rows, :]

        def load_count(where, lanes):
            return count_ref[where, lanes].astype(F32)

        count = halves(load_count)
        sides = [
            to_east_of(count, east_rim(static_east_ref, COUNT_AT)),
            to_west_of(count, west_rim(static_west_ref, COUNT_AT)),
            to_north_of(load_count, count, static_top_ref, COUNT_AT),
            to_south_of(load_count, count, static_south_ref, COUNT_AT),
        ]
        shared = [[jnp.minimum(count[half], side[half]) for half in range(2)] for side in sides]
        closed = jnp.logical_and(jnp.logical_and(on_top, is_last), last_row)

        values = [[[None, None] for _ in range(NZ)] for _ in range(TRACERS)]
        for level in range(NZ):
            east = halves(lambda where, lanes: east_ref[level, where, lanes])
            west = to_west_of(east, west_rim(static_west_ref, CHANNELS + level))

            def load_north(where, lanes):
                return north_ref[level, where, lanes]

            north = halves(load_north)
            south = to_south_of(load_north, north, static_south_ref, CHANNELS + level)
            coefs = []
            for half in range(2):
                limit = float(level)
                up = jnp.where(closed, 0.0, north[half])
                open_e, open_w, open_n, open_s = [side[half] > limit for side in shared]

                def into(opened, speed):
                    return jnp.where(opened, DIFFUSE - jnp.minimum(speed, 0.0), 0.0)

                def away(opened, speed):
                    return jnp.where(opened, DIFFUSE + jnp.maximum(speed, 0.0), 0.0)

                from_e, lost_e = into(open_e, east[half]), away(open_e, east[half])
                from_w, lost_w = away(open_w, west[half]), into(open_w, west[half])
                from_n, lost_n = into(open_n, up), away(open_n, up)
                from_s, lost_s = away(open_s, south[half]), into(open_s, south[half])
                kept = 1.0 - ((lost_e + lost_w) + (lost_n + lost_s))
                coefs.append((kept, from_e, from_w, from_n, from_s))
            for tracer in range(TRACERS):
                channel = tracer * NZ + level

                def load_q(where, lanes):
                    return q_ref[channel, where, lanes]

                q = halves(load_q)
                q_e = to_east_of(q, east_rim(from_east_ref, channel))
                q_w = to_west_of(q, west_rim(from_west_ref, channel))
                q_n = to_north_of(load_q, q, top_ref, channel)
                q_s = to_south_of(load_q, q, from_south_ref, channel)
                for half in range(2):
                    kept, from_e, from_w, from_n, from_s = coefs[half]
                    values[tracer][level][half] = (
                        kept * q[half]
                        + (from_e * q_e[half] + from_w * q_w[half])
                        + (from_n * q_n[half] + from_s * q_s[half])
                    )
        for half in range(2):
            lanes = slice(half * LANES, (half + 1) * LANES)
            sides_here = [[values[t][k][half] for k in range(NZ)] for t in range(TRACERS)]
            surface = count[half] > 0.0
            if forced:
                sides_here.append([jnp.where(surface, 1.0, 0.0)] + [None] * (NZ - 1))
            else:
                for tracer in range(TRACERS):
                    forcing = jnp.where(surface, forcing_ref[tracer, rows, lanes], 0.0)
                    sides_here[tracer][0] = sides_here[tracer][0] + forcing
            ratios = []
            partials = [[] for _ in sides_here]
            for level in range(NZ):
                thickness = 1.0 + level / NZ
                upper = lower = None
                if level >= 1:
                    mix = mix_ref[level - 1, rows, lanes]
                    upper = jnp.where(count[half] > float(level), mix * (1.0 / thickness), 0.0)
                if level <= NZ - 2:
                    mix = mix_ref[level, rows, lanes]
                    lower = jnp.where(
                        count[half] > float(level + 1), mix * (1.0 / thickness), 0.0
                    )
                if upper is None:
                    pivot = 1.0 + lower
                elif lower is None:
                    pivot = 1.0 + upper - upper * ratios[-1]
                else:
                    pivot = 1.0 + upper + lower - upper * ratios[-1]
                inverse = 1.0 / pivot
                if lower is not None:
                    ratios.append(lower * inverse)
                for side, partial in zip(sides_here, partials, strict=True):
                    right = side[level]
                    if level >= 1:
                        carried = upper * partial[-1]
                        right = carried if right is None else right + carried
                    partial.append(right * inverse)
            for index, partial in enumerate(partials):
                solved = partial[-1]
                for level in range(NZ - 1, -1, -1):
                    if level < NZ - 1:
                        solved = partial[level] + ratios[level] * solved
                    if index < TRACERS:
                        out_ref[index * NZ + level, rows, lanes] = solved
                    else:
                        gain_ref[level, rows, lanes] = solved
        if not forced:
            block_copy(block).start()
        return carry

    def block_copy(block):
        rows = pl.ds(pl.multiple_of(block * 8, 8), 8)
        return pltpu.make_async_copy(out_ref.at[:, rows, :], out_hbm.at[:, rows, :], sems.at[block])

    lax.fori_loop(0, ROWS // 8, block_step, 0)
    if not forced:
        for block in range(ROWS // 8):
            block_copy(block).wait()


def land_kernel(slots, own_slot, reset, *refs):
    operand_refs, refs = refs[:-9], refs[-9:]
    if own_slot:
        own, operand_refs = operand_refs[:4], operand_refs[4:]
    here = lax.axis_index("gy")
    helps = among(here, HELPED_BY)
    if reset is not None:
        start_ref = operand_refs[-1]
    total_ref, lists_ref, columns_ref, cells_ref = refs[:4]
    high_ref, low_ref, high_hot_ref, low_hot_ref, weights_ref = refs[4:]
    largest = jnp.zeros((8, LANES), F32)
    row_number = lax.broadcasted_iota(jnp.int32, (SLOT_ROWS, LANES), 0).astype(F32) + 1.0
    ends = []

    def unpack(slot):
        source, target, weight = weights_ref[0], weights_ref[1], weights_ref[2]
        rows = pl.ds(slot * SLOT_ROWS, SLOT_ROWS)
        source_row = jnp.floor(source * (1.0 / LANES))
        target_row = jnp.floor(target * (1.0 / COLUMNS))
        columns_ref[rows, :] = (source - source_row * LANES).astype(jnp.int32)
        lists_ref[0, rows, :] = source_row
        lists_ref[1, rows, :] = target_row
        lists_ref[2, rows, :] = target - target_row * COLUMNS
        lists_ref[3, rows, :] = weight
        return jnp.max(jnp.where(weight != 0.0, row_number, 0.0)).astype(jnp.int32)

    if own_slot:
        tile = here if reset else chosen(here, HELPED_BY, here)
        rows = pl.ds(pl.multiple_of(tile * SLOT_ROWS, SLOT_ROWS), SLOT_ROWS)
        for kind in range(3):
            part = own[kind][rows, :].astype(F32)
            if kind == 2 and reset:
                part = jnp.where(helps, part, 0.0)
            weights_ref[kind] = part
        ends.append(unpack(0))
        for field in range(FIELDS):
            largest = jnp.maximum(largest, jnp.abs(own[3][field, 0:8, :]))
            largest = jnp.maximum(largest, jnp.abs(own[3][field, 8:16, :]))
            for row in range(ATMOS_ROWS):
                cells_ref[0, row, field : field + 1, :] = own[3][field, row : row + 1, :]
    count = own_slot + len(slots)
    for slot, (operand, list_at, cells_at, only) in enumerate(slots, own_slot):
        ref = operand_refs[operand]
        for kind in range(3):
            rows = pl.ds(list_at + kind * SLOT_ROWS, SLOT_ROWS)
            part = ref[rows, :]
            if kind == 2 and only is not None:
                part = jnp.where(helps == only, part, 0.0)
            weights_ref[kind] = part
        ends.append(unpack(slot))
        for row in range(ATMOS_ROWS):
            cells = ref[pl.ds(cells_at + row * FIELDS, FIELDS), :]
            cells_ref[slot, row] = cells
            largest = jnp.maximum(largest, jnp.abs(cells))
    scale = LOW_TOP / jnp.maximum(jnp.max(largest), 1e-30)
    unscale = 1.0 / scale

    spare = count * SLOT_ROWS
    lists_ref[:, spare : spare + 8, :] = jnp.zeros((4, 8, LANES), F32)
    columns_ref[spare : spare + 8, :] = jnp.zeros((8, LANES), jnp.int32)
    firsts = [jnp.int32(0)]
    for end in ends:
        firsts.append(firsts[-1] + end)
    live = firsts.pop()

    def row_of(place):
        shift = jnp.int32(0)
        for slot in range(1, count):
            shift = jnp.where(place >= firsts[slot], slot * SLOT_ROWS - firsts[slot], shift)
        return jnp.where(place < live, place + shift, spare)

    if reset is None:
        total_ref[...] = jnp.zeros_like(total_ref)
    elif reset:

        @pl.when(helps)
        def _():
            total_ref[...] = jnp.zeros_like(total_ref)

        @pl.when(jnp.logical_not(helps))
        def _():
            total_ref[...] = start_ref[...]
    else:
        total_ref[...] = start_ref[...]
    ones, zeros = jnp.ones((), BF16), jnp.zeros((), BF16)
    iota = lax.broadcasted_iota(jnp.int32, (COLUMNS, LANES), 0).astype(F32).astype(BF16)

    def hot(values, height):
        line = jnp.broadcast_to(values, (16, LANES)).astype(BF16)
        return [jnp.where(line == iota[at : at + 16], ones, zeros) for at in range(0, height, 16)]

    def chunk(place, entries):
        for entry in range(entries):
            at = row_of(place + entry)
            one = pl.ds(at, 1)
            slot = jnp.minimum(lax.div(at, SLOT_ROWS), count - 1)
            lanes = slice(entry * LANES, (entry + 1) * LANES)
            row_here = jnp.broadcast_to(lists_ref[0, one, :], (FIELDS, LANES))
            column_here = jnp.broadcast_to(columns_ref[one, :], (FIELDS, LANES))
            picked = jnp.zeros((FIELDS, LANES), F32)
            for row in range(ATMOS_ROWS):
                found_here = jnp.take_along_axis(
                    cells_ref[slot, row], column_here, axis=1, mode="promise_in_bounds"
                )
                picked = jnp.where(row_here == float(row), found_here, picked)
            weighted = picked * lists_ref[3, one, :]
            high = weighted.astype(BF16).astype(F32)
            low = (weighted - high) * scale
            row_hot = hot(lists_ref[1, one, :], ROWS)
            for field in range(FIELDS):
                first = field * ROWS
                line = jnp.broadcast_to(high[field : field + 1, :], (16, LANES)).astype(BF16)
                for part in range(4):
                    high_ref[first + part * 16 : first + part * 16 + 16, lanes] = line * row_hot[part]
                line = jnp.broadcast_to(low[field : field + 1, :], (16, LANES)).astype(BF16)
                for part in range(2):
                    both = [line * row_hot[2 * part], line * row_hot[2 * part + 1]]
                    low_ref[first + part * 32 : first + part * 32 + 32, lanes] = jnp.concatenate(
                        both, axis=0
                    ).astype(F8)
            column_hot = hot(lists_ref[2, one, :], COLUMNS)
            for part in range(COLUMNS // 16):
                high_hot_ref[part * 16 : part * 16 + 16, lanes] = column_hot[part]
            for part in range(COLUMNS // 32):
                low_hot_ref[part * 32 : part * 32 + 32, lanes] = jnp.concatenate(
                    column_hot[2 * part : 2 * part + 2], axis=0
                ).astype(F8)
        over_entries = (((1,), (1,)), ((), ()))
        used = slice(0, entries * LANES)
        total_ref[...] += lax.dot_general(
            high_ref[:, used], high_hot_ref[:, used], over_entries, preferred_element_type=F32
        ) + unscale * lax.dot_general(
            low_ref[:, used], low_hot_ref[:, used], over_entries, preferred_element_type=F32
        )

    def chunk_step(at, carry):
        chunk(at * CHUNK_ROWS, CHUNK_ROWS)
        return carry

    half = CHUNK_ROWS // 2
    wholes = lax.div(live + (half - 1), CHUNK_ROWS)
    lax.fori_loop(0, wholes, chunk_step, 0)

    @pl.when(live > wholes * CHUNK_ROWS)
    def _():
        chunk(wholes * CHUNK_ROWS, half)


def finish_kernel(
    total_ref,
    helped_ref,
    solved_ref,
    gain_ref,
    result_ref,
    flux_ref,
    forcing_ref,
    to_far_ref,
    to_near_ref,
    sibling_ref,
    other_ref,
):
    def block_step(block, carry):
        rows = pl.ds(pl.multiple_of(block * 8, 8), 8)
        flux = []
        for field in range(FIELDS):
            from_rows = pl.ds(pl.multiple_of(field * ROWS + block * 8, 8), 8)
            value = total_ref[from_rows, :] + helped_ref[from_rows, :]
            flux_ref[field, rows, :] = value
            flux.append(value)
        heat = flux[0] + flux[1] + flux[2] + flux[3] + flux[4]
        salt = flux[7] - flux[5] - flux[6]
        forcing_ref[0, rows, :] = heat
        forcing_ref[1, rows, :] = salt
        for level in range(NZ):
            gain = gain_ref[level, rows, :]
            for tracer, forcing in enumerate((heat, salt)):
                channel = tracer * NZ + level
                result_ref[channel, rows, :] = solved_ref[channel, rows, :] + forcing * gain
        return carry

    lax.fori_loop(0, ROWS // 8, block_step, 0)
    pack_columns(
        lambda channel, row: (result_ref[channel, pl.ds(row, 8), LANES:], LANES - 1),
        range(CHANNELS),
        lambda channel, row: (result_ref[channel, pl.ds(row, 8), :LANES], 0),
        range(CHANNELS),
        to_far_ref,
        to_near_ref,
    )
    pack_rows(
        lambda channel: result_ref[channel, ROWS - 1 : ROWS, :],
        lambda channel: result_ref[channel, 0:1, :],
        range(CHANNELS),
        sibling_ref,
        other_ref,
    )


FAR = [(x, (x + 1 if x % 2 else x - 1) % GX) for x in range(GX)]
NEAR = [(x, (x - 1 if x % 2 else x + 1) % GX) for x in range(GX)]
SIBLINGS = [(y, y ^ 1) for y in range(GY)]
OTHERS = [
    (x * GY + y, x * GY + (y + 1 if y % 2 else y - 1)) for x in range(GX) for y in range(1, GY - 1)
]
FOLD = [(x * GY + GY - 1, (GX - 1 - x) * GY + GY - 1) for x in range(GX)]


def exchange(to_far, to_near, sibling, other, fold=None):
    if fold is None:
        others = lax.ppermute(other, ("gx", "gy"), OTHERS + FOLD)
        folded = others
    else:
        others = lax.ppermute(other, ("gx", "gy"), OTHERS)
        folded = fold
    return (
        lax.ppermute(to_far, "gx", FAR),
        lax.ppermute(to_near, "gx", NEAR),
        lax.ppermute(sibling, "gy", SIBLINGS),
        others,
        folded,
    )


def land(operands, slots, own_slot, reset):
    count = own_slot + len(slots)
    (total,) = call(
        functools.partial(land_kernel, slots, own_slot, reset),
        [(FIELDS * ROWS, COLUMNS)],
        operands,
        [
            pltpu.VMEM((4, count * SLOT_ROWS + 8, LANES), F32),
            pltpu.VMEM((count * SLOT_ROWS + 8, LANES), jnp.int32),
            pltpu.VMEM((count, ATMOS_ROWS, FIELDS, LANES), F32),
            pltpu.VMEM((FIELDS * ROWS, CHUNK), BF16),
            pltpu.VMEM((FIELDS * ROWS, CHUNK), F8),
            pltpu.VMEM((COLUMNS, CHUNK), BF16),
            pltpu.VMEM((COLUMNS, CHUNK), F8),
            pltpu.VMEM((3, SLOT_ROWS, LANES), F32),
        ],
        moved=100_000,
    )
    return total


def local(
    tracers,
    east_speed,
    north_speed,
    vertical_mix,
    level_count,
    atmosphere_flux,
    intersection_source,
    intersection_target,
    intersection_weight,
):
    q = tracers.reshape(CHANNELS, ROWS, COLUMNS)
    statics = [east_speed, north_speed, level_count, vertical_mix]
    lists = [intersection_source, intersection_target, intersection_weight, atmosphere_flux]
    column_rim, row_rim = (ROWS, LANES), (2 * RIM, LANES)
    both = (2 * RIM + LIST + PAYLOAD, LANES)
    steps = len(ENTRY_STEPS)
    packed = call(
        pack_kernel,
        [column_rim, column_rim, both, both, row_rim] + [(PAYLOAD, LANES)] * steps,
        [q, *statics[:3], *lists],
        [
            *[pltpu.VMEM(part.shape, part.dtype) for part in (q, *statics[:3], *lists)],
            pltpu.VMEM((ATMOS, LANES), F32),
            pltpu.SemaphoreType.DMA((8,)),
        ],
        in_hbm=True,
    )
    entries = [
        lax.ppermute(part, "gy", list(pairs))
        for part, pairs in zip(packed[5:], ENTRY_STEPS, strict=True)
    ]
    rims = exchange(*packed[:5])
    first, second, cells = 2 * RIM, 2 * RIM + LIST, 2 * RIM + 2 * LIST
    most = land([*lists, rims[2]], ((0, first, cells, None),), 1, None)
    partial = land(
        [rims[3], *entries, most], ((0, first, cells, None), (1, 0, LIST, True)), 0, False
    )
    helped = lax.ppermute(partial, "gy", list(DENSE))
    total = land(
        [*lists, rims[2], rims[3], *entries, partial],
        ((0, second, cells, None), (1, second, cells, None), (2, 0, LIST, False))
        + tuple((2 + step, 0, LIST, None) for step in range(1, steps)),
        1,
        True,
    )
    fold, _ = lax.optimization_barrier((rims[4], total))
    rims = (*rims[:4], lax.ppermute(fold, ("gx", "gy"), FOLD))
    rim_scratch = [pltpu.VMEM(row_rim, F32)] * 4 + [pltpu.VMEM(column_rim, F32)] * 4
    solved, gain = call(
        functools.partial(step_kernel, True),
        [q.shape, east_speed.shape],
        [q, *rims, *rims, *statics, partial],
        rim_scratch,
        moved=8_000_000,
    )
    result, flux, forcing, *out_rims = call(
        finish_kernel,
        [q.shape, (FIELDS, ROWS, COLUMNS), (TRACERS, ROWS, COLUMNS)]
        + [column_rim, column_rim, row_rim, row_rim],
        [total, helped, solved, gain],
    )
    second_rims = exchange(*out_rims)
    (result,) = call(
        functools.partial(step_kernel, False),
        [q.shape],
        [result, *second_rims, *rims, *statics, forcing],
        [pltpu.VMEM(q.shape, F32), pltpu.SemaphoreType.DMA((ROWS // 8,)), *rim_scratch],
        moved=8_000_000,
        out_hbm=True,
    )
    return result.reshape(tracers.shape), flux


def solution(mesh):
    in_specs = (
        P(None, None, "gy", "gx"),
        P(None, "gy", "gx"),
        P(None, "gy", "gx"),
        P(None, "gy", "gx"),
        P("gy", "gx"),
        P(None, "gy", "gx"),
        P("gy", "gx"),
        P("gy", "gx"),
        P("gy", "gx"),
    )
    out_specs = (P(None, None, "gy", "gx"), P(None, "gy", "gx"))
    return jax.shard_map(local, mesh=mesh, in_specs=in_specs, out_specs=out_specs, check_vma=False)
```
